256 devices in a mesh: dp: 16 (over y_hi, z), layer: 4 (over x), query: 4 (over y_lo, core).
Axes of the slice: x: 4, y: 4 (y_hi: 2, y_lo: 2; y = y_hi * 2 + y_lo), z: 8, core: 2. Of those that a mesh axis runs over, the one named last changes fastest.
Arguments:
- mantissas: bfloat16 [4096, 4, 4096], P('dp', 'layer'), may hold values from -6 to 6
- exponents: int32 [4096, 4, 32], P('dp', 'layer'), may hold values from -2 to 1
- queries: bfloat16 [1024, 4, 4096], P('query', 'layer'), may hold values from -0.046875 to 0.046875
- doc_ids: int32 [4096], P('dp'), may hold values from 0 to 1023, never falling along the last dimension, each value on 1 to 32 neighbouring positions
- owners: int32 [1024], replicated, may hold values from 0 to 1023, each once
Outputs:
- fisher: float32 [4, 4096, 4096], P('layer', 'dp', 'query')
- doc_scores: float32 [1024, 1024], P('dp', 'query')
The draws below stay inside these ranges and needn't reach their ends.
Inputs may be any that keep to these rules, and one draw needn't show every extreme that they name: `doc_ids`: never falling along the rows; every document has 1 to 32 rows, one exactly 32. `owners`: each slot is taken by exactly one document.
All inputs are finite; a program needn't handle non-finite values.
Results may differ from the reference program's by a relative error of at most 0.0003.
Values may be sent and summed in bfloat16 or wider, within the bound.
No kernel may reach another device: no remote copies, remote signals or barrier semaphores. Data moves between devices by JAX's collectives and lax.ppermute only.
A program may use at most 64 MiB of HBM per device.

```python
import math
import jax
import jax.numpy as jnp
import numpy as np
from jax import lax

K = 4096
NQ = 1024
MOST = 32
LAYERS = 4
ROWS = 4096
DOCS = 1024


def with_ends(array, stream_key, least, largest):
    index_at = [jax.random.randint(jax.random.fold_in(stream_key, axis), (), 0, length) for axis, length in enumerate(array.shape)]
    main_axis = array.shape.index(max(array.shape))
    next_to = index_at[:main_axis] + [(index_at[main_axis] + 1) % array.shape[main_axis]] + index_at[main_axis + 1:]
    return array.at[tuple(index_at)].set(least).at[tuple(next_to)].set(largest)


def steps_of(own_key, extent, cuts, least, high):
    level = 1.0
    for position, parts in cuts:
        steps = jax.random.uniform(jax.random.fold_in(jax.random.fold_in(own_key, 6), position), (parts,), jnp.float32, least / len(cuts), high / len(cuts))
        level = level * jnp.repeat(jnp.exp(steps), extent[position] // parts).reshape((-1,) + (1,) * (len(extent) - 1 - position))
    return level


def split_up(count, total, most, skew):
    portions = [(1 << 20) // math.isqrt(rank ** skew) + 1 for rank in range(2, count + 1)]
    rest, given = total - most - (count - 1), [1] * (count - 1)
    while rest > 0:
        movable = [i for i in range(count - 1) if given[i] < most]
        mass, remaining = sum([portions[i] for i in movable]), rest
        for i in movable:
            more = min(most - given[i], max(1, remaining * portions[i] // mass), rest)
            given[i] = given[i] + more
            rest = rest - more
    return np.array([most] + given)


def ragged_sizes(key, amount, total, bound, slope):
    if amount == 2:
        one = jax.random.randint(key, (), max(1, total - bound), min(bound, total - 1) + 1)
        return jnp.stack([one, total - one])
    tallies = jnp.asarray(split_up(amount, total, bound, slope), jnp.int32)
    pairs = (amount - 1) // 2
    giver, taker = tallies[1:1 + 2 * pairs:2], tallies[2:2 + 2 * pairs:2]
    room = jnp.minimum(giver - 1, bound - taker)
    passed = jax.random.randint(jax.random.fold_in(key, 1), (pairs,), 0, 1 << 20) % (room + 1)
    tallies = tallies.at[1:1 + 2 * pairs:2].set(giver - passed).at[2:2 + 2 * pairs:2].set(taker + passed)
    return tallies[jax.random.permutation(jax.random.fold_in(key, 2), amount)]


def noise(stream_key, extent, spread, most, cuts=(), held_as=jnp.bfloat16):
    drawn = spread * jax.random.normal(stream_key, extent, jnp.float32)
    if cuts:
        drawn = drawn * steps_of(stream_key, extent, cuts, -0.22, 0.18)
    return jnp.clip(drawn, -most, most).astype(held_as)


def setup_inputs(seed: int = 0) -> dict:
    keys = jax.random.split(jax.random.key(seed), 6)
    return {
        "mantissas": noise(keys[0], (ROWS, LAYERS, K), 1.0, 6.0, ((0, 16), (1, 4))),
        "exponents": with_ends(jax.random.randint(keys[1], (ROWS, LAYERS, K // 128), -2, 2), jax.random.fold_in(keys[1], 1), -2, 1).astype(jnp.int32),
        "queries": noise(keys[2], (NQ, LAYERS, K), (LAYERS * K) ** -0.5, 0.046875, ((0, 4), (1, 4))),
        "doc_ids": jnp.searchsorted(jnp.cumsum(ragged_sizes(keys[3], DOCS, ROWS, MOST, 2)), jnp.arange(ROWS), side="right").astype(jnp.int32),
        "owners": jax.random.permutation(keys[4], DOCS).astype(jnp.int32),
    }


def dequant(mantissas, exponents):
    scale = jnp.exp2(exponents.astype(jnp.float32)).astype(jnp.bfloat16)
    rows, layers, width = mantissas.shape
    blocks = mantissas.reshape(rows, layers, width // 128, 128) * scale[..., None]
    return blocks.reshape(rows, layers, width)


def reference(mantissas, exponents, queries, doc_ids, owners):
    grads = dequant(mantissas, exponents)
    rows, layers, width = grads.shape

    def one_layer(slab):
        gram = lax.dot_general(slab, slab, (((0,), (0,)), ((), ())), preferred_element_type=jnp.float32)
        return gram * (1.0 / ROWS)

    fisher = lax.map(one_layer, jnp.transpose(grads, (1, 0, 2)))
    flat_grads = grads.reshape(rows, layers * width)
    flat_queries = queries.reshape(queries.shape[0], layers * width)
    scores = lax.dot_general(flat_grads, flat_queries, (((1,), (1,)), ((), ())), preferred_element_type=jnp.float32)
    slots = owners[doc_ids]
    doc_scores = jax.ops.segment_sum(scores, slots, num_segments=DOCS)
    return fisher, doc_scores
```

```python
import jax
import jax.numpy as jnp
from jax import lax
from jax.sharding import Mesh, PartitionSpec as P

YH, Z, X, YL, CORE = 2, 8, 4, 2, 2
ROW_AXES = ("yh", "z")
COL_AXES = ("yl", "core")


def powers(exponents):
    return jnp.exp2(exponents.astype(jnp.float32)).astype(jnp.bfloat16)


def spread(scale):
    blocks = scale.shape[1]
    lane_block = jnp.arange(blocks * 128, dtype=jnp.int32) // 128
    pick = (lane_block[None, :] == jnp.arange(blocks, dtype=jnp.int32)[:, None]).astype(jnp.bfloat16)
    wide = lax.dot_general(scale, pick, (((1,), (0,)), ((), ())), preferred_element_type=jnp.float32)
    return wide.astype(jnp.bfloat16)


def ring_gather(block, forward_steps, backward_steps):
    ahead = [(i, (i + 1) % Z) for i in range(Z)]
    behind = [(i, (i - 1) % Z) for i in range(Z)]
    shards = {0: block}
    now = block
    for step in range(1, forward_steps + 1):
        now = lax.ppermute(now, "z", ahead)
        shards[(-step) % Z] = now
    now = block
    for step in range(1, backward_steps + 1):
        now = lax.ppermute(now, "z", behind)
        shards[step % Z] = now
    return [shards[i] for i in range(Z)]


def fisher_block(mantissas, scale, total_rows):
    yh, z = lax.axis_index("yh"), lax.axis_index("z")
    yl, core = lax.axis_index("yl"), lax.axis_index("core")
    rows, width = mantissas.shape
    col_width = width // (YL * CORE)
    col_index = yl * CORE + core
    own = lax.dynamic_slice_in_dim(mantissas, col_index * col_width, col_width, 1)
    own = own * spread(lax.dynamic_slice_in_dim(scale, col_index * (col_width // 128), col_width // 128, 1))
    low = jnp.concatenate([own[:, i : i + 128] for i in range(0, col_width, 256)], 1)
    high = jnp.concatenate([own[:, i : i + 128] for i in range(128, col_width, 256)], 1)
    lows = jnp.concatenate(ring_gather(low, 4, 3), 0)
    highs = jnp.concatenate(ring_gather(high, 3, 4), 0)

    start = lax.rem(z, 4) * 128
    here = jnp.concatenate(
        [lax.dynamic_slice_in_dim(lows, start, 128, 1), lax.dynamic_slice_in_dim(highs, start, 128, 1)], 1
    )
    holder = z // 4
    sent = lax.ppermute(
        here, ("z", "core"), [(i * CORE + i // 4, i * CORE + 1 - i // 4) for i in range(Z)]
    )
    mine = jnp.where(core == holder, here, sent)
    swap = [(0, 1), (1, 0)]
    half = mine.shape[0] // 2
    piece = lax.ppermute(lax.dynamic_slice_in_dim(mine, core * half, half, 0), "yl", swap)
    other_piece = lax.ppermute(piece, "core", swap)
    theirs = jnp.where(
        core == 0,
        jnp.concatenate([piece, other_piece], 0),
        jnp.concatenate([other_piece, piece], 0),
    )
    kept = jnp.where(yl == yh, mine, theirs)
    given = jnp.where(yl == yh, theirs, mine)

    def term(left, right):
        return lax.dot_general(left, right, (((0,), (0,)), ((), ())), preferred_element_type=jnp.float32)

    halves = []
    for right in (lows, highs):
        got = lax.ppermute(term(given, right), "yh", swap)
        halves.append((term(kept, right) + got) * (1.0 / total_rows))
    return jnp.concatenate(
        [h[:, i : i + 128] for i in range(0, col_width // 2, 128) for h in halves], 1
    )


def score_block(mantissas, scale, queries, doc_ids, owners):
    yh = lax.axis_index("yh")
    docs = owners.shape[0]
    grads = mantissas * spread(scale)
    scores = lax.dot_general(queries, grads, (((1,), (1,)), ((), ())), preferred_element_type=jnp.float32)
    count, rows = scores.shape
    share = count // X
    summed = lax.all_to_all(scores.reshape(X, share, rows), "x", 0, 0, tiled=True).sum(0)
    slots = owners[doc_ids]
    own_docs = docs // (YH * Z)
    half = own_docs // 2
    place = jnp.arange(YH * Z, dtype=jnp.int32)[:, None] * own_docs + jnp.arange(half, dtype=jnp.int32)[None, :]
    place = place.reshape(-1, 1)
    member = jnp.concatenate([place == slots[None, :], place + half == slots[None, :]], 1).astype(jnp.float32)
    zero = jnp.zeros_like(summed)
    spaced = jnp.concatenate(
        [jnp.concatenate([summed, zero], 1), jnp.concatenate([zero, summed], 1)], 0
    )
    placed = lax.dot_general(
        member, spaced, (((1,), (1,)), ((), ())),
        precision=lax.Precision.HIGHEST, preferred_element_type=jnp.float32,
    )
    placed = placed.reshape(YH, Z, half, 2 * share)
    kept = lax.dynamic_index_in_dim(placed, yh, 0, keepdims=False)
    given = lax.dynamic_index_in_dim(placed, 1 - yh, 0, keepdims=False)
    placed = kept + lax.ppermute(given, "yh", [(0, 1), (1, 0)])
    mine = lax.all_to_all(placed, "z", 0, 0, tiled=True).sum(0)
    every = lax.all_gather(mine, "x")
    return every.reshape(X, half, 2, share).transpose(2, 1, 0, 3).reshape(own_docs, count)


def per_device(mantissas, exponents, queries, doc_ids, owners):
    mantissas = mantissas[:, 0, :]
    scale = powers(exponents[:, 0, :])
    total_rows = mantissas.shape[0] * YH * Z
    fisher = fisher_block(mantissas, scale, total_rows)
    doc_scores = score_block(mantissas, scale, queries[:, 0, :], doc_ids, owners)
    return fisher[None], doc_scores


def solution(mesh):
    fine = Mesh(mesh.devices.reshape(YH, Z, X, YL, CORE), ("yh", "z", "x", "yl", "core"))
    in_specs = (
        P(ROW_AXES, "x", None),
        P(ROW_AXES, "x", None),
        P(COL_AXES, "x", None),
        P(ROW_AXES),
        P(),
    )
    out_specs = (P("x", ROW_AXES, COL_AXES), P(ROW_AXES, COL_AXES))
    return jax.shard_map(per_device, mesh=fine, in_specs=in_specs, out_specs=out_specs, check_vma=False)
```

```python
import functools

import jax
import jax.numpy as jnp
from jax import lax
from jax.experimental import pallas as pl
from jax.experimental.pallas import tpu as pltpu
from jax.sharding import Mesh, PartitionSpec as P

YH, Z, X, YL, CORE = 2, 8, 4, 2, 2
ROW_AXES = ("yh", "z")
COL_AXES = ("yl", "core")
SWAP = [(0, 1), (1, 0)]
RING = [(2 * i, 2 * ((i + 1) % Z)) for i in range(Z)] + [(2 * i + 1, 2 * ((i - 1) % Z) + 1) for i in range(Z)]
TURNED = (((0,), (0,)), ((), ()))


def powers(exponents):
    return jnp.exp2(exponents.astype(jnp.float32)).astype(jnp.bfloat16)


def params():
    return pltpu.CompilerParams(vmem_limit_bytes=24 << 20)


def cost(flops, moved):
    return pl.CostEstimate(flops=flops, bytes_accessed=moved, transcendentals=0)


AT_Z, AT_CORE, AT_YL, AT_FAR = 0, 1, 2, 3


def wide_scale(turned, first_block, columns):
    blocks = turned.shape[0]
    lane_block = lax.broadcasted_iota(jnp.int32, (blocks, columns), 1) // 128 + first_block
    pick = (lane_block == lax.broadcasted_iota(jnp.int32, (blocks, columns), 0)).astype(jnp.bfloat16)
    return lax.dot_general(turned, pick, TURNED, preferred_element_type=jnp.float32)


def dequant_kernel(at, exps, values, far_values, low, high, far):
    step = pl.program_id(0)
    turned = powers(exps[...])
    grads = values[...].astype(jnp.float32) * wide_scale(turned, at[AT_YL] * 16 + step * 4, 512)
    grads = grads.astype(jnp.bfloat16)
    low[...] = jnp.concatenate([grads[:, 0:128], grads[:, 256:384]], 1)
    high[...] = jnp.concatenate([grads[:, 128:256], grads[:, 384:512]], 1)

    @pl.when(step == 0)
    def _():
        half = far.shape[0]
        scale = wide_scale(turned, at[AT_FAR] * 2, 256)
        scale = jnp.where(at[AT_CORE] == 0, scale[:half], scale[half:])
        far[...] = (far_values[...].astype(jnp.float32) * scale).astype(jnp.bfloat16)


def dequant(at, exps, mantissas):
    rows, width = mantissas.shape
    side = jax.ShapeDtypeStruct((rows, width // 4), jnp.bfloat16)
    return pl.pallas_call(
        dequant_kernel,
        grid_spec=pltpu.PrefetchScalarGridSpec(
            num_scalar_prefetch=1,
            grid=(4,),
            in_specs=[
                pl.BlockSpec(exps.shape, lambda g, at: (0, 0)),
                pl.BlockSpec((rows, 512), lambda g, at: (0, at[AT_YL] * 4 + g)),
                pl.BlockSpec((rows // 2, 256), lambda g, at: (at[AT_CORE], at[AT_FAR])),
            ],
            out_specs=[
                pl.BlockSpec((rows, 256), lambda g, at: (0, g)),
                pl.BlockSpec((rows, 256), lambda g, at: (0, g)),
                pl.BlockSpec((rows // 2, 256), lambda g, at: (0, 0)),
            ],
        ),
        out_shape=[side, side, jax.ShapeDtypeStruct((rows // 2, 256), jnp.bfloat16)],
        compiler_params=params(),
        cost_estimate=cost(1 << 25, 2 << 20),
        name="dequant",
    )(at, exps, mantissas, mantissas)


def pick_kernel(count, at, *refs):
    sides, out = refs[:-1], refs[-1]
    row = 0
    for i in range(count):
        rows = sides[2 * i].shape[0]
        out[row : row + rows] = jnp.concatenate([sides[2 * i][...], sides[2 * i + 1][...]], 1)
        row += rows


def lanes_at_z(rows, by_core):
    if by_core:
        return pl.BlockSpec((rows, 128), lambda g, at: (at[AT_CORE], at[AT_Z]))
    return pl.BlockSpec((rows, 128), lambda g, at: (0, at[AT_Z]))


def pick(at, pieces):
    rows = sum(n for n, _, _, _ in pieces)
    specs = [lanes_at_z(n, by_core) for n, by_core, _, _ in pieces for _ in range(2)]
    return pl.pallas_call(
        functools.partial(pick_kernel, len(pieces)),
        grid_spec=pltpu.PrefetchScalarGridSpec(
            num_scalar_prefetch=1, grid=(1,), in_specs=specs,
            out_specs=pl.BlockSpec((rows, 256), lambda g, at: (0, 0)),
        ),
        out_shape=jax.ShapeDtypeStruct((rows, 256), jnp.bfloat16),
        compiler_params=params(),
        cost_estimate=cost(0, rows * 1024),
        name="pick",
    )(at, *[side for _, _, low, high in pieces for side in (low, high)])


def gram_kernel(sizes, kept, added, at, *refs):
    count = len(sizes)
    lows, highs, rights = refs[:count], refs[count : 2 * count], refs[2 * count : 3 * count]
    near, third, far = refs[3 * count : 3 * count + 3]
    out = refs[-1]
    mine_first = at[AT_YL] == at[4]
    use_mine = mine_first if kept else jnp.logical_not(mine_first)
    total, row = None, 0
    for i, rows in enumerate(sizes):
        mine = jnp.concatenate([lows[i][...], highs[i][...]], 1)
        if i < count - 2:
            theirs = near[row : row + rows]
            row += rows
        else:
            theirs = third[...] if i == count - 2 else far[...]
        left = jnp.where(use_mine, mine, theirs)
        term = lax.dot_general(left, rights[i][...], TURNED, preferred_element_type=jnp.float32)
        total = term if total is None else total + term
    if added:
        total = total + refs[3 * count + 3][...]
    out[...] = total


def gram(at, pieces, side, received, kept, own, addend=None):
    sizes = tuple(n for n, _, _, _ in pieces)
    specs = [lanes_at_z(n, by_core) for n, by_core, _, _ in pieces] * 2
    for n, by_core, _, _ in pieces:
        specs.append(
            pl.BlockSpec(
                (n, 512),
                lambda g, at, by_core=by_core: (
                    at[AT_CORE] if by_core else 0,
                    at[AT_CORE] if own else 1 - at[AT_CORE],
                ),
            )
        )
    specs += [pl.BlockSpec(r.shape, lambda g, at: (0, 0)) for r in received]
    operands = [p[2] for p in pieces] + [p[3] for p in pieces] + [p[2 + side] for p in pieces] + list(received)
    if addend is not None:
        specs.append(pl.BlockSpec(addend.shape, lambda g, at: (0, 0)))
        operands.append(addend)
    return pl.pallas_call(
        functools.partial(gram_kernel, sizes, kept, addend is not None),
        grid_spec=pltpu.PrefetchScalarGridSpec(
            num_scalar_prefetch=1, grid=(1,), in_specs=specs,
            out_specs=pl.BlockSpec((256, 512), lambda g, at: (0, 0)),
        ),
        out_shape=jax.ShapeDtypeStruct((256, 512), jnp.float32),
        compiler_params=params(),
        cost_estimate=cost(2 * sum(sizes) * 256 * 512, 3 << 20),
        name="gram",
    )(at, *operands)


def finish_kernel(factor, low, high, low_got, high_got, out):
    for i in range(4):
        lanes = slice(i * 128, i * 128 + 128)
        out[:, i * 256 : i * 256 + 128] = (low[:, lanes] + low_got[:, lanes]) * factor
        out[:, i * 256 + 128 : i * 256 + 256] = (high[:, lanes] + high_got[:, lanes]) * factor


def finish(factor, terms):
    rows, columns = terms[0].shape
    return pl.pallas_call(
        functools.partial(finish_kernel, factor),
        grid=(2,),
        in_specs=[pl.BlockSpec((rows // 2, columns), lambda g: (g, 0))] * 4,
        out_specs=pl.BlockSpec((rows // 2, 2 * columns), lambda g: (g, 0)),
        out_shape=jax.ShapeDtypeStruct((rows, 2 * columns), jnp.float32),
        compiler_params=params(),
        cost_estimate=cost(1 << 19, 3 << 20),
        name="finish",
    )(*terms)


def fisher_block(mantissas, exps, total_rows):
    yh, z = lax.axis_index("yh"), lax.axis_index("z")
    yl, core = lax.axis_index("yl"), lax.axis_index("core")
    rows = mantissas.shape[0]
    far_block = (1 - yl) * Z + lax.rem(z + Z // 2, Z)
    at = jnp.stack([z, core, yl, far_block, yh]).astype(jnp.int32)
    low, high, far = dequant(at, exps, mantissas)
    far = lax.ppermute(far, "z", [(i, (i + Z // 2) % Z) for i in range(Z)])

    half = rows // 2
    pieces = [(half, True, low, high)]
    for step in range(1, Z // 2 + 1):
        if step == Z // 2:
            low = lax.dynamic_slice_in_dim(low, core * half, half, 0)
            high = lax.dynamic_slice_in_dim(high, core * half, half, 0)
        low = lax.ppermute(low, ("z", "core"), RING)
        high = lax.ppermute(high, ("z", "core"), RING)
        pieces.append((low.shape[0], False, low, high))
    near = lax.ppermute(pick(at, pieces[:3]), "yl", SWAP)
    third = lax.ppermute(pick(at, pieces[3:4]), "yl", SWAP)
    received = (near, third, far)

    given = [lax.ppermute(gram(at, pieces, s, received, False, False), "core", SWAP) for s in range(2)]
    given = [lax.ppermute(gram(at, pieces, s, received, False, True, given[s]), "yh", SWAP) for s in range(2)]
    kept = [lax.ppermute(gram(at, pieces, s, received, True, False), "core", SWAP) for s in range(2)]
    kept = [gram(at, pieces, s, received, True, True, kept[s]) for s in range(2)]
    return finish(1.0 / total_rows, kept + given)


def spread(scale):
    blocks = scale.shape[1]
    lane_block = jnp.arange(blocks * 128, dtype=jnp.int32) // 128
    pick = (lane_block[None, :] == jnp.arange(blocks, dtype=jnp.int32)[:, None]).astype(jnp.bfloat16)
    wide = lax.dot_general(scale, pick, (((1,), (0,)), ((), ())), preferred_element_type=jnp.float32)
    return wide.astype(jnp.bfloat16)


def score_block(mantissas, scale, queries, doc_ids, owners):
    docs = owners.shape[0]
    grads = mantissas * spread(scale)
    scores = lax.dot_general(queries, grads, (((1,), (1,)), ((), ())), preferred_element_type=jnp.float32)
    count, rows = scores.shape
    share = count // X
    summed = lax.all_to_all(scores.reshape(X, share, rows), "x", 0, 0, tiled=True).sum(0)
    slots = owners[doc_ids]
    own_docs = docs // (YH * Z)
    half = own_docs // 2
    place = jnp.arange(YH * Z, dtype=jnp.int32)[:, None] * own_docs + jnp.arange(half, dtype=jnp.int32)[None, :]
    place = place.reshape(-1, 1)
    member = jnp.concatenate([place == slots[None, :], place + half == slots[None, :]], 1).astype(jnp.float32)
    zero = jnp.zeros_like(summed)
    spaced = jnp.concatenate(
        [jnp.concatenate([summed, zero], 1), jnp.concatenate([zero, summed], 1)], 0
    )
    placed = lax.dot_general(
        member, spaced, (((1,), (1,)), ((), ())),
        precision=lax.Precision.HIGHEST, preferred_element_type=jnp.float32,
    )
    placed = placed.reshape(YH * Z, half, 2 * share)
    mine = lax.all_to_all(placed, ("yh", "z"), 0, 0, tiled=True).sum(0)
    every = lax.all_to_all(jnp.broadcast_to(mine[None], (X, half, 2 * share)), "x", 0, 0, tiled=True)
    return every.reshape(X, half, 2, share).transpose(2, 1, 0, 3).reshape(own_docs, count)


def per_device(mantissas, exponents, queries, doc_ids, owners):
    mantissas = mantissas[:, 0, :]
    exponents = exponents[:, 0, :]
    total_rows = mantissas.shape[0] * YH * Z
    fisher = fisher_block(mantissas, exponents.T, total_rows)
    doc_scores = score_block(mantissas, powers(exponents), queries[:, 0, :], doc_ids, owners)
    return fisher[None], doc_scores


def solution(mesh):
    fine = Mesh(mesh.devices.reshape(YH, Z, X, YL, CORE), ("yh", "z", "x", "yl", "core"))
    in_specs = (
        P(ROW_AXES, "x", None),
        P(ROW_AXES, "x", None),
        P(COL_AXES, "x", None),
        P(ROW_AXES),
        P(),
    )
    out_specs = (P("x", ROW_AXES, COL_AXES), P(ROW_AXES, COL_AXES))
    return jax.shard_map(per_device, mesh=fine, in_specs=in_specs, out_specs=out_specs, check_vma=False)
```

```python
import functools

import jax
import jax.numpy as jnp
from jax import lax
from jax.experimental import pallas as pl
from jax.experimental.pallas import tpu as pltpu
from jax.sharding import Mesh, PartitionSpec as P

YH, Z, X, YL, CORE = 2, 8, 4, 2, 2
ROW_AXES = ("yh", "z")
COL_AXES = ("yl", "core")
SWAP = [(0, 1), (1, 0)]
RING = [(2 * i, 2 * ((i + 1) % Z)) for i in range(Z)] + [(2 * i + 1, 2 * ((i - 1) % Z) + 1) for i in range(Z)]
TURNED = (((0,), (0,)), ((), ()))


def powers(exponents):
    return jnp.exp2(exponents.astype(jnp.float32)).astype(jnp.bfloat16)


def params(mebibytes):
    return pltpu.CompilerParams(vmem_limit_bytes=mebibytes << 20)


def cost(flops, moved):
    return pl.CostEstimate(flops=flops, bytes_accessed=moved, transcendentals=0)


AT_Z, AT_CORE, AT_YL, AT_FAR, AT_YH, AT_X = 0, 1, 2, 3, 4, 5


def wide_scale(turned, first_block, columns):
    blocks = turned.shape[0]
    lane_block = lax.broadcasted_iota(jnp.int32, (blocks, columns), 1) // 128 + first_block
    pick = (lane_block == lax.broadcasted_iota(jnp.int32, (blocks, columns), 0)).astype(jnp.bfloat16)
    return lax.dot_general(turned, pick, TURNED, preferred_element_type=jnp.float32)


def dequant_kernel(at, exps, values, far_values, low, high, far):
    step = pl.program_id(0)
    turned = powers(exps[...])
    grads = values[...].astype(jnp.float32) * wide_scale(turned, at[AT_YL] * 16 + step * 4, 512)
    grads = grads.astype(jnp.bfloat16)
    low[...] = jnp.concatenate([grads[:, 0:128], grads[:, 256:384]], 1)
    high[...] = jnp.concatenate([grads[:, 128:256], grads[:, 384:512]], 1)

    @pl.when(step == 0)
    def _():
        half = far.shape[0]
        scale = wide_scale(turned, at[AT_FAR] * 2, 256)
        scale = jnp.where(at[AT_CORE] == 0, scale[:half], scale[half:])
        far[...] = (far_values[...].astype(jnp.float32) * scale).astype(jnp.bfloat16)


def dequant(at, exps, mantissas):
    rows, width = mantissas.shape
    side = jax.ShapeDtypeStruct((rows, width // 4), jnp.bfloat16)
    return pl.pallas_call(
        dequant_kernel,
        grid_spec=pltpu.PrefetchScalarGridSpec(
            num_scalar_prefetch=1,
            grid=(4,),
            in_specs=[
                pl.BlockSpec(exps.shape, lambda g, at: (0, 0)),
                pl.BlockSpec((rows, 512), lambda g, at: (0, at[AT_YL] * 4 + g)),
                pl.BlockSpec((rows // 2, 256), lambda g, at: (at[AT_CORE], at[AT_FAR])),
            ],
            out_specs=[
                pl.BlockSpec((rows, 256), lambda g, at: (0, g)),
                pl.BlockSpec((rows, 256), lambda g, at: (0, g)),
                pl.BlockSpec((rows // 2, 256), lambda g, at: (0, 0)),
            ],
        ),
        out_shape=[side, side, jax.ShapeDtypeStruct((rows // 2, 256), jnp.bfloat16)],
        compiler_params=params(58),
        cost_estimate=cost(1 << 25, 2 << 20),
        name="dequant",
    )(at, exps, mantissas, mantissas)


def pick_kernel(count, at, *refs):
    sides, out = refs[:-1], refs[-1]
    row = 0
    for i in range(count):
        rows = sides[2 * i].shape[0]
        out[row : row + rows] = jnp.concatenate([sides[2 * i][...], sides[2 * i + 1][...]], 1)
        row += rows


def lanes_at_z(rows, by_core):
    if by_core:
        return pl.BlockSpec((rows, 128), lambda g, at: (at[AT_CORE], at[AT_Z]))
    return pl.BlockSpec((rows, 128), lambda g, at: (0, at[AT_Z]))


def pick(at, pieces):
    rows = sum(n for n, _, _, _ in pieces)
    specs = [lanes_at_z(n, by_core) for n, by_core, _, _ in pieces for _ in range(2)]
    return pl.pallas_call(
        functools.partial(pick_kernel, len(pieces)),
        grid_spec=pltpu.PrefetchScalarGridSpec(
            num_scalar_prefetch=1, grid=(1,), in_specs=specs,
            out_specs=pl.BlockSpec((rows, 256), lambda g, at: (0, 0)),
        ),
        out_shape=jax.ShapeDtypeStruct((rows, 256), jnp.bfloat16),
        compiler_params=params(6),
        cost_estimate=cost(0, rows * 1024),
        name="pick",
    )(at, *[side for _, _, low, high in pieces for side in (low, high)])


def gram_kernel(sizes, kept, at, *refs):
    count = len(sizes)
    lows, highs = refs[:count], refs[count : 2 * count]
    low_rights, high_rights = refs[2 * count : 3 * count], refs[3 * count : 4 * count]
    near, third, far = refs[4 * count : 4 * count + 3]
    low_other, high_other, low_own, high_own = refs[4 * count + 3 : 4 * count + 7]
    left = refs[-1]
    step = pl.program_id(0)

    @pl.when(step == 0)
    def _():
        mine_first = at[AT_YL] == at[AT_YH]
        use_mine = mine_first if kept else jnp.logical_not(mine_first)
        row, start = 0, 0
        for i, rows in enumerate(sizes):
            mine = jnp.concatenate([lows[i][...], highs[i][...]], 1)
            if i < count - 2:
                theirs = near[row : row + rows]
                row += rows
            else:
                theirs = third[...] if i == count - 2 else far[...]
            left[start : start + rows] = jnp.where(use_mine, mine, theirs)
            start += rows

    def terms(rights):
        total, start = None, 0
        for i, rows in enumerate(sizes):
            term = lax.dot_general(
                left[start : start + rows], rights[i][...], TURNED, preferred_element_type=jnp.float32
            )
            total = term if total is None else total + term
            start += rows
        return total

    @pl.when(step == 0)
    def _():
        low_other[...] = terms(low_rights)
        high_other[...] = terms(high_rights)

    @pl.when(step == 1)
    def _():
        low_own[...] = terms(low_rights)
        high_own[...] = terms(high_rights)


def gram(at, pieces, received, kept):
    sizes = tuple(n for n, _, _, _ in pieces)
    specs = [lanes_at_z(n, by_core) for n, by_core, _, _ in pieces] * 2
    for n, by_core, _, _ in pieces:
        specs.append(
            pl.BlockSpec(
                (n, 512),
                lambda g, at, by_core=by_core: (
                    at[AT_CORE] if by_core else 0,
                    (1 - g) * (1 - at[AT_CORE]) + g * at[AT_CORE],
                ),
            )
        )
    specs += specs[-len(pieces) :]
    specs += [pl.BlockSpec(r.shape, lambda g, at: (0, 0)) for r in received]
    sides = [p[2] for p in pieces], [p[3] for p in pieces]
    return pl.pallas_call(
        functools.partial(gram_kernel, sizes, kept),
        grid_spec=pltpu.PrefetchScalarGridSpec(
            num_scalar_prefetch=1, grid=(2,), in_specs=specs,
            out_specs=[pl.BlockSpec((256, 512), lambda g, at: (0, 0))] * 4,
            scratch_shapes=[pltpu.VMEM((sum(sizes), 256), jnp.bfloat16)],
        ),
        out_shape=[jax.ShapeDtypeStruct((256, 512), jnp.float32)] * 4,
        compiler_params=params(20),
        cost_estimate=cost(2 * sum(sizes) * 256 * 2048, 7 << 20),
        name="gram",
    )(at, *sides[0], *sides[1], *sides[0], *sides[1], *received)


def add_kernel(left, right, out):
    out[...] = left[...] + right[...]


def add(left, right):
    rows, columns = left.shape
    spec = pl.BlockSpec((rows // 2, columns), lambda g: (g, 0))
    return pl.pallas_call(
        add_kernel,
        grid=(2,),
        in_specs=[spec, spec],
        out_specs=spec,
        out_shape=jax.ShapeDtypeStruct(left.shape, left.dtype),
        compiler_params=params(6),
        cost_estimate=cost(1 << 18, 3 << 19),
        name="add",
    )(left, right)


def finish_kernel(factor, low, high, low_core, high_core, low_got, high_got, out):
    for i in range(4):
        lanes = slice(i * 128, i * 128 + 128)
        first = (low[:, lanes] + low_core[:, lanes]) + low_got[:, lanes]
        second = (high[:, lanes] + high_core[:, lanes]) + high_got[:, lanes]
        out[:, i * 256 : i * 256 + 128] = first * factor
        out[:, i * 256 + 128 : i * 256 + 256] = second * factor


def finish(factor, terms):
    rows, columns = terms[0].shape
    return pl.pallas_call(
        functools.partial(finish_kernel, factor),
        grid=(4,),
        in_specs=[pl.BlockSpec((rows // 4, columns), lambda g: (g, 0))] * 6,
        out_specs=pl.BlockSpec((rows // 4, 2 * columns), lambda g: (g, 0)),
        out_shape=jax.ShapeDtypeStruct((rows, 2 * columns), jnp.float32),
        compiler_params=params(8),
        cost_estimate=cost(1 << 20, 4 << 20),
        name="finish",
    )(*terms)


def tie_kernel(*refs):
    del refs


def tie(value, *earlier):
    return pl.pallas_call(
        tie_kernel,
        in_specs=[pl.BlockSpec(memory_space=pl.ANY)] * (1 + len(earlier)),
        out_specs=pl.BlockSpec(memory_space=pl.ANY),
        out_shape=jax.ShapeDtypeStruct(value.shape, value.dtype),
        input_output_aliases={0: 0},
        compiler_params=params(1),
        cost_estimate=cost(0, 0),
        name="tie",
    )(value, *earlier)


def fisher_block(at, mantissas, exps, total_rows, stages):
    core = lax.axis_index("core")
    rows = mantissas.shape[0]
    low, high, far = dequant(at, exps, mantissas)

    half = rows // 2
    pieces = [(half, True, low, high)]
    for step in range(1, Z // 2 + 1):
        if step == Z // 2:
            low = lax.dynamic_slice_in_dim(low, core * half, half, 0)
            high = lax.dynamic_slice_in_dim(high, core * half, half, 0)
        low = lax.ppermute(low, ("z", "core"), RING)
        high = lax.ppermute(high, ("z", "core"), RING)
        if step == 1:
            far = lax.ppermute(far, "z", [(i, (i + Z // 2) % Z) for i in range(Z)])
        if step < Z // 2:
            low = tie(low, stages[step - 1])
        pieces.append((low.shape[0], False, low, high))
    near = lax.ppermute(pick(at, pieces[:3]), "yl", SWAP)
    third = lax.ppermute(pick(at, pieces[3:4]), "yl", SWAP)
    received = (near, third, far)

    *given_other, low_given, high_given = gram(at, pieces, received, False)
    swapped = [lax.ppermute(g, "core", SWAP) for g in given_other]
    given = [lax.ppermute(add(g, s), "yh", SWAP) for g, s in zip((low_given, high_given), swapped)]
    *kept_other, low_kept, high_kept = gram(at, pieces, received, True)
    kept = [lax.ppermute(k, "core", SWAP) for k in kept_other]
    return finish(1.0 / total_rows, [low_kept, high_kept, *kept, *given])


def spread(scale):
    blocks = scale.shape[1]
    lane_block = jnp.arange(blocks * 128, dtype=jnp.int32) // 128
    pick = (lane_block[None, :] == jnp.arange(blocks, dtype=jnp.int32)[:, None]).astype(jnp.bfloat16)
    wide = lax.dot_general(scale, pick, (((1,), (0,)), ((), ())), preferred_element_type=jnp.float32)
    return wide.astype(jnp.bfloat16)


def place_kernel(parts, ids, owners, out):
    docs, rows = owners.shape[1], ids.shape[1]
    summed = (parts[0] + parts[1]) + (parts[2] + parts[3])
    owner = jnp.broadcast_to(owners[...], (8, docs))
    digit = jnp.where(lax.broadcasted_iota(jnp.int32, (8, docs), 0) == 0, owner >> 5, owner & 31)
    doc = (lax.broadcasted_iota(jnp.int32, (docs, rows), 0) == ids[...]).astype(jnp.bfloat16)
    digits = lax.dot_general(
        digit.astype(jnp.float32).astype(jnp.bfloat16), doc, (((1,), (0,)), ((), ())),
        preferred_element_type=jnp.float32,
    )
    slots = (digits[0:1] * 32.0 + digits[1:2]).astype(jnp.int32)
    count = out.shape[0]
    own_docs = docs // (YH * Z)
    half = own_docs // 2
    place = lax.broadcasted_iota(jnp.int32, (count, rows), 0)
    place = (place // half) * own_docs + place % half
    member = jnp.concatenate([place == slots, place + half == slots], 1)
    member = jnp.where(member, 1.0, 0.0).astype(jnp.bfloat16)
    zero = jnp.zeros_like(summed)
    rest = jnp.concatenate(
        [jnp.concatenate([summed, zero], 1), jnp.concatenate([zero, summed], 1)], 0
    )
    total = None
    for _ in range(3):
        part = rest.astype(jnp.bfloat16)
        rest = rest - part.astype(jnp.float32)
        term = lax.dot_general(member, part, (((1,), (1,)), ((), ())), preferred_element_type=jnp.float32)
        total = term if total is None else total + term
    out[...] = total


def sum_kernel(parts, out):
    total = parts[0]
    for i in range(1, parts.shape[0]):
        total = total + parts[i]
    out[...] = total


def assemble_kernel(at, *refs):
    parts, out = refs[:-1], refs[-1]
    half, double = parts[0].shape
    share = double // 2
    values = []
    for source in range(X):
        value = parts[0][...]
        for shift in range(1, X):
            value = jnp.where(lax.rem(source + shift, X) == at[AT_X], parts[shift][...], value)
        values.append(value)
    out[0:half] = jnp.concatenate([v[:, :share] for v in values], 1)
    out[half:] = jnp.concatenate([v[:, share:] for v in values], 1)


def score_stages(mantissas, scale, queries, doc_ids, owners):
    docs = owners.shape[0]
    grads = mantissas * spread(scale)
    scores = lax.dot_general(queries, grads, (((1,), (1,)), ((), ())), preferred_element_type=jnp.float32)
    count, rows = scores.shape
    share, half = count // X, docs // (YH * Z) // 2
    parts = lax.all_to_all(scores.reshape(X, share, rows), "x", 0, 0, tiled=True)
    placed = pl.pallas_call(
        place_kernel,
        out_shape=jax.ShapeDtypeStruct((YH * Z * half, 2 * share), jnp.float32),
        compiler_params=params(10),
        cost_estimate=cost(1 << 28, 1 << 20),
        name="place",
    )(parts, doc_ids.reshape(1, rows), owners.reshape(1, docs))
    blocks = lax.all_to_all(placed.reshape(YH * Z, half, 2 * share), ("yh", "z"), 0, 0, tiled=True)
    mine = pl.pallas_call(
        sum_kernel,
        out_shape=jax.ShapeDtypeStruct((half, 2 * share), jnp.float32),
        compiler_params=params(4),
        cost_estimate=cost(1 << 16, 1 << 18),
        name="sum",
    )(blocks)
    return scores, placed, mine


def assemble(at, mine):
    half, double = mine.shape
    parts = [mine] + [lax.ppermute(mine, "x", [(i, (i + s) % X) for i in range(X)]) for s in range(1, X)]
    return pl.pallas_call(
        assemble_kernel,
        grid_spec=pltpu.PrefetchScalarGridSpec(
            num_scalar_prefetch=1, grid=(1,),
            in_specs=[pl.BlockSpec((half, double), lambda g, at: (0, 0))] * X,
            out_specs=pl.BlockSpec((2 * half, X * double // 2), lambda g, at: (0, 0)),
        ),
        out_shape=jax.ShapeDtypeStruct((2 * half, X * double // 2), jnp.float32),
        compiler_params=params(2),
        cost_estimate=cost(0, 1 << 17),
        name="assemble",
    )(at, *parts)


def per_device(mantissas, exponents, queries, doc_ids, owners):
    mantissas = mantissas[:, 0, :]
    exponents = exponents[:, 0, :]
    total_rows = mantissas.shape[0] * YH * Z
    yh, z, x = lax.axis_index("yh"), lax.axis_index("z"), lax.axis_index("x")
    yl, core = lax.axis_index("yl"), lax.axis_index("core")
    far_block = (1 - yl) * Z + lax.rem(z + Z // 2, Z)
    at = jnp.stack([z, core, yl, far_block, yh, x]).astype(jnp.int32)
    stages = score_stages(mantissas, powers(exponents), queries[:, 0, :], doc_ids, owners)
    fisher = fisher_block(at, mantissas, exponents.T, total_rows, stages)
    return fisher[None], assemble(at, stages[-1])


def solution(mesh):
    fine = Mesh(mesh.devices.reshape(YH, Z, X, YL, CORE), ("yh", "z", "x", "yl", "core"))
    in_specs = (
        P(ROW_AXES, "x", None),
        P(ROW_AXES, "x", None),
        P(COL_AXES, "x", None),
        P(ROW_AXES),
        P(),
    )
    out_specs = (P("x", ROW_AXES, COL_AXES), P(ROW_AXES, COL_AXES))
    return jax.shard_map(per_device, mesh=fine, in_specs=in_specs, out_specs=out_specs, check_vma=False)
```

```python
import functools

import jax
import jax.numpy as jnp
from jax import lax
from jax.experimental import pallas as pl
from jax.experimental.pallas import tpu as pltpu
from jax.sharding import Mesh, PartitionSpec as P

YH, Z, X, YL, CORE = 2, 8, 4, 2, 2
ROW_AXES = ("yh", "z")
COL_AXES = ("yl", "core")
SWAP = [(0, 1), (1, 0)]
RING = [(2 * i, 2 * ((i + 1) % Z)) for i in range(Z)] + [(2 * i + 1, 2 * ((i - 1) % Z) + 1) for i in range(Z)]
TURNED = (((0,), (0,)), ((), ()))


def powers(exponents):
    return jnp.exp2(exponents.astype(jnp.float32)).astype(jnp.bfloat16)


def params(mebibytes):
    return pltpu.CompilerParams(vmem_limit_bytes=mebibytes << 20)


def cost(flops, moved):
    return pl.CostEstimate(flops=flops, bytes_accessed=moved, transcendentals=0)


AT_Z, AT_CORE, AT_YL, AT_OWN, AT_FAR, AT_YH, AT_X = 0, 1, 2, 3, 4, 5, 6


def wide_scale(turned, first_block, columns):
    blocks = turned.shape[0]
    lane_block = lax.broadcasted_iota(jnp.int32, (blocks, columns), 1) // 128 + first_block
    pick = (lane_block == lax.broadcasted_iota(jnp.int32, (blocks, columns), 0)).astype(jnp.bfloat16)
    return lax.dot_general(turned, pick, TURNED, preferred_element_type=jnp.float32)


def dequant_kernel(at, exps, values, own_values, far_values, low, high, own, far):
    step = pl.program_id(0)
    turned = powers(exps[...])
    grads = values[...].astype(jnp.float32) * wide_scale(turned, at[AT_YL] * 16 + step * 4, 512)
    grads = grads.astype(jnp.bfloat16)
    low[...] = jnp.concatenate([grads[:, 0:128], grads[:, 256:384]], 1)
    high[...] = jnp.concatenate([grads[:, 128:256], grads[:, 384:512]], 1)

    @pl.when(step == 0)
    def _():
        half = far.shape[0]
        for block, source, result in ((AT_OWN, own_values, own), (AT_FAR, far_values, far)):
            scale = wide_scale(turned, at[block] * 2, 256)
            scale = jnp.where(at[AT_CORE] == 0, scale[:half], scale[half:])
            result[...] = (source[...].astype(jnp.float32) * scale).astype(jnp.bfloat16)


def dequant(at, exps, mantissas):
    rows, width = mantissas.shape
    side = jax.ShapeDtypeStruct((rows, width // 4), jnp.bfloat16)
    return pl.pallas_call(
        dequant_kernel,
        grid_spec=pltpu.PrefetchScalarGridSpec(
            num_scalar_prefetch=1,
            grid=(4,),
            in_specs=[
                pl.BlockSpec(exps.shape, lambda g, at: (0, 0)),
                pl.BlockSpec((rows, 512), lambda g, at: (0, at[AT_YL] * 4 + g)),
                pl.BlockSpec((rows // 2, 256), lambda g, at: (at[AT_CORE], at[AT_OWN])),
                pl.BlockSpec((rows // 2, 256), lambda g, at: (at[AT_CORE], at[AT_FAR])),
            ],
            out_specs=[
                pl.BlockSpec((rows, 256), lambda g, at: (0, g)),
                pl.BlockSpec((rows, 256), lambda g, at: (0, g)),
                pl.BlockSpec((rows // 2, 256), lambda g, at: (0, 0)),
                pl.BlockSpec((rows // 2, 256), lambda g, at: (0, 0)),
            ],
        ),
        out_shape=[side, side] + [jax.ShapeDtypeStruct((rows // 2, 256), jnp.bfloat16)] * 2,
        compiler_params=params(58),
        cost_estimate=cost(1 << 25, 2 << 20),
        name="dequant",
    )(at, exps, mantissas, mantissas, mantissas)


def pick_kernel(count, at, *refs):
    sides, out = refs[:-1], refs[-1]
    row = 0
    for i in range(count):
        rows = sides[2 * i].shape[0]
        out[row : row + rows] = jnp.concatenate([sides[2 * i][...], sides[2 * i + 1][...]], 1)
        row += rows


def lanes_at_z(rows, by_core):
    if by_core:
        return pl.BlockSpec((rows, 128), lambda g, at: (at[AT_CORE], at[AT_Z]))
    return pl.BlockSpec((rows, 128), lambda g, at: (0, at[AT_Z]))


def pick(at, pieces):
    rows = sum(n for n, _, _, _ in pieces)
    specs = [lanes_at_z(n, by_core) for n, by_core, _, _ in pieces for _ in range(2)]
    return pl.pallas_call(
        functools.partial(pick_kernel, len(pieces)),
        grid_spec=pltpu.PrefetchScalarGridSpec(
            num_scalar_prefetch=1, grid=(1,), in_specs=specs,
            out_specs=pl.BlockSpec((rows, 256), lambda g, at: (0, 0)),
        ),
        out_shape=jax.ShapeDtypeStruct((rows, 256), jnp.bfloat16),
        compiler_params=params(6),
        cost_estimate=cost(0, rows * 1024),
        name="pick",
    )(at, *[side for _, _, low, high in pieces for side in (low, high)])


def gram_kernel(sizes, kept, at, *refs):
    count = len(sizes)
    lows, highs = refs[:count], refs[count : 2 * count]
    low_rights, high_rights = refs[2 * count : 3 * count], refs[3 * count : 4 * count]
    own, near, third, far = refs[4 * count : 4 * count + 4]
    low_other, high_other, low_own, high_own = refs[-5:-1]
    left = refs[-1]
    step = pl.program_id(0)

    @pl.when(step == 0)
    def _():
        mine_first = at[AT_YL] == at[AT_YH]
        use_mine = mine_first if kept else jnp.logical_not(mine_first)
        row, start = 0, 0
        for i, rows in enumerate(sizes):
            mine = jnp.concatenate([lows[i][...], highs[i][...]], 1)
            if 0 < i < count - 2:
                theirs = near[row : row + rows]
                row += rows
            else:
                theirs = (own if i == 0 else third if i == count - 2 else far)[...]
            left[start : start + rows] = jnp.where(use_mine, mine, theirs)
            start += rows

    def terms(rights):
        total, start = None, 0
        for i, rows in enumerate(sizes):
            term = lax.dot_general(
                left[start : start + rows], rights[i][...], TURNED, preferred_element_type=jnp.float32
            )
            total = term if total is None else total + term
            start += rows
        return total

    @pl.when(step == 0)
    def _():
        low_other[...] = terms(low_rights)
        high_other[...] = terms(high_rights)

    @pl.when(step == 1)
    def _():
        low_own[...] = terms(low_rights)
        high_own[...] = terms(high_rights)


def gram(at, pieces, received, kept, *after):
    sizes = tuple(n for n, _, _, _ in pieces)
    specs = [lanes_at_z(n, by_core) for n, by_core, _, _ in pieces] * 2
    for n, by_core, _, _ in pieces:
        specs.append(
            pl.BlockSpec(
                (n, 512),
                lambda g, at, by_core=by_core: (
                    at[AT_CORE] if by_core else 0,
                    (1 - g) * (1 - at[AT_CORE]) + g * at[AT_CORE],
                ),
            )
        )
    specs += specs[-len(pieces) :]
    specs += [pl.BlockSpec(r.shape, lambda g, at: (0, 0)) for r in received]
    specs += [pl.BlockSpec(memory_space=pl.ANY)] * len(after)
    sides = [p[2] for p in pieces], [p[3] for p in pieces]
    return pl.pallas_call(
        functools.partial(gram_kernel, sizes, kept),
        grid_spec=pltpu.PrefetchScalarGridSpec(
            num_scalar_prefetch=1, grid=(2,), in_specs=specs,
            out_specs=[pl.BlockSpec((256, 512), lambda g, at: (0, 0))] * 4,
            scratch_shapes=[pltpu.VMEM((sum(sizes), 256), jnp.bfloat16)],
        ),
        out_shape=[jax.ShapeDtypeStruct((256, 512), jnp.float32)] * 4,
        compiler_params=params(20),
        cost_estimate=cost(2 * sum(sizes) * 256 * 2048, 7 << 20),
        name="gram",
    )(at, *sides[0], *sides[1], *sides[0], *sides[1], *received, *after)


def add_kernel(left, right, out):
    out[...] = left[...] + right[...]


def add(left, right):
    rows, columns = left.shape
    spec = pl.BlockSpec((rows // 2, columns), lambda g: (g, 0))
    return pl.pallas_call(
        add_kernel,
        grid=(2,),
        in_specs=[spec, spec],
        out_specs=spec,
        out_shape=jax.ShapeDtypeStruct(left.shape, left.dtype),
        compiler_params=params(6),
        cost_estimate=cost(1 << 18, 3 << 19),
        name="add",
    )(left, right)


def finish_kernel(factor, low, high, low_core, high_core, low_got, high_got, out):
    for i in range(4):
        lanes = slice(i * 128, i * 128 + 128)
        first = (low[:, lanes] + low_core[:, lanes]) + low_got[:, lanes]
        second = (high[:, lanes] + high_core[:, lanes]) + high_got[:, lanes]
        out[:, i * 256 : i * 256 + 128] = first * factor
        out[:, i * 256 + 128 : i * 256 + 256] = second * factor


def finish(factor, terms):
    rows, columns = terms[0].shape
    return pl.pallas_call(
        functools.partial(finish_kernel, factor),
        grid=(4,),
        in_specs=[pl.BlockSpec((rows // 4, columns), lambda g: (g, 0))] * 6,
        out_specs=pl.BlockSpec((rows // 4, 2 * columns), lambda g: (g, 0)),
        out_shape=jax.ShapeDtypeStruct((rows, 2 * columns), jnp.float32),
        compiler_params=params(8),
        cost_estimate=cost(1 << 20, 4 << 20),
        name="finish",
    )(*terms)


def tie_kernel(*refs):
    del refs


def tie(value, *earlier):
    return pl.pallas_call(
        tie_kernel,
        in_specs=[pl.BlockSpec(memory_space=pl.ANY)] * (1 + len(earlier)),
        out_specs=pl.BlockSpec(memory_space=pl.ANY),
        out_shape=jax.ShapeDtypeStruct(value.shape, value.dtype),
        input_output_aliases={0: 0},
        compiler_params=params(1),
        cost_estimate=cost(0, 0),
        name="tie",
    )(value, *earlier)


def fisher_terms(at, mantissas, exps, scores, placed):
    core = lax.axis_index("core")
    rows = mantissas.shape[0]
    low, high, own, far = dequant(at, exps, mantissas)

    half = rows // 2
    pieces = [(half, True, low, high)]
    for step in range(1, Z // 2 + 1):
        if step == Z // 2:
            low = lax.dynamic_slice_in_dim(low, core * half, half, 0)
            high = lax.dynamic_slice_in_dim(high, core * half, half, 0)
        low = lax.ppermute(low, ("z", "core"), RING)
        high = lax.ppermute(high, ("z", "core"), RING)
        if step == 1:
            far = lax.ppermute(far, "z", [(i, (i + Z // 2) % Z) for i in range(Z)])
            low = tie(low, far, scores)
        if step == 3:
            low = tie(low, placed)
        pieces.append((low.shape[0], False, low, high))
    near = lax.ppermute(pick(at, pieces[1:3]), "yl", SWAP)
    third = pick(at, pieces[3:4])
    mine = own_slots(tie(placed, third))
    third = lax.ppermute(third, "yl", SWAP)
    received = (own, near, third, far)

    *given_other, low_given, high_given = gram(at, pieces, received, False)
    swapped = [lax.ppermute(g, "core", SWAP) for g in given_other]
    *kept_other, low_kept, high_kept = gram(at, pieces, received, True, mine)
    given = [add(g, s) for g, s in zip((low_given, high_given), swapped)]
    kept = [lax.ppermute(k, "core", SWAP) for k in kept_other]
    return given, [low_kept, high_kept, *kept], mine


def spread(scale):
    blocks = scale.shape[1]
    lane_block = jnp.arange(blocks * 128, dtype=jnp.int32) // 128
    pick = (lane_block[None, :] == jnp.arange(blocks, dtype=jnp.int32)[:, None]).astype(jnp.bfloat16)
    wide = lax.dot_general(scale, pick, (((1,), (0,)), ((), ())), preferred_element_type=jnp.float32)
    return wide.astype(jnp.bfloat16)


def place_kernel(at, pair, got, ids, owners, out):
    docs, rows = owners.shape[1], ids.shape[1]
    summed = jnp.where(at[AT_X] % 2 == 0, pair[0], pair[1]) + got[...]
    owner = jnp.broadcast_to(owners[...], (8, docs))
    digit = jnp.where(lax.broadcasted_iota(jnp.int32, (8, docs), 0) == 0, owner >> 5, owner & 31)
    doc = (lax.broadcasted_iota(jnp.int32, (docs, rows), 0) == ids[...]).astype(jnp.bfloat16)
    digits = lax.dot_general(
        digit.astype(jnp.float32).astype(jnp.bfloat16), doc, (((1,), (0,)), ((), ())),
        preferred_element_type=jnp.float32,
    )
    slots = (digits[0:1] * 32.0 + digits[1:2]).astype(jnp.int32)
    count = out.shape[0]
    own_docs = docs // (YH * Z)
    half = own_docs // 2
    place = lax.broadcasted_iota(jnp.int32, (count, rows), 0)
    place = (place // half) * own_docs + place % half
    member = jnp.concatenate([place == slots, place + half == slots], 1)
    member = jnp.where(member, 1.0, 0.0).astype(jnp.bfloat16)
    zero = jnp.zeros_like(summed)
    rest = jnp.concatenate(
        [jnp.concatenate([summed, zero], 1), jnp.concatenate([zero, summed], 1)], 0
    )
    total = None
    for _ in range(3):
        part = rest.astype(jnp.bfloat16)
        rest = rest - part.astype(jnp.float32)
        term = lax.dot_general(member, part, (((1,), (1,)), ((), ())), preferred_element_type=jnp.float32)
        total = term if total is None else total + term
    out[...] = total


def sum_kernel(parts, out):
    total = parts[0]
    for i in range(1, parts.shape[0]):
        total = total + parts[i]
    out[...] = total


def flipped(bit):
    return [(i, i ^ bit) for i in range(X)]


def whole(shape):
    return pl.BlockSpec(shape, lambda g, at: (0,) * len(shape))


def placed_scores(at, mantissas, scale, queries, doc_ids, owners):
    docs = owners.shape[0]
    x = lax.axis_index("x")
    grads = mantissas * spread(scale)
    scores = lax.dot_general(queries, grads, (((1,), (1,)), ((), ())), preferred_element_type=jnp.float32)
    count, rows = scores.shape
    share, half = count // X, docs // (YH * Z) // 2
    upper = x // 2
    got = lax.ppermute(lax.dynamic_slice_in_dim(scores, (1 - upper) * 2 * share, 2 * share, 0), "x", flipped(2))
    pair = lax.dynamic_slice_in_dim(scores, upper * 2 * share, 2 * share, 0) + got
    got = lax.ppermute(lax.dynamic_slice_in_dim(pair, (1 - x % 2) * share, share, 0), "x", flipped(1))
    shapes = (X // 2, share, rows), (share, rows), (1, rows), (1, docs)
    placed = pl.pallas_call(
        place_kernel,
        grid_spec=pltpu.PrefetchScalarGridSpec(
            num_scalar_prefetch=1, grid=(1,), in_specs=[whole(shape) for shape in shapes],
            out_specs=whole((YH * Z * half, 2 * share)),
        ),
        out_shape=jax.ShapeDtypeStruct((YH * Z * half, 2 * share), jnp.float32),
        compiler_params=params(10),
        cost_estimate=cost(1 << 28, 1 << 20),
        name="place",
    )(at, pair.reshape(shapes[0]), got, doc_ids.reshape(1, rows), owners.reshape(1, docs))
    return scores, placed


def assemble_kernel(at, pair, far_pair, out):
    half, double = pair.shape[1:]
    share = double // 2
    values = []
    for source in range(X):
        near = (source // 2) == at[AT_X] // 2
        first = (source % 2) == at[AT_X] % 2
        own = jnp.where(first, pair[0], pair[1])
        other = jnp.where(first, far_pair[0], far_pair[1])
        values.append(jnp.where(near, own, other))
    out[0:half] = jnp.concatenate([v[:, :share] for v in values], 1)
    out[half:] = jnp.concatenate([v[:, share:] for v in values], 1)


def own_slots(placed):
    double = placed.shape[1]
    half = placed.shape[0] // (YH * Z)
    blocks = lax.all_to_all(placed.reshape(YH * Z, half, double), ("yh", "z"), 0, 0, tiled=True)
    return pl.pallas_call(
        sum_kernel,
        out_shape=jax.ShapeDtypeStruct((half, double), jnp.float32),
        compiler_params=params(4),
        cost_estimate=cost(1 << 16, 1 << 18),
        name="sum",
    )(blocks)


def doc_block(at, mine):
    half, double = mine.shape
    pair = jnp.stack([mine, lax.ppermute(mine, "x", flipped(1))])
    far_pair = lax.ppermute(pair, "x", flipped(2))
    return pl.pallas_call(
        assemble_kernel,
        grid_spec=pltpu.PrefetchScalarGridSpec(
            num_scalar_prefetch=1, grid=(1,), in_specs=[whole(pair.shape)] * 2,
            out_specs=whole((2 * half, X * double // 2)),
        ),
        out_shape=jax.ShapeDtypeStruct((2 * half, X * double // 2), jnp.float32),
        compiler_params=params(2),
        cost_estimate=cost(0, 1 << 17),
        name="assemble",
    )(at, pair, far_pair)


def per_device(mantissas, exponents, queries, doc_ids, owners):
    mantissas = mantissas[:, 0, :]
    exponents = exponents[:, 0, :]
    total_rows = mantissas.shape[0] * YH * Z
    yh, z, x = lax.axis_index("yh"), lax.axis_index("z"), lax.axis_index("x")
    yl, core = lax.axis_index("yl"), lax.axis_index("core")
    other = (1 - yl) * Z
    at = jnp.stack([z, core, yl, other + z, other + lax.rem(z + Z // 2, Z), yh, x]).astype(jnp.int32)
    scores, placed = placed_scores(at, mantissas, powers(exponents), queries[:, 0, :], doc_ids, owners)
    given, kept, mine = fisher_terms(at, mantissas, exponents.T, scores, placed)
    got = [lax.ppermute(g, "yh", SWAP) for g in given]
    return finish(1.0 / total_rows, kept + got)[None], doc_block(at, mine)


def solution(mesh):
    fine = Mesh(mesh.devices.reshape(YH, Z, X, YL, CORE), ("yh", "z", "x", "yl", "core"))
    in_specs = (
        P(ROW_AXES, "x", None),
        P(ROW_AXES, "x", None),
        P(COL_AXES, "x", None),
        P(ROW_AXES),
        P(),
    )
    out_specs = (P("x", ROW_AXES, COL_AXES), P(ROW_AXES, COL_AXES))
    return jax.shard_map(per_device, mesh=fine, in_specs=in_specs, out_specs=out_specs, check_vma=False)
```

```python
import functools

import jax
import jax.numpy as jnp
from jax import lax
from jax.experimental import pallas as pl
from jax.experimental.pallas import tpu as pltpu
from jax.sharding import Mesh, PartitionSpec as P

YH, Z, X, YL, CORE = 2, 8, 4, 2, 2
ROW_AXES = ("yh", "z")
COL_AXES = ("yl", "core")
SWAP = [(0, 1), (1, 0)]
RING = [(2 * i, 2 * ((i + 1) % Z)) for i in range(Z)] + [(2 * i + 1, 2 * ((i - 1) % Z) + 1) for i in range(Z)]
TURNED = (((0,), (0,)), ((), ()))


def powers(exponents):
    return jnp.exp2(exponents.astype(jnp.float32)).astype(jnp.bfloat16)


def params(mebibytes):
    return pltpu.CompilerParams(vmem_limit_bytes=mebibytes << 20)


def cost(flops, moved):
    return pl.CostEstimate(flops=flops, bytes_accessed=moved, transcendentals=0)


AT_Z, AT_CORE, AT_YL, AT_OWN, AT_FAR, AT_YH, AT_X = 0, 1, 2, 3, 4, 5, 6


def wide_scale(turned, first_block, columns):
    blocks = turned.shape[0]
    lane_block = lax.broadcasted_iota(jnp.int32, (blocks, columns), 1) // 128 + first_block
    pick = (lane_block == lax.broadcasted_iota(jnp.int32, (blocks, columns), 0)).astype(jnp.bfloat16)
    return lax.dot_general(turned, pick, TURNED, preferred_element_type=jnp.float32)


def dequant_kernel(at, exps, values, own_values, far_values, low, high, own, far):
    step = pl.program_id(0)
    turned = powers(exps[...])
    grads = values[...].astype(jnp.float32) * wide_scale(turned, at[AT_YL] * 16 + step * 4, 512)
    grads = grads.astype(jnp.bfloat16)
    low[...] = jnp.concatenate([grads[:, 0:128], grads[:, 256:384]], 1)
    high[...] = jnp.concatenate([grads[:, 128:256], grads[:, 384:512]], 1)

    @pl.when(step == 0)
    def _():
        half = far.shape[0]
        for block, source, result in ((AT_OWN, own_values, own), (AT_FAR, far_values, far)):
            scale = wide_scale(turned, at[block] * 2, 256)
            scale = jnp.where(at[AT_CORE] == 0, scale[:half], scale[half:])
            result[...] = (source[...].astype(jnp.float32) * scale).astype(jnp.bfloat16)


def dequant(at, exps, mantissas):
    rows, width = mantissas.shape
    side = jax.ShapeDtypeStruct((rows, width // 4), jnp.bfloat16)
    return pl.pallas_call(
        dequant_kernel,
        grid_spec=pltpu.PrefetchScalarGridSpec(
            num_scalar_prefetch=1,
            grid=(4,),
            in_specs=[
                pl.BlockSpec(exps.shape, lambda g, at: (0, 0)),
                pl.BlockSpec((rows, 512), lambda g, at: (0, at[AT_YL] * 4 + g)),
                pl.BlockSpec((rows // 2, 256), lambda g, at: (at[AT_CORE], at[AT_OWN])),
                pl.BlockSpec((rows // 2, 256), lambda g, at: (at[AT_CORE], at[AT_FAR])),
            ],
            out_specs=[
                pl.BlockSpec((rows, 256), lambda g, at: (0, g)),
                pl.BlockSpec((rows, 256), lambda g, at: (0, g)),
                pl.BlockSpec((rows // 2, 256), lambda g, at: (0, 0)),
                pl.BlockSpec((rows // 2, 256), lambda g, at: (0, 0)),
            ],
        ),
        out_shape=[side, side] + [jax.ShapeDtypeStruct((rows // 2, 256), jnp.bfloat16)] * 2,
        compiler_params=params(61),
        cost_estimate=cost(1 << 25, 2 << 20),
        name="dequant",
    )(at, exps, mantissas, mantissas, mantissas)


def pick_kernel(count, at, *refs):
    sides, out = refs[: 2 * count], refs[-1]
    row = 0
    for i in range(count):
        rows = sides[2 * i].shape[0]
        out[row : row + rows] = jnp.concatenate([sides[2 * i][...], sides[2 * i + 1][...]], 1)
        row += rows


def lanes_at_z(rows, by_core):
    if by_core:
        return pl.BlockSpec((rows, 128), lambda g, at: (at[AT_CORE], at[AT_Z]))
    return pl.BlockSpec((rows, 128), lambda g, at: (0, at[AT_Z]))


def pick(at, pieces, *after):
    rows = sum(n for n, _, _, _ in pieces)
    specs = [lanes_at_z(n, by_core) for n, by_core, _, _ in pieces for _ in range(2)]
    specs += [pl.BlockSpec(memory_space=pl.ANY)] * len(after)
    return pl.pallas_call(
        functools.partial(pick_kernel, len(pieces)),
        grid_spec=pltpu.PrefetchScalarGridSpec(
            num_scalar_prefetch=1, grid=(1,), in_specs=specs,
            out_specs=pl.BlockSpec((rows, 256), lambda g, at: (0, 0)),
        ),
        out_shape=jax.ShapeDtypeStruct((rows, 256), jnp.bfloat16),
        compiler_params=params(6),
        cost_estimate=cost(0, rows * 1024),
        name="pick",
    )(at, *[side for _, _, low, high in pieces for side in (low, high)], *after)


def gram_kernel(sizes, kept, at, *refs):
    count = len(sizes)
    lows, highs = refs[:count], refs[count : 2 * count]
    low_rights, high_rights = refs[2 * count : 3 * count], refs[3 * count : 4 * count]
    own, near, third, far = refs[4 * count : 4 * count + 4]
    low_other, high_other, low_own, high_own = refs[-5:-1]
    left = refs[-1]
    step = pl.program_id(0)

    @pl.when(step == 0)
    def _():
        mine_first = at[AT_YL] == at[AT_YH]
        use_mine = mine_first if kept else jnp.logical_not(mine_first)
        row, start = 0, 0
        for i, rows in enumerate(sizes):
            mine = jnp.concatenate([lows[i][...], highs[i][...]], 1)
            if 0 < i < count - 2:
                theirs = near[row : row + rows]
                row += rows
            else:
                theirs = (own if i == 0 else third if i == count - 2 else far)[...]
            left[start : start + rows] = jnp.where(use_mine, mine, theirs)
            start += rows

    def terms(rights):
        total, start = None, 0
        for i, rows in enumerate(sizes):
            term = lax.dot_general(
                left[start : start + rows], rights[i][...], TURNED, preferred_element_type=jnp.float32
            )
            total = term if total is None else total + term
            start += rows
        return total

    @pl.when(step == 0)
    def _():
        low_other[...] = terms(low_rights)
        high_other[...] = terms(high_rights)

    @pl.when(step == 1)
    def _():
        low_own[...] = terms(low_rights)
        high_own[...] = terms(high_rights)


def gram(at, pieces, received, kept, *after):
    sizes = tuple(n for n, _, _, _ in pieces)
    specs = [lanes_at_z(n, by_core) for n, by_core, _, _ in pieces] * 2
    for n, by_core, _, _ in pieces:
        specs.append(
            pl.BlockSpec(
                (n, 512),
                lambda g, at, by_core=by_core: (
                    at[AT_CORE] if by_core else 0,
                    (1 - g) * (1 - at[AT_CORE]) + g * at[AT_CORE],
                ),
            )
        )
    specs += specs[-len(pieces) :]
    specs += [pl.BlockSpec(r.shape, lambda g, at: (0, 0)) for r in received]
    specs += [pl.BlockSpec(memory_space=pl.ANY)] * len(after)
    sides = [p[2] for p in pieces], [p[3] for p in pieces]
    return pl.pallas_call(
        functools.partial(gram_kernel, sizes, kept),
        grid_spec=pltpu.PrefetchScalarGridSpec(
            num_scalar_prefetch=1, grid=(2,), in_specs=specs,
            out_specs=[pl.BlockSpec((256, 512), lambda g, at: (0, 0))] * 4,
            scratch_shapes=[pltpu.VMEM((sum(sizes), 256), jnp.bfloat16)],
        ),
        out_shape=[jax.ShapeDtypeStruct((256, 512), jnp.float32)] * 4,
        compiler_params=params(20),
        cost_estimate=cost(2 * sum(sizes) * 256 * 2048, 7 << 20),
        name="gram",
    )(at, *sides[0], *sides[1], *sides[0], *sides[1], *received, *after)


def add_kernel(left, right, out):
    out[...] = left[...] + right[...]


def add(left, right):
    rows, columns = left.shape
    spec = pl.BlockSpec((rows // 2, columns), lambda g: (g, 0))
    return pl.pallas_call(
        add_kernel,
        grid=(2,),
        in_specs=[spec, spec],
        out_specs=spec,
        out_shape=jax.ShapeDtypeStruct(left.shape, left.dtype),
        compiler_params=params(6),
        cost_estimate=cost(1 << 18, 3 << 19),
        name="add",
    )(left, right)


def finish_kernel(factor, low, high, low_core, high_core, low_got, high_got, out):
    for i in range(4):
        lanes = slice(i * 128, i * 128 + 128)
        first = (low[:, lanes] + low_core[:, lanes]) + low_got[:, lanes]
        second = (high[:, lanes] + high_core[:, lanes]) + high_got[:, lanes]
        out[:, i * 256 : i * 256 + 128] = first * factor
        out[:, i * 256 + 128 : i * 256 + 256] = second * factor


def finish(factor, terms):
    rows, columns = terms[0].shape
    return pl.pallas_call(
        functools.partial(finish_kernel, factor),
        grid=(4,),
        in_specs=[pl.BlockSpec((rows // 4, columns), lambda g: (g, 0))] * 6,
        out_specs=pl.BlockSpec((rows // 4, 2 * columns), lambda g: (g, 0)),
        out_shape=jax.ShapeDtypeStruct((rows, 2 * columns), jnp.float32),
        compiler_params=params(8),
        cost_estimate=cost(1 << 20, 4 << 20),
        name="finish",
    )(*terms)


def tie_kernel(*refs):
    del refs


def tie(value, *earlier):
    return pl.pallas_call(
        tie_kernel,
        in_specs=[pl.BlockSpec(memory_space=pl.ANY)] * (1 + len(earlier)),
        out_specs=pl.BlockSpec(memory_space=pl.ANY),
        out_shape=jax.ShapeDtypeStruct(value.shape, value.dtype),
        input_output_aliases={0: 0},
        compiler_params=params(1),
        cost_estimate=cost(0, 0),
        name="tie",
    )(value, *earlier)


def fisher_terms(at, mantissas, exps, pair, placed):
    core = lax.axis_index("core")
    rows = mantissas.shape[0]
    low, high, own, far = dequant(at, exps, mantissas)

    half = rows // 2
    pieces = [(half, True, low, high)]
    for step in range(1, Z // 2 + 1):
        if step == Z // 2:
            low = lax.dynamic_slice_in_dim(low, core * half, half, 0)
            high = lax.dynamic_slice_in_dim(high, core * half, half, 0)
        low = lax.ppermute(low, ("z", "core"), RING)
        high = lax.ppermute(high, ("z", "core"), RING)
        if step == 1:
            far = lax.ppermute(tie(far, low), "z", [(i, (i + Z // 2) % Z) for i in range(Z)])
            low = tie(low, pair)
        if step == 2:
            low = tie(low, placed)
            placed = tie(placed, high)
        pieces.append((low.shape[0], False, low, high))
    near = lax.ppermute(pick(at, pieces[1:3]), "yl", SWAP)
    mine = own_slots(placed)
    third = pick(at, pieces[3:4], mine, far)
    third = lax.ppermute(third, "yl", SWAP)
    received = (own, near, third, far)

    *given_other, low_given, high_given = gram(at, pieces, received, False)
    swapped = [lax.ppermute(g, "core", SWAP) for g in given_other]
    *kept_other, low_kept, high_kept = gram(at, pieces, received, True)
    given = [add(g, s) for g, s in zip((low_given, high_given), swapped)]
    kept = [lax.ppermute(k, "core", SWAP) for k in kept_other]
    return given, [low_kept, high_kept, *kept], mine


def spread(scale):
    blocks = scale.shape[1]
    lane_block = jnp.arange(blocks * 128, dtype=jnp.int32) // 128
    pick = (lane_block[None, :] == jnp.arange(blocks, dtype=jnp.int32)[:, None]).astype(jnp.bfloat16)
    wide = lax.dot_general(scale, pick, (((1,), (0,)), ((), ())), preferred_element_type=jnp.float32)
    return wide.astype(jnp.bfloat16)


def place_kernel(at, pair, got, ids, owners, out):
    docs, rows = owners.shape[1], ids.shape[1]
    summed = jnp.where(at[AT_X] % 2 == 0, pair[0], pair[1]) + got[...]
    owner = jnp.broadcast_to(owners[...], (8, docs))
    digit = jnp.where(lax.broadcasted_iota(jnp.int32, (8, docs), 0) == 0, owner >> 5, owner & 31)
    doc = (lax.broadcasted_iota(jnp.int32, (docs, rows), 0) == ids[...]).astype(jnp.bfloat16)
    digits = lax.dot_general(
        digit.astype(jnp.float32).astype(jnp.bfloat16), doc, (((1,), (0,)), ((), ())),
        preferred_element_type=jnp.float32,
    )
    slots = (digits[0:1] * 32.0 + digits[1:2]).astype(jnp.int32)
    count = out.shape[0]
    own_docs = docs // (YH * Z)
    half = own_docs // 2
    place = lax.broadcasted_iota(jnp.int32, (count, rows), 0)
    place = (place // half) * own_docs + place % half
    member = jnp.concatenate([place == slots, place + half == slots], 1)
    member = jnp.where(member, 1.0, 0.0).astype(jnp.bfloat16)
    zero = jnp.zeros_like(summed)
    rest = jnp.concatenate(
        [jnp.concatenate([summed, zero], 1), jnp.concatenate([zero, summed], 1)], 0
    )
    total = None
    for _ in range(3):
        part = rest.astype(jnp.bfloat16)
        rest = rest - part.astype(jnp.float32)
        term = lax.dot_general(member, part, (((1,), (1,)), ((), ())), preferred_element_type=jnp.float32)
        total = term if total is None else total + term
    out[...] = total


def sum_kernel(parts, out):
    total = parts[0]
    for i in range(1, parts.shape[0]):
        total = total + parts[i]
    out[...] = total


def flipped(bit):
    return [(i, i ^ bit) for i in range(X)]


def whole(shape):
    return pl.BlockSpec(shape, lambda g, at: (0,) * len(shape))


def placed_scores(at, mantissas, scale, queries, doc_ids, owners):
    docs = owners.shape[0]
    x = lax.axis_index("x")
    grads = mantissas * spread(scale)
    scores = lax.dot_general(queries, grads, (((1,), (1,)), ((), ())), preferred_element_type=jnp.float32)
    count, rows = scores.shape
    share, half = count // X, docs // (YH * Z) // 2
    upper = x // 2
    got = lax.ppermute(lax.dynamic_slice_in_dim(scores, (1 - upper) * 2 * share, 2 * share, 0), "x", flipped(2))
    pair = lax.dynamic_slice_in_dim(scores, upper * 2 * share, 2 * share, 0) + got
    got = lax.ppermute(lax.dynamic_slice_in_dim(pair, (1 - x % 2) * share, share, 0), "x", flipped(1))
    shapes = (X // 2, share, rows), (share, rows), (1, rows), (1, docs)
    placed = pl.pallas_call(
        place_kernel,
        grid_spec=pltpu.PrefetchScalarGridSpec(
            num_scalar_prefetch=1, grid=(1,), in_specs=[whole(shape) for shape in shapes],
            out_specs=whole((YH * Z * half, 2 * share)),
        ),
        out_shape=jax.ShapeDtypeStruct((YH * Z * half, 2 * share), jnp.float32),
        compiler_params=params(10),
        cost_estimate=cost(1 << 28, 1 << 20),
        name="place",
    )(at, pair.reshape(shapes[0]), got, doc_ids.reshape(1, rows), owners.reshape(1, docs))
    return pair, placed


def assemble_kernel(at, pair, far_pair, out):
    half, double = pair.shape[1:]
    share = double // 2
    values = []
    for source in range(X):
        near = (source // 2) == at[AT_X] // 2
        first = (source % 2) == at[AT_X] % 2
        own = jnp.where(first, pair[0], pair[1])
        other = jnp.where(first, far_pair[0], far_pair[1])
        values.append(jnp.where(near, own, other))
    out[0:half] = jnp.concatenate([v[:, :share] for v in values], 1)
    out[half:] = jnp.concatenate([v[:, share:] for v in values], 1)


def own_slots(placed):
    double = placed.shape[1]
    half = placed.shape[0] // (YH * Z)
    blocks = lax.all_to_all(placed.reshape(YH * Z, half, double), ("yh", "z"), 0, 0, tiled=True)
    return pl.pallas_call(
        sum_kernel,
        out_shape=jax.ShapeDtypeStruct((half, double), jnp.float32),
        compiler_params=params(4),
        cost_estimate=cost(1 << 16, 1 << 18),
        name="sum",
    )(blocks)


def doc_block(at, mine):
    half, double = mine.shape
    pair = jnp.stack([mine, lax.ppermute(mine, "x", flipped(1))])
    far_pair = lax.ppermute(pair, "x", flipped(2))
    return pl.pallas_call(
        assemble_kernel,
        grid_spec=pltpu.PrefetchScalarGridSpec(
            num_scalar_prefetch=1, grid=(1,), in_specs=[whole(pair.shape)] * 2,
            out_specs=whole((2 * half, X * double // 2)),
        ),
        out_shape=jax.ShapeDtypeStruct((2 * half, X * double // 2), jnp.float32),
        compiler_params=params(2),
        cost_estimate=cost(0, 1 << 17),
        name="assemble",
    )(at, pair, far_pair)


def per_device(mantissas, exponents, queries, doc_ids, owners):
    mantissas = mantissas[:, 0, :]
    exponents = exponents[:, 0, :]
    total_rows = mantissas.shape[0] * YH * Z
    yh, z, x = lax.axis_index("yh"), lax.axis_index("z"), lax.axis_index("x")
    yl, core = lax.axis_index("yl"), lax.axis_index("core")
    other = (1 - yl) * Z
    at = jnp.stack([z, core, yl, other + z, other + lax.rem(z + Z // 2, Z), yh, x]).astype(jnp.int32)
    pair, placed = placed_scores(at, mantissas, powers(exponents), queries[:, 0, :], doc_ids, owners)
    given, kept, mine = fisher_terms(at, mantissas, exponents.T, pair, placed)
    got = [lax.ppermute(g, "yh", SWAP) for g in given]
    return finish(1.0 / total_rows, kept + got)[None], doc_block(at, mine)


def solution(mesh):
    fine = Mesh(mesh.devices.reshape(YH, Z, X, YL, CORE), ("yh", "z", "x", "yl", "core"))
    in_specs = (
        P(ROW_AXES, "x", None),
        P(ROW_AXES, "x", None),
        P(COL_AXES, "x", None),
        P(ROW_AXES),
        P(),
    )
    out_specs = (P("x", ROW_AXES, COL_AXES), P(ROW_AXES, COL_AXES))
    return jax.shard_map(per_device, mesh=fine, in_specs=in_specs, out_specs=out_specs, check_vma=False)
```

```python
import functools

import jax
import jax.numpy as jnp
from jax import lax
from jax.experimental import pallas as pl
from jax.experimental.pallas import tpu as pltpu
from jax.sharding import Mesh, PartitionSpec as P

YH, Z, X, YL, CORE = 2, 8, 4, 2, 2
ROW_AXES = ("yh", "z")
COL_AXES = ("yl", "core")
SWAP = [(0, 1), (1, 0)]
RING = [(2 * i, 2 * ((i + 1) % Z)) for i in range(Z)] + [(2 * i + 1, 2 * ((i - 1) % Z) + 1) for i in range(Z)]
TURNED = (((0,), (0,)), ((), ()))


def powers(exponents):
    return jnp.exp2(exponents.astype(jnp.float32)).astype(jnp.bfloat16)


def params(mebibytes):
    return pltpu.CompilerParams(vmem_limit_bytes=mebibytes << 20)


def cost(flops, moved):
    return pl.CostEstimate(flops=flops, bytes_accessed=moved, transcendentals=0)


AT_Z, AT_CORE, AT_YL, AT_OWN, AT_FAR, AT_YH, AT_X = 0, 1, 2, 3, 4, 5, 6


def wide_scale(turned, first_block, columns):
    blocks = turned.shape[0]
    lane_block = lax.broadcasted_iota(jnp.int32, (blocks, columns), 1) // 128 + first_block
    pick = (lane_block == lax.broadcasted_iota(jnp.int32, (blocks, columns), 0)).astype(jnp.bfloat16)
    return lax.dot_general(turned, pick, TURNED, preferred_element_type=jnp.float32)


def dequant_kernel(at, exps, values, own_values, far_values, low, high, own, far):
    step = pl.program_id(0)
    turned = powers(exps[...])
    grads = values[...].astype(jnp.float32) * wide_scale(turned, at[AT_YL] * 16 + step * 4, 512)
    grads = grads.astype(jnp.bfloat16)
    low[...] = jnp.concatenate([grads[:, 0:128], grads[:, 256:384]], 1)
    high[...] = jnp.concatenate([grads[:, 128:256], grads[:, 384:512]], 1)

    @pl.when(step == 0)
    def _():
        half = far.shape[0]
        for block, source, result in ((AT_OWN, own_values, own), (AT_FAR, far_values, far)):
            scale = wide_scale(turned, at[block] * 2, 256)
            scale = jnp.where(at[AT_CORE] == 0, scale[:half], scale[half:])
            result[...] = (source[...].astype(jnp.float32) * scale).astype(jnp.bfloat16)


def dequant(at, exps, mantissas):
    rows, width = mantissas.shape
    side = jax.ShapeDtypeStruct((rows, width // 4), jnp.bfloat16)
    return pl.pallas_call(
        dequant_kernel,
        grid_spec=pltpu.PrefetchScalarGridSpec(
            num_scalar_prefetch=1,
            grid=(4,),
            in_specs=[
                pl.BlockSpec(exps.shape, lambda g, at: (0, 0)),
                pl.BlockSpec((rows, 512), lambda g, at: (0, at[AT_YL] * 4 + g)),
                pl.BlockSpec((rows // 2, 256), lambda g, at: (at[AT_CORE], at[AT_OWN])),
                pl.BlockSpec((rows // 2, 256), lambda g, at: (at[AT_CORE], at[AT_FAR])),
            ],
            out_specs=[
                pl.BlockSpec((rows, 256), lambda g, at: (0, g)),
                pl.BlockSpec((rows, 256), lambda g, at: (0, g)),
                pl.BlockSpec((rows // 2, 256), lambda g, at: (0, 0)),
                pl.BlockSpec((rows // 2, 256), lambda g, at: (0, 0)),
            ],
        ),
        out_shape=[side, side] + [jax.ShapeDtypeStruct((rows // 2, 256), jnp.bfloat16)] * 2,
        compiler_params=params(61),
        cost_estimate=cost(1 << 25, 2 << 20),
        name="dequant",
    )(at, exps, mantissas, mantissas, mantissas)


def pick_kernel(count, at, *refs):
    sides, out = refs[: 2 * count], refs[-1]
    row = 0
    for i in range(count):
        rows = sides[2 * i].shape[0]
        out[row : row + rows] = jnp.concatenate([sides[2 * i][...], sides[2 * i + 1][...]], 1)
        row += rows


def lanes_at_z(rows, by_core):
    if by_core:
        return pl.BlockSpec((rows, 128), lambda g, at: (at[AT_CORE], at[AT_Z]))
    return pl.BlockSpec((rows, 128), lambda g, at: (0, at[AT_Z]))


def pick(at, pieces, *after):
    rows = sum(n for n, _, _, _ in pieces)
    specs = [lanes_at_z(n, by_core) for n, by_core, _, _ in pieces for _ in range(2)]
    specs += [pl.BlockSpec(memory_space=pl.ANY)] * len(after)
    return pl.pallas_call(
        functools.partial(pick_kernel, len(pieces)),
        grid_spec=pltpu.PrefetchScalarGridSpec(
            num_scalar_prefetch=1, grid=(1,), in_specs=specs,
            out_specs=pl.BlockSpec((rows, 256), lambda g, at: (0, 0)),
        ),
        out_shape=jax.ShapeDtypeStruct((rows, 256), jnp.bfloat16),
        compiler_params=params(6),
        cost_estimate=cost(0, rows * 1024),
        name="pick",
    )(at, *[side for _, _, low, high in pieces for side in (low, high)], *after)


def gram_kernel(sizes, kept, at, *refs):
    count = len(sizes)
    lows, highs = refs[:count], refs[count : 2 * count]
    low_rights, high_rights = refs[2 * count : 3 * count], refs[3 * count : 4 * count]
    own, near, third, far = refs[4 * count : 4 * count + 4]
    low_other, high_other, low_own, high_own = refs[-5:-1]
    left = refs[-1]
    step = pl.program_id(0)

    @pl.when(step == 0)
    def _():
        mine_first = at[AT_YL] == at[AT_YH]
        use_mine = mine_first if kept else jnp.logical_not(mine_first)
        row, start = 0, 0
        for i, rows in enumerate(sizes):
            mine = jnp.concatenate([lows[i][...], highs[i][...]], 1)
            if 0 < i < count - 2:
                theirs = near[row : row + rows]
                row += rows
            else:
                theirs = (own if i == 0 else third if i == count - 2 else far)[...]
            left[start : start + rows] = jnp.where(use_mine, mine, theirs)
            start += rows

    def terms(rights):
        total, start = None, 0
        for i, rows in enumerate(sizes):
            term = lax.dot_general(
                left[start : start + rows], rights[i][...], TURNED, preferred_element_type=jnp.float32
            )
            total = term if total is None else total + term
            start += rows
        return total

    @pl.when(step == 0)
    def _():
        low_other[...] = terms(low_rights)
        high_other[...] = terms(high_rights)

    @pl.when(step == 1)
    def _():
        low_own[...] = terms(low_rights)
        high_own[...] = terms(high_rights)


def gram(at, pieces, received, kept, *after):
    sizes = tuple(n for n, _, _, _ in pieces)
    specs = [lanes_at_z(n, by_core) for n, by_core, _, _ in pieces] * 2
    for n, by_core, _, _ in pieces:
        specs.append(
            pl.BlockSpec(
                (n, 512),
                lambda g, at, by_core=by_core: (
                    at[AT_CORE] if by_core else 0,
                    (1 - g) * (1 - at[AT_CORE]) + g * at[AT_CORE],
                ),
            )
        )
    specs += specs[-len(pieces) :]
    specs += [pl.BlockSpec(r.shape, lambda g, at: (0, 0)) for r in received]
    specs += [pl.BlockSpec(memory_space=pl.ANY)] * len(after)
    sides = [p[2] for p in pieces], [p[3] for p in pieces]
    return pl.pallas_call(
        functools.partial(gram_kernel, sizes, kept),
        grid_spec=pltpu.PrefetchScalarGridSpec(
            num_scalar_prefetch=1, grid=(2,), in_specs=specs,
            out_specs=[pl.BlockSpec((256, 512), lambda g, at: (0, 0))] * 4,
            scratch_shapes=[pltpu.VMEM((sum(sizes), 256), jnp.bfloat16)],
        ),
        out_shape=[jax.ShapeDtypeStruct((256, 512), jnp.float32)] * 4,
        compiler_params=params(20),
        cost_estimate=cost(2 * sum(sizes) * 256 * 2048, 7 << 20),
        name="gram",
    )(at, *sides[0], *sides[1], *sides[0], *sides[1], *received, *after)


def add_kernel(left, right, out):
    out[...] = left[...] + right[...]


def add(left, right):
    rows, columns = left.shape
    spec = pl.BlockSpec((rows // 2, columns), lambda g: (g, 0))
    return pl.pallas_call(
        add_kernel,
        grid=(2,),
        in_specs=[spec, spec],
        out_specs=spec,
        out_shape=jax.ShapeDtypeStruct(left.shape, left.dtype),
        compiler_params=params(6),
        cost_estimate=cost(1 << 18, 3 << 19),
        name="add",
    )(left, right)


def finish_kernel(factor, low, high, low_core, high_core, low_got, high_got, out):
    for i in range(4):
        lanes = slice(i * 128, i * 128 + 128)
        first = (low[:, lanes] + low_core[:, lanes]) + low_got[:, lanes]
        second = (high[:, lanes] + high_core[:, lanes]) + high_got[:, lanes]
        out[:, i * 256 : i * 256 + 128] = first * factor
        out[:, i * 256 + 128 : i * 256 + 256] = second * factor


def finish(factor, terms):
    rows, columns = terms[0].shape
    return pl.pallas_call(
        functools.partial(finish_kernel, factor),
        grid=(4,),
        in_specs=[pl.BlockSpec((rows // 4, columns), lambda g: (g, 0))] * 6,
        out_specs=pl.BlockSpec((rows // 4, 2 * columns), lambda g: (g, 0)),
        out_shape=jax.ShapeDtypeStruct((rows, 2 * columns), jnp.float32),
        compiler_params=params(8),
        cost_estimate=cost(1 << 20, 4 << 20),
        name="finish",
    )(*terms)


def tie_kernel(*refs):
    del refs


def tie(value, *earlier):
    return pl.pallas_call(
        tie_kernel,
        in_specs=[pl.BlockSpec(memory_space=pl.ANY)] * (1 + len(earlier)),
        out_specs=pl.BlockSpec(memory_space=pl.ANY),
        out_shape=jax.ShapeDtypeStruct(value.shape, value.dtype),
        input_output_aliases={0: 0},
        compiler_params=params(1),
        cost_estimate=cost(0, 0),
        name="tie",
    )(value, *earlier)


def fisher_terms(at, mantissas, exps, pair, placed):
    core = lax.axis_index("core")
    rows = mantissas.shape[0]
    low, high, own, far = dequant(at, exps, mantissas)

    half = rows // 2
    pieces = [(half, True, low, high)]
    for step in range(1, Z // 2 + 1):
        if step == Z // 2:
            low = lax.dynamic_slice_in_dim(low, core * half, half, 0)
            high = lax.dynamic_slice_in_dim(high, core * half, half, 0)
        low = lax.ppermute(low, ("z", "core"), RING)
        high = lax.ppermute(high, ("z", "core"), RING)
        if step == 1:
            far = lax.ppermute(tie(far, low), "z", [(i, (i + Z // 2) % Z) for i in range(Z)])
            low = tie(low, pair)
        if step == 2:
            low = tie(low, placed, far)
            placed = tie(placed, high)
        pieces.append((low.shape[0], False, low, high))
    near = lax.ppermute(pick(at, pieces[1:3]), "yl", SWAP)
    mine = own_slots(placed)
    third = pick(at, pieces[3:4])
    third = lax.ppermute(third, "yl", SWAP)
    received = (own, near, third, far)

    *given_other, low_given, high_given = gram(at, pieces, received, False, mine)
    swapped = [lax.ppermute(g, "core", SWAP) for g in given_other]
    *kept_other, low_kept, high_kept = gram(at, pieces, received, True)
    given = [add(g, s) for g, s in zip((low_given, high_given), swapped)]
    kept = [lax.ppermute(k, "core", SWAP) for k in kept_other]
    return given, [low_kept, high_kept, *kept], mine


def spread(scale):
    blocks = scale.shape[1]
    lane_block = jnp.arange(blocks * 128, dtype=jnp.int32) // 128
    pick = (lane_block[None, :] == jnp.arange(blocks, dtype=jnp.int32)[:, None]).astype(jnp.bfloat16)
    wide = lax.dot_general(scale, pick, (((1,), (0,)), ((), ())), preferred_element_type=jnp.float32)
    return wide.astype(jnp.bfloat16)


def place_kernel(at, pair, got, ids, owners, out):
    docs, rows = owners.shape[1], ids.shape[1]
    summed = jnp.where(at[AT_X] % 2 == 0, pair[0], pair[1]) + got[...]
    owner = jnp.broadcast_to(owners[...], (8, docs))
    digit = jnp.where(lax.broadcasted_iota(jnp.int32, (8, docs), 0) == 0, owner >> 5, owner & 31)
    doc = (lax.broadcasted_iota(jnp.int32, (docs, rows), 0) == ids[...]).astype(jnp.bfloat16)
    digits = lax.dot_general(
        digit.astype(jnp.float32).astype(jnp.bfloat16), doc, (((1,), (0,)), ((), ())),
        preferred_element_type=jnp.float32,
    )
    slots = (digits[0:1] * 32.0 + digits[1:2]).astype(jnp.int32)
    count = out.shape[0]
    own_docs = docs // (YH * Z)
    half = own_docs // 2
    place = lax.broadcasted_iota(jnp.int32, (count, rows), 0)
    place = (place // half) * own_docs + place % half
    member = jnp.concatenate([place == slots, place + half == slots], 1)
    member = jnp.where(member, 1.0, 0.0).astype(jnp.bfloat16)
    zero = jnp.zeros_like(summed)
    rest = jnp.concatenate(
        [jnp.concatenate([summed, zero], 1), jnp.concatenate([zero, summed], 1)], 0
    )
    total = None
    for _ in range(3):
        part = rest.astype(jnp.bfloat16)
        rest = rest - part.astype(jnp.float32)
        term = lax.dot_general(member, part, (((1,), (1,)), ((), ())), preferred_element_type=jnp.float32)
        total = term if total is None else total + term
    out[...] = total


def sum_kernel(parts, out):
    total = parts[0]
    for i in range(1, parts.shape[0]):
        total = total + parts[i]
    out[...] = total


def flipped(bit):
    return [(i, i ^ bit) for i in range(X)]


def whole(shape):
    return pl.BlockSpec(shape, lambda g, at: (0,) * len(shape))


def placed_scores(at, mantissas, scale, queries, doc_ids, owners):
    docs = owners.shape[0]
    x = lax.axis_index("x")
    grads = mantissas * spread(scale)
    scores = lax.dot_general(queries, grads, (((1,), (1,)), ((), ())), preferred_element_type=jnp.float32)
    count, rows = scores.shape
    share, half = count // X, docs // (YH * Z) // 2
    upper = x // 2
    got = lax.ppermute(lax.dynamic_slice_in_dim(scores, (1 - upper) * 2 * share, 2 * share, 0), "x", flipped(2))
    pair = lax.dynamic_slice_in_dim(scores, upper * 2 * share, 2 * share, 0) + got
    got = lax.ppermute(lax.dynamic_slice_in_dim(pair, (1 - x % 2) * share, share, 0), "x", flipped(1))
    shapes = (X // 2, share, rows), (share, rows), (1, rows), (1, docs)
    placed = pl.pallas_call(
        place_kernel,
        grid_spec=pltpu.PrefetchScalarGridSpec(
            num_scalar_prefetch=1, grid=(1,), in_specs=[whole(shape) for shape in shapes],
            out_specs=whole((YH * Z * half, 2 * share)),
        ),
        out_shape=jax.ShapeDtypeStruct((YH * Z * half, 2 * share), jnp.float32),
        compiler_params=params(10),
        cost_estimate=cost(1 << 28, 1 << 20),
        name="place",
    )(at, pair.reshape(shapes[0]), got, doc_ids.reshape(1, rows), owners.reshape(1, docs))
    return pair, placed


def assemble_kernel(at, pair, far_pair, out):
    half, double = pair.shape[1:]
    share = double // 2
    values = []
    for source in range(X):
        near = (source // 2) == at[AT_X] // 2
        first = (source % 2) == at[AT_X] % 2
        own = jnp.where(first, pair[0], pair[1])
        other = jnp.where(first, far_pair[0], far_pair[1])
        values.append(jnp.where(near, own, other))
    out[0:half] = jnp.concatenate([v[:, :share] for v in values], 1)
    out[half:] = jnp.concatenate([v[:, share:] for v in values], 1)


def own_slots(placed):
    double = placed.shape[1]
    half = placed.shape[0] // (YH * Z)
    blocks = lax.all_to_all(placed.reshape(YH * Z, half, double), ("yh", "z"), 0, 0, tiled=True)
    return pl.pallas_call(
        sum_kernel,
        out_shape=jax.ShapeDtypeStruct((half, double), jnp.float32),
        compiler_params=params(4),
        cost_estimate=cost(1 << 16, 1 << 18),
        name="sum",
    )(blocks)


def doc_block(at, mine):
    half, double = mine.shape
    pair = jnp.stack([mine, lax.ppermute(mine, "x", flipped(1))])
    far_pair = lax.ppermute(pair, "x", flipped(2))
    return pl.pallas_call(
        assemble_kernel,
        grid_spec=pltpu.PrefetchScalarGridSpec(
            num_scalar_prefetch=1, grid=(1,), in_specs=[whole(pair.shape)] * 2,
            out_specs=whole((2 * half, X * double // 2)),
        ),
        out_shape=jax.ShapeDtypeStruct((2 * half, X * double // 2), jnp.float32),
        compiler_params=params(2),
        cost_estimate=cost(0, 1 << 17),
        name="assemble",
    )(at, pair, far_pair)


def per_device(mantissas, exponents, queries, doc_ids, owners):
    mantissas = mantissas[:, 0, :]
    exponents = exponents[:, 0, :]
    total_rows = mantissas.shape[0] * YH * Z
    yh, z, x = lax.axis_index("yh"), lax.axis_index("z"), lax.axis_index("x")
    yl, core = lax.axis_index("yl"), lax.axis_index("core")
    other = (1 - yl) * Z
    at = jnp.stack([z, core, yl, other + z, other + lax.rem(z + Z // 2, Z), yh, x]).astype(jnp.int32)
    pair, placed = placed_scores(at, mantissas, powers(exponents), queries[:, 0, :], doc_ids, owners)
    given, kept, mine = fisher_terms(at, mantissas, exponents.T, pair, placed)
    got = [lax.ppermute(g, "yh", SWAP) for g in given]
    return finish(1.0 / total_rows, kept + got)[None], doc_block(at, mine)


def solution(mesh):
    fine = Mesh(mesh.devices.reshape(YH, Z, X, YL, CORE), ("yh", "z", "x", "yl", "core"))
    in_specs = (
        P(ROW_AXES, "x", None),
        P(ROW_AXES, "x", None),
        P(COL_AXES, "x", None),
        P(ROW_AXES),
        P(),
    )
    out_specs = (P("x", ROW_AXES, COL_AXES), P(ROW_AXES, COL_AXES))
    return jax.shard_map(per_device, mesh=fine, in_specs=in_specs, out_specs=out_specs, check_vma=False)
```

```python
import functools

import jax
import jax.numpy as jnp
from jax import lax
from jax.experimental import pallas as pl
from jax.experimental.pallas import tpu as pltpu
from jax.sharding import Mesh, PartitionSpec as P

YH, Z, X, YL, CORE = 2, 8, 4, 2, 2
ROW_AXES = ("yh", "z")
COL_AXES = ("yl", "core")
SWAP = [(0, 1), (1, 0)]
RING = [(2 * i, 2 * ((i + 1) % Z)) for i in range(Z)] + [(2 * i + 1, 2 * ((i - 1) % Z) + 1) for i in range(Z)]
TURNED = (((0,), (0,)), ((), ()))


def powers(exponents):
    return jnp.exp2(exponents.astype(jnp.float32)).astype(jnp.bfloat16)


def params(mebibytes):
    return pltpu.CompilerParams(vmem_limit_bytes=mebibytes << 20)


def cost(flops, moved):
    return pl.CostEstimate(flops=flops, bytes_accessed=moved, transcendentals=0)


AT_Z, AT_CORE, AT_YL, AT_OWN, AT_FAR, AT_YH, AT_X = 0, 1, 2, 3, 4, 5, 6


def wide_scale(turned, first_block, columns):
    blocks = turned.shape[0]
    lane_block = lax.broadcasted_iota(jnp.int32, (blocks, columns), 1) // 128 + first_block
    pick = (lane_block == lax.broadcasted_iota(jnp.int32, (blocks, columns), 0)).astype(jnp.bfloat16)
    return lax.dot_general(turned, pick, TURNED, preferred_element_type=jnp.float32)


FAR = 32


def dequant_kernel(at, exps, values, own_values, far_values, low, high, own, far_scale):
    step = pl.program_id(0)
    rows, half = values.shape[0], own.shape[0]
    turned = powers(exps[...])

    @pl.when(step == 0)
    def _():
        far_scale[...] = wide_scale(turned, at[AT_FAR] * 2, 256)
        scale = wide_scale(turned, at[AT_OWN] * 2, 256)
        scale = jnp.where(at[AT_CORE] == 0, scale[:half], scale[half:])
        own[...] = (own_values[...].astype(jnp.float32) * scale).astype(jnp.bfloat16)

    grads = values[...].astype(jnp.float32) * wide_scale(turned, at[AT_YL] * 16 + step * 4, 512)
    grads = grads.astype(jnp.bfloat16)
    low[0:rows] = jnp.concatenate([grads[:, 0:128], grads[:, 256:384]], 1)
    high[...] = jnp.concatenate([grads[:, 128:256], grads[:, 384:512]], 1)
    scale = far_scale[pl.ds(pl.multiple_of(at[AT_CORE] * half + step * FAR, FAR), FAR)]
    low[rows : rows + FAR] = (far_values[...].astype(jnp.float32) * scale).astype(jnp.bfloat16)


def dequant(at, exps, mantissas):
    rows, width = mantissas.shape
    half = rows // 2
    return pl.pallas_call(
        dequant_kernel,
        grid_spec=pltpu.PrefetchScalarGridSpec(
            num_scalar_prefetch=1,
            grid=(4,),
            in_specs=[
                pl.BlockSpec(exps.shape, lambda g, at: (0, 0)),
                pl.BlockSpec((rows, 512), lambda g, at: (0, at[AT_YL] * 4 + g)),
                pl.BlockSpec((half, 256), lambda g, at: (at[AT_CORE], at[AT_OWN])),
                pl.BlockSpec((FAR, 256), lambda g, at: (at[AT_CORE] * 4 + g, at[AT_FAR])),
            ],
            out_specs=[
                pl.BlockSpec((rows + FAR, 256), lambda g, at: (0, g)),
                pl.BlockSpec((rows, 256), lambda g, at: (0, g)),
                pl.BlockSpec((half, 256), lambda g, at: (0, 0)),
            ],
            scratch_shapes=[pltpu.VMEM((rows, 256), jnp.float32)],
        ),
        out_shape=[
            jax.ShapeDtypeStruct((rows + FAR, width // 4), jnp.bfloat16),
            jax.ShapeDtypeStruct((rows, width // 4), jnp.bfloat16),
            jax.ShapeDtypeStruct((half, 256), jnp.bfloat16),
        ],
        compiler_params=params(62),
        cost_estimate=cost(1 << 25, 2 << 20),
        name="dequant",
    )(at, exps, mantissas, mantissas, mantissas)


def halve_kernel(at, low, far, high, low_lanes, high_lanes, after, low_half, high_half, third):
    del after
    half = low.shape[0]
    low_half[0:half] = low[...]
    low_half[half : half + FAR] = far[...]
    high_half[...] = high[...]
    third[...] = jnp.concatenate([low_lanes[...], high_lanes[...]], 1)


def halve(at, low, high, after):
    rows, width = high.shape
    half = rows // 2
    return pl.pallas_call(
        halve_kernel,
        grid_spec=pltpu.PrefetchScalarGridSpec(
            num_scalar_prefetch=1,
            grid=(1,),
            in_specs=[
                pl.BlockSpec((half, width), lambda g, at: (at[AT_CORE], 0)),
                pl.BlockSpec((FAR, width), lambda g, at: (rows // FAR, 0)),
                pl.BlockSpec((half, width), lambda g, at: (at[AT_CORE], 0)),
                lanes_at_z(rows, False),
                lanes_at_z(rows, False),
                pl.BlockSpec(memory_space=pl.ANY),
            ],
            out_specs=[
                pl.BlockSpec((half + FAR, width), lambda g, at: (0, 0)),
                pl.BlockSpec((half, width), lambda g, at: (0, 0)),
                pl.BlockSpec((rows, 256), lambda g, at: (0, 0)),
            ],
        ),
        out_shape=[
            jax.ShapeDtypeStruct((half + FAR, width), jnp.bfloat16),
            jax.ShapeDtypeStruct((half, width), jnp.bfloat16),
            jax.ShapeDtypeStruct((rows, 256), jnp.bfloat16),
        ],
        compiler_params=params(8),
        cost_estimate=cost(0, 2 << 20),
        name="halve",
    )(at, low, low, high, low, high, after)


def pick_kernel(count, at, *refs):
    sides, out = refs[: 2 * count], refs[-1]
    row = 0
    for i in range(count):
        rows = sides[2 * i].shape[0]
        out[row : row + rows] = jnp.concatenate([sides[2 * i][...], sides[2 * i + 1][...]], 1)
        row += rows


def lanes_at_z(rows, by_core):
    if by_core:
        return pl.BlockSpec((rows, 128), lambda g, at: (at[AT_CORE], at[AT_Z]))
    return pl.BlockSpec((rows, 128), lambda g, at: (0, at[AT_Z]))


def pick(at, pieces, *after):
    rows = sum(n for n, _, _, _ in pieces)
    specs = [lanes_at_z(n, by_core) for n, by_core, _, _ in pieces for _ in range(2)]
    specs += [pl.BlockSpec(memory_space=pl.ANY)] * len(after)
    return pl.pallas_call(
        functools.partial(pick_kernel, len(pieces)),
        grid_spec=pltpu.PrefetchScalarGridSpec(
            num_scalar_prefetch=1, grid=(1,), in_specs=specs,
            out_specs=pl.BlockSpec((rows, 256), lambda g, at: (0, 0)),
        ),
        out_shape=jax.ShapeDtypeStruct((rows, 256), jnp.bfloat16),
        compiler_params=params(6),
        cost_estimate=cost(0, rows * 1024),
        name="pick",
    )(at, *[side for _, _, low, high in pieces for side in (low, high)], *after)


def gram_kernel(sizes, kept, at, *refs):
    count = len(sizes)
    lows, highs = refs[:count], refs[count : 2 * count]
    low_rights, high_rights = refs[2 * count : 3 * count], refs[3 * count : 4 * count]
    own, near, third, far = refs[4 * count : 4 * count + 4]
    low_other, high_other, low_own, high_own = refs[-5:-1]
    left = refs[-1]
    step = pl.program_id(0)

    @pl.when(step == 0)
    def _():
        mine_first = at[AT_YL] == at[AT_YH]
        use_mine = mine_first if kept else jnp.logical_not(mine_first)
        row, start = 0, 0
        for i, rows in enumerate(sizes):
            mine = jnp.concatenate([lows[i][...], highs[i][...]], 1)
            if 0 < i < count - 2:
                theirs = near[row : row + rows]
                row += rows
            else:
                theirs = (own if i == 0 else third)[...] if i < count - 1 else jnp.concatenate(
                    [far[:, lane : lane + 256] for lane in range(0, 1024, 256)], 0
                )
            left[start : start + rows] = jnp.where(use_mine, mine, theirs)
            start += rows

    def terms(rights):
        total, start = None, 0
        for i, rows in enumerate(sizes):
            term = lax.dot_general(
                left[start : start + rows], rights[i][...], TURNED, preferred_element_type=jnp.float32
            )
            total = term if total is None else total + term
            start += rows
        return total

    @pl.when(step == 0)
    def _():
        low_other[...] = terms(low_rights)
        high_other[...] = terms(high_rights)

    @pl.when(step == 1)
    def _():
        low_own[...] = terms(low_rights)
        high_own[...] = terms(high_rights)


def gram(at, pieces, received, kept, *after):
    sizes = tuple(n for n, _, _, _ in pieces)
    specs = [lanes_at_z(n, by_core) for n, by_core, _, _ in pieces] * 2
    for n, by_core, _, _ in pieces:
        specs.append(
            pl.BlockSpec(
                (n, 512),
                lambda g, at, by_core=by_core: (
                    at[AT_CORE] if by_core else 0,
                    (1 - g) * (1 - at[AT_CORE]) + g * at[AT_CORE],
                ),
            )
        )
    specs += specs[-len(pieces) :]
    specs += [pl.BlockSpec(r.shape, lambda g, at: (0, 0)) for r in received]
    last = pieces[-1][2]
    specs.append(pl.BlockSpec((FAR, last.shape[1]), lambda g, at: (last.shape[0] // FAR - 1, 0)))
    specs += [pl.BlockSpec(memory_space=pl.ANY)] * len(after)
    sides = [p[2] for p in pieces], [p[3] for p in pieces]
    return pl.pallas_call(
        functools.partial(gram_kernel, sizes, kept),
        grid_spec=pltpu.PrefetchScalarGridSpec(
            num_scalar_prefetch=1, grid=(2,), in_specs=specs,
            out_specs=[pl.BlockSpec((256, 512), lambda g, at: (0, 0))] * 4,
            scratch_shapes=[pltpu.VMEM((sum(sizes), 256), jnp.bfloat16)],
        ),
        out_shape=[jax.ShapeDtypeStruct((256, 512), jnp.float32)] * 4,
        compiler_params=params(20),
        cost_estimate=cost(2 * sum(sizes) * 256 * 2048, 7 << 20),
        name="gram",
    )(at, *sides[0], *sides[1], *sides[0], *sides[1], *received, last, *after)


def add_kernel(left, right, out):
    out[...] = left[...] + right[...]


def add(left, right):
    rows, columns = left.shape
    spec = pl.BlockSpec((rows // 2, columns), lambda g: (g, 0))
    return pl.pallas_call(
        add_kernel,
        grid=(2,),
        in_specs=[spec, spec],
        out_specs=spec,
        out_shape=jax.ShapeDtypeStruct(left.shape, left.dtype),
        compiler_params=params(6),
        cost_estimate=cost(1 << 18, 3 << 19),
        name="add",
    )(left, right)


def finish_kernel(factor, low, high, low_core, high_core, low_got, high_got, out):
    for i in range(4):
        lanes = slice(i * 128, i * 128 + 128)
        first = (low[:, lanes] + low_core[:, lanes]) + low_got[:, lanes]
        second = (high[:, lanes] + high_core[:, lanes]) + high_got[:, lanes]
        out[:, i * 256 : i * 256 + 128] = first * factor
        out[:, i * 256 + 128 : i * 256 + 256] = second * factor


def finish(factor, terms):
    rows, columns = terms[0].shape
    return pl.pallas_call(
        functools.partial(finish_kernel, factor),
        grid=(4,),
        in_specs=[pl.BlockSpec((rows // 4, columns), lambda g: (g, 0))] * 6,
        out_specs=pl.BlockSpec((rows // 4, 2 * columns), lambda g: (g, 0)),
        out_shape=jax.ShapeDtypeStruct((rows, 2 * columns), jnp.float32),
        compiler_params=params(8),
        cost_estimate=cost(1 << 20, 4 << 20),
        name="finish",
    )(*terms)


def tie_kernel(*refs):
    del refs


def tie(value, *earlier):
    return pl.pallas_call(
        tie_kernel,
        in_specs=[pl.BlockSpec(memory_space=pl.ANY)] * (1 + len(earlier)),
        out_specs=pl.BlockSpec(memory_space=pl.ANY),
        out_shape=jax.ShapeDtypeStruct(value.shape, value.dtype),
        input_output_aliases={0: 0},
        compiler_params=params(1),
        cost_estimate=cost(0, 0),
        name="tie",
    )(value, *earlier)


def fisher_terms(at, mantissas, exps, pair, placed):
    rows = mantissas.shape[0]
    low, high, own = dequant(at, exps, mantissas)

    half = rows // 2
    pieces = [(half, True, low, high)]
    for step in range(1, Z // 2 + 1):
        if step == Z // 2:
            low, high, third = halve(at, low, high, near)
        low = lax.ppermute(low, ("z", "core"), RING)
        high = lax.ppermute(high, ("z", "core"), RING)
        if step == 1:
            low = tie(low, pair)
        if step == 2:
            low = tie(low, placed)
        pieces.append((rows if step < Z // 2 else half, False, low, high))
        if step == 2:
            near = pick(at, pieces[1:3])
            placed = tie(placed, near)
            near = lax.ppermute(near, "yl", SWAP)
    mine = own_slots(placed)
    received = (own, near, lax.ppermute(third, "yl", SWAP))

    *given_other, low_given, high_given = gram(at, pieces, received, False, mine)
    swapped = [lax.ppermute(g, "core", SWAP) for g in given_other]
    *kept_other, low_kept, high_kept = gram(at, pieces, received, True)
    given = [add(g, s) for g, s in zip((low_given, high_given), swapped)]
    kept = [lax.ppermute(k, "core", SWAP) for k in kept_other]
    return given, [low_kept, high_kept, *kept], mine


def spread(scale):
    blocks = scale.shape[1]
    lane_block = jnp.arange(blocks * 128, dtype=jnp.int32) // 128
    pick = (lane_block[None, :] == jnp.arange(blocks, dtype=jnp.int32)[:, None]).astype(jnp.bfloat16)
    wide = lax.dot_general(scale, pick, (((1,), (0,)), ((), ())), preferred_element_type=jnp.float32)
    return wide.astype(jnp.bfloat16)


def place_kernel(at, pair, got, ids, owners, out):
    docs, rows = owners.shape[1], ids.shape[1]
    summed = jnp.where(at[AT_X] % 2 == 0, pair[0], pair[1]) + got[...]
    owner = jnp.broadcast_to(owners[...], (8, docs))
    digit = jnp.where(lax.broadcasted_iota(jnp.int32, (8, docs), 0) == 0, owner >> 5, owner & 31)
    doc = (lax.broadcasted_iota(jnp.int32, (docs, rows), 0) == ids[...]).astype(jnp.bfloat16)
    digits = lax.dot_general(
        digit.astype(jnp.float32).astype(jnp.bfloat16), doc, (((1,), (0,)), ((), ())),
        preferred_element_type=jnp.float32,
    )
    slots = (digits[0:1] * 32.0 + digits[1:2]).astype(jnp.int32)
    count = out.shape[0]
    own_docs = docs // (YH * Z)
    half = own_docs // 2
    place = lax.broadcasted_iota(jnp.int32, (count, rows), 0)
    place = (place // half) * own_docs + place % half
    member = jnp.concatenate([place == slots, place + half == slots], 1)
    member = jnp.where(member, 1.0, 0.0).astype(jnp.bfloat16)
    zero = jnp.zeros_like(summed)
    rest = jnp.concatenate(
        [jnp.concatenate([summed, zero], 1), jnp.concatenate([zero, summed], 1)], 0
    )
    total = None
    for _ in range(3):
        part = rest.astype(jnp.bfloat16)
        rest = rest - part.astype(jnp.float32)
        term = lax.dot_general(member, part, (((1,), (1,)), ((), ())), preferred_element_type=jnp.float32)
        total = term if total is None else total + term
    out[...] = total


def sum_kernel(parts, out):
    total = parts[0]
    for i in range(1, parts.shape[0]):
        total = total + parts[i]
    out[...] = total


def flipped(bit):
    return [(i, i ^ bit) for i in range(X)]


def whole(shape):
    return pl.BlockSpec(shape, lambda g, at: (0,) * len(shape))


def placed_scores(at, mantissas, scale, queries, doc_ids, owners):
    docs = owners.shape[0]
    x = lax.axis_index("x")
    grads = mantissas * spread(scale)
    scores = lax.dot_general(queries, grads, (((1,), (1,)), ((), ())), preferred_element_type=jnp.float32)
    count, rows = scores.shape
    share, half = count // X, docs // (YH * Z) // 2
    upper = x // 2
    got = lax.ppermute(lax.dynamic_slice_in_dim(scores, (1 - upper) * 2 * share, 2 * share, 0), "x", flipped(2))
    pair = lax.dynamic_slice_in_dim(scores, upper * 2 * share, 2 * share, 0) + got
    got = lax.ppermute(lax.dynamic_slice_in_dim(pair, (1 - x % 2) * share, share, 0), "x", flipped(1))
    shapes = (X // 2, share, rows), (share, rows), (1, rows), (1, docs)
    placed = pl.pallas_call(
        place_kernel,
        grid_spec=pltpu.PrefetchScalarGridSpec(
            num_scalar_prefetch=1, grid=(1,), in_specs=[whole(shape) for shape in shapes],
            out_specs=whole((YH * Z * half, 2 * share)),
        ),
        out_shape=jax.ShapeDtypeStruct((YH * Z * half, 2 * share), jnp.float32),
        compiler_params=params(10),
        cost_estimate=cost(1 << 28, 1 << 20),
        name="place",
    )(at, pair.reshape(shapes[0]), got, doc_ids.reshape(1, rows), owners.reshape(1, docs))
    return pair, placed


def assemble_kernel(at, pair, far_pair, out):
    half, double = pair.shape[1:]
    share = double // 2
    values = []
    for source in range(X):
        near = (source // 2) == at[AT_X] // 2
        first = (source % 2) == at[AT_X] % 2
        own = jnp.where(first, pair[0], pair[1])
        other = jnp.where(first, far_pair[0], far_pair[1])
        values.append(jnp.where(near, own, other))
    out[0:half] = jnp.concatenate([v[:, :share] for v in values], 1)
    out[half:] = jnp.concatenate([v[:, share:] for v in values], 1)


def own_slots(placed):
    double = placed.shape[1]
    half = placed.shape[0] // (YH * Z)
    blocks = lax.all_to_all(placed.reshape(YH * Z, half, double), ("yh", "z"), 0, 0, tiled=True)
    return pl.pallas_call(
        sum_kernel,
        out_shape=jax.ShapeDtypeStruct((half, double), jnp.float32),
        compiler_params=params(4),
        cost_estimate=cost(1 << 16, 1 << 18),
        name="sum",
    )(blocks)


def doc_block(at, mine):
    half, double = mine.shape
    pair = jnp.stack([mine, lax.ppermute(mine, "x", flipped(1))])
    far_pair = lax.ppermute(pair, "x", flipped(2))
    return pl.pallas_call(
        assemble_kernel,
        grid_spec=pltpu.PrefetchScalarGridSpec(
            num_scalar_prefetch=1, grid=(1,), in_specs=[whole(pair.shape)] * 2,
            out_specs=whole((2 * half, X * double // 2)),
        ),
        out_shape=jax.ShapeDtypeStruct((2 * half, X * double // 2), jnp.float32),
        compiler_params=params(2),
        cost_estimate=cost(0, 1 << 17),
        name="assemble",
    )(at, pair, far_pair)


def per_device(mantissas, exponents, queries, doc_ids, owners):
    mantissas = mantissas[:, 0, :]
    exponents = exponents[:, 0, :]
    total_rows = mantissas.shape[0] * YH * Z
    yh, z, x = lax.axis_index("yh"), lax.axis_index("z"), lax.axis_index("x")
    yl, core = lax.axis_index("yl"), lax.axis_index("core")
    other = (1 - yl) * Z
    at = jnp.stack([z, core, yl, other + z, other + lax.rem(z + Z // 2, Z), yh, x]).astype(jnp.int32)
    pair, placed = placed_scores(at, mantissas, powers(exponents), queries[:, 0, :], doc_ids, owners)
    given, kept, mine = fisher_terms(at, mantissas, exponents.T, pair, placed)
    got = [lax.ppermute(g, "yh", SWAP) for g in given]
    return finish(1.0 / total_rows, kept + got)[None], doc_block(at, mine)


def solution(mesh):
    fine = Mesh(mesh.devices.reshape(YH, Z, X, YL, CORE), ("yh", "z", "x", "yl", "core"))
    in_specs = (
        P(ROW_AXES, "x", None),
        P(ROW_AXES, "x", None),
        P(COL_AXES, "x", None),
        P(ROW_AXES),
        P(),
    )
    out_specs = (P("x", ROW_AXES, COL_AXES), P(ROW_AXES, COL_AXES))
    return jax.shard_map(per_device, mesh=fine, in_specs=in_specs, out_specs=out_specs, check_vma=False)
```

```python
import functools

import jax
import jax.numpy as jnp
from jax import lax
from jax.experimental import pallas as pl
from jax.experimental.pallas import tpu as pltpu
from jax.sharding import Mesh, PartitionSpec as P

YH, Z, X, YL, CORE = 2, 8, 4, 2, 2
ROW_AXES = ("yh", "z")
COL_AXES = ("yl", "core")
SWAP = [(0, 1), (1, 0)]
RING = [(2 * i, 2 * ((i + 1) % Z)) for i in range(Z)] + [(2 * i + 1, 2 * ((i - 1) % Z) + 1) for i in range(Z)]
TURNED = (((0,), (0,)), ((), ()))


def powers(exponents):
    return jnp.exp2(exponents.astype(jnp.float32)).astype(jnp.bfloat16)


def params(mebibytes):
    return pltpu.CompilerParams(vmem_limit_bytes=mebibytes << 20)


def cost(flops, moved):
    return pl.CostEstimate(flops=flops, bytes_accessed=moved, transcendentals=0)


AT_Z, AT_CORE, AT_YL, AT_OWN, AT_FAR, AT_YH, AT_X = 0, 1, 2, 3, 4, 5, 6


def wide_scale(turned, first_block, columns):
    blocks = turned.shape[0]
    lane_block = lax.broadcasted_iota(jnp.int32, (blocks, columns), 1) // 128 + first_block
    pick = (lane_block == lax.broadcasted_iota(jnp.int32, (blocks, columns), 0)).astype(jnp.bfloat16)
    return lax.dot_general(turned, pick, TURNED, preferred_element_type=jnp.float32)


FAR = 32


def dequant_kernel(at, exps, values, own_values, far_values, low, high, own, far_scale):
    step = pl.program_id(0)
    rows, half = values.shape[0], own.shape[0]
    turned = powers(exps[...])

    @pl.when(step == 0)
    def _():
        far_scale[...] = wide_scale(turned, at[AT_FAR] * 2, 256)
        scale = wide_scale(turned, at[AT_OWN] * 2, 256)
        scale = jnp.where(at[AT_CORE] == 0, scale[:half], scale[half:])
        own[...] = (own_values[...].astype(jnp.float32) * scale).astype(jnp.bfloat16)

    grads = values[...].astype(jnp.float32) * wide_scale(turned, at[AT_YL] * 16 + step * 4, 512)
    grads = grads.astype(jnp.bfloat16)
    low[0:rows] = jnp.concatenate([grads[:, 0:128], grads[:, 256:384]], 1)
    high[...] = jnp.concatenate([grads[:, 128:256], grads[:, 384:512]], 1)
    scale = far_scale[pl.ds(pl.multiple_of(at[AT_CORE] * half + step * FAR, FAR), FAR)]
    low[rows : rows + FAR] = (far_values[...].astype(jnp.float32) * scale).astype(jnp.bfloat16)


def dequant(at, exps, mantissas):
    rows, width = mantissas.shape
    half = rows // 2
    return pl.pallas_call(
        dequant_kernel,
        grid_spec=pltpu.PrefetchScalarGridSpec(
            num_scalar_prefetch=1,
            grid=(4,),
            in_specs=[
                pl.BlockSpec(exps.shape, lambda g, at: (0, 0)),
                pl.BlockSpec((rows, 512), lambda g, at: (0, at[AT_YL] * 4 + g)),
                pl.BlockSpec((half, 256), lambda g, at: (at[AT_CORE], at[AT_OWN])),
                pl.BlockSpec((FAR, 256), lambda g, at: (at[AT_CORE] * 4 + g, at[AT_FAR])),
            ],
            out_specs=[
                pl.BlockSpec((rows + FAR, 256), lambda g, at: (0, g)),
                pl.BlockSpec((rows, 256), lambda g, at: (0, g)),
                pl.BlockSpec((half, 256), lambda g, at: (0, 0)),
            ],
            scratch_shapes=[pltpu.VMEM((rows, 256), jnp.float32)],
        ),
        out_shape=[
            jax.ShapeDtypeStruct((rows + FAR, width // 4), jnp.bfloat16),
            jax.ShapeDtypeStruct((rows, width // 4), jnp.bfloat16),
            jax.ShapeDtypeStruct((half, 256), jnp.bfloat16),
        ],
        compiler_params=params(62),
        cost_estimate=cost(1 << 25, 2 << 20),
        name="dequant",
    )(at, exps, mantissas, mantissas, mantissas)


def halve_kernel(at, low, far, high, low_lanes, high_lanes, after, low_half, high_half, third):
    del after
    half = low.shape[0]
    low_half[0:half] = low[...]
    low_half[half : half + FAR] = far[...]
    high_half[...] = high[...]
    third[...] = jnp.concatenate([low_lanes[...], high_lanes[...]], 1)


def halve(at, low, high, after):
    rows, width = high.shape
    half = rows // 2
    return pl.pallas_call(
        halve_kernel,
        grid_spec=pltpu.PrefetchScalarGridSpec(
            num_scalar_prefetch=1,
            grid=(1,),
            in_specs=[
                pl.BlockSpec((half, width), lambda g, at: (at[AT_CORE], 0)),
                pl.BlockSpec((FAR, width), lambda g, at: (rows // FAR, 0)),
                pl.BlockSpec((half, width), lambda g, at: (at[AT_CORE], 0)),
                lanes_at_z(rows, False),
                lanes_at_z(rows, False),
                pl.BlockSpec(memory_space=pl.ANY),
            ],
            out_specs=[
                pl.BlockSpec((half + FAR, width), lambda g, at: (0, 0)),
                pl.BlockSpec((half, width), lambda g, at: (0, 0)),
                pl.BlockSpec((rows, 256), lambda g, at: (0, 0)),
            ],
        ),
        out_shape=[
            jax.ShapeDtypeStruct((half + FAR, width), jnp.bfloat16),
            jax.ShapeDtypeStruct((half, width), jnp.bfloat16),
            jax.ShapeDtypeStruct((rows, 256), jnp.bfloat16),
        ],
        compiler_params=params(8),
        cost_estimate=cost(0, 2 << 20),
        name="halve",
    )(at, low, low, high, low, high, after)


def pick_kernel(count, at, *refs):
    sides, out = refs[: 2 * count], refs[-1]
    row = 0
    for i in range(count):
        rows = sides[2 * i].shape[0]
        out[row : row + rows] = jnp.concatenate([sides[2 * i][...], sides[2 * i + 1][...]], 1)
        row += rows


def lanes_at_z(rows, by_core):
    if by_core:
        return pl.BlockSpec((rows, 128), lambda g, at: (at[AT_CORE], at[AT_Z]))
    return pl.BlockSpec((rows, 128), lambda g, at: (0, at[AT_Z]))


def pick(at, pieces, *after):
    rows = sum(n for n, _, _, _ in pieces)
    specs = [lanes_at_z(n, by_core) for n, by_core, _, _ in pieces for _ in range(2)]
    specs += [pl.BlockSpec(memory_space=pl.ANY)] * len(after)
    return pl.pallas_call(
        functools.partial(pick_kernel, len(pieces)),
        grid_spec=pltpu.PrefetchScalarGridSpec(
            num_scalar_prefetch=1, grid=(1,), in_specs=specs,
            out_specs=pl.BlockSpec((rows, 256), lambda g, at: (0, 0)),
        ),
        out_shape=jax.ShapeDtypeStruct((rows, 256), jnp.bfloat16),
        compiler_params=params(6),
        cost_estimate=cost(0, rows * 1024),
        name="pick",
    )(at, *[side for _, _, low, high in pieces for side in (low, high)], *after)


def gram_kernel(sizes, kept, parts, at, *refs):
    count = len(sizes)
    lows, highs = refs[:count], refs[count : 2 * count]
    low_rights, high_rights = refs[2 * count : 3 * count], refs[3 * count : 4 * count]
    own, near, third, far = refs[4 * count : 4 * count + 4]
    outs = refs[-1 - 2 * parts : -1]
    left = refs[-1]
    step = pl.program_id(0)

    @pl.when(step == 0)
    def _():
        mine_first = at[AT_YL] == at[AT_YH]
        use_mine = mine_first if kept else jnp.logical_not(mine_first)
        row, start = 0, 0
        for i, rows in enumerate(sizes):
            mine = jnp.concatenate([lows[i][...], highs[i][...]], 1)
            if 0 < i < count - 2:
                theirs = near[row : row + rows]
                row += rows
            else:
                theirs = (own if i == 0 else third)[...] if i < count - 1 else jnp.concatenate(
                    [far[:, lane : lane + 256] for lane in range(0, 1024, 256)], 0
                )
            left[start : start + rows] = jnp.where(use_mine, mine, theirs)
            start += rows

    def terms(rights):
        total, start = None, 0
        for i, rows in enumerate(sizes):
            term = lax.dot_general(
                left[start : start + rows], rights[i][...], TURNED, preferred_element_type=jnp.float32
            )
            total = term if total is None else total + term
            start += rows
        return total

    for part in range(parts):

        @pl.when(step == part)
        def _(part=part):
            outs[2 * part][...] = terms(low_rights)
            outs[2 * part + 1][...] = terms(high_rights)


def gram(at, pieces, received, kept, parts, *after):
    first = parts[0]
    sizes = tuple(n for n, _, _, _ in pieces)
    specs = [lanes_at_z(n, by_core) for n, by_core, _, _ in pieces] * 2
    for n, by_core, _, _ in pieces:
        specs.append(
            pl.BlockSpec(
                (n, 512),
                lambda g, at, by_core=by_core: (
                    at[AT_CORE] if by_core else 0,
                    (1 - first - g) * (1 - at[AT_CORE]) + (first + g) * at[AT_CORE],
                ),
            )
        )
    specs += specs[-len(pieces) :]
    specs += [pl.BlockSpec(r.shape, lambda g, at: (0, 0)) for r in received]
    last = pieces[-1][2]
    specs.append(pl.BlockSpec((FAR, last.shape[1]), lambda g, at: (last.shape[0] // FAR - 1, 0)))
    specs += [pl.BlockSpec(memory_space=pl.ANY)] * len(after)
    sides = [p[2] for p in pieces], [p[3] for p in pieces]
    return pl.pallas_call(
        functools.partial(gram_kernel, sizes, kept, len(parts)),
        grid_spec=pltpu.PrefetchScalarGridSpec(
            num_scalar_prefetch=1, grid=(len(parts),), in_specs=specs,
            out_specs=[pl.BlockSpec((256, 512), lambda g, at: (0, 0))] * (2 * len(parts)),
            scratch_shapes=[pltpu.VMEM((sum(sizes), 256), jnp.bfloat16)],
        ),
        out_shape=[jax.ShapeDtypeStruct((256, 512), jnp.float32)] * (2 * len(parts)),
        compiler_params=params(20),
        cost_estimate=cost(0, 0),
        name="gram",
    )(at, *sides[0], *sides[1], *sides[0], *sides[1], *received, last, *after)


def add_kernel(low, high, low_got, high_got, out):
    columns = low.shape[1]
    out[:, 0:columns] = low[...] + low_got[...]
    out[:, columns:] = high[...] + high_got[...]


def add(terms):
    rows, columns = terms[0].shape
    return pl.pallas_call(
        add_kernel,
        grid=(2,),
        in_specs=[pl.BlockSpec((rows // 2, columns), lambda g: (g, 0))] * 4,
        out_specs=pl.BlockSpec((rows // 2, 2 * columns), lambda g: (g, 0)),
        out_shape=jax.ShapeDtypeStruct((rows, 2 * columns), jnp.float32),
        compiler_params=params(6),
        cost_estimate=cost(0, 0),
        name="add",
    )(*terms)


def finish_kernel(factor, low, high, low_core, high_core, got, out):
    for i in range(4):
        lanes = slice(i * 128, i * 128 + 128)
        first = (low[:, lanes] + low_core[:, lanes]) + got[:, lanes]
        second = (high[:, lanes] + high_core[:, lanes]) + got[:, 512 + i * 128 : 640 + i * 128]
        out[:, i * 256 : i * 256 + 128] = first * factor
        out[:, i * 256 + 128 : i * 256 + 256] = second * factor


def finish(factor, terms):
    rows, columns = terms[0].shape
    return pl.pallas_call(
        functools.partial(finish_kernel, factor),
        grid=(4,),
        in_specs=[pl.BlockSpec((rows // 4, columns), lambda g: (g, 0))] * 4
        + [pl.BlockSpec((rows // 4, 2 * columns), lambda g: (g, 0))],
        out_specs=pl.BlockSpec((rows // 4, 2 * columns), lambda g: (g, 0)),
        out_shape=jax.ShapeDtypeStruct((rows, 2 * columns), jnp.float32),
        compiler_params=params(8),
        cost_estimate=cost(1 << 20, 4 << 20),
        name="finish",
    )(*terms)


def tie_kernel(*refs):
    del refs


def tie(value, *earlier):
    return pl.pallas_call(
        tie_kernel,
        in_specs=[pl.BlockSpec(memory_space=pl.ANY)] * (1 + len(earlier)),
        out_specs=pl.BlockSpec(memory_space=pl.ANY),
        out_shape=jax.ShapeDtypeStruct(value.shape, value.dtype),
        input_output_aliases={0: 0},
        compiler_params=params(1),
        cost_estimate=cost(0, 0),
        name="tie",
    )(value, *earlier)


def fisher_terms(at, mantissas, exps, pair, placed):
    rows = mantissas.shape[0]
    low, high, own = dequant(at, exps, mantissas)

    half = rows // 2
    pieces = [(half, True, low, high)]
    for step in range(1, Z // 2 + 1):
        if step == Z // 2:
            low, high, third = halve(at, low, high, near)
        low = lax.ppermute(low, ("z", "core"), RING)
        high = lax.ppermute(high, ("z", "core"), RING)
        if step == 1:
            low = tie(low, pair)
        if step == 2:
            low = tie(low, placed)
        pieces.append((rows if step < Z // 2 else half, False, low, high))
        if step == 2:
            near = pick(at, pieces[1:3])
            placed = tie(placed, near)
            near = lax.ppermute(near, "yl", SWAP)
    mine = own_slots(placed)
    received = (own, near, lax.ppermute(third, "yl", SWAP))

    given_other = gram(at, pieces, received, False, (0,), mine)
    swapped = [lax.ppermute(g, "core", SWAP) for g in given_other]
    given_own = gram(at, pieces, received, False, (1,), *given_other)
    given = add([*given_own, *swapped])
    *kept_other, low_kept, high_kept = gram(at, pieces, received, True, (0, 1), given)
    kept = [lax.ppermute(k, "core", SWAP) for k in kept_other]
    return given, [low_kept, high_kept, *kept], mine


def spread(scale):
    blocks = scale.shape[1]
    lane_block = jnp.arange(blocks * 128, dtype=jnp.int32) // 128
    pick = (lane_block[None, :] == jnp.arange(blocks, dtype=jnp.int32)[:, None]).astype(jnp.bfloat16)
    wide = lax.dot_general(scale, pick, (((1,), (0,)), ((), ())), preferred_element_type=jnp.float32)
    return wide.astype(jnp.bfloat16)


def place_kernel(at, pair, got, ids, owners, out):
    docs, rows = owners.shape[1], ids.shape[1]
    summed = jnp.where(at[AT_X] % 2 == 0, pair[0], pair[1]) + got[...]
    owner = jnp.broadcast_to(owners[...], (8, docs))
    digit = jnp.where(lax.broadcasted_iota(jnp.int32, (8, docs), 0) == 0, owner >> 5, owner & 31)
    doc = (lax.broadcasted_iota(jnp.int32, (docs, rows), 0) == ids[...]).astype(jnp.bfloat16)
    digits = lax.dot_general(
        digit.astype(jnp.float32).astype(jnp.bfloat16), doc, (((1,), (0,)), ((), ())),
        preferred_element_type=jnp.float32,
    )
    slots = (digits[0:1] * 32.0 + digits[1:2]).astype(jnp.int32)
    count = out.shape[0]
    own_docs = docs // (YH * Z)
    half = own_docs // 2
    place = lax.broadcasted_iota(jnp.int32, (count, rows), 0)
    place = (place // half) * own_docs + place % half
    member = jnp.concatenate([place == slots, place + half == slots], 1)
    member = jnp.where(member, 1.0, 0.0).astype(jnp.bfloat16)
    zero = jnp.zeros_like(summed)
    rest = jnp.concatenate(
        [jnp.concatenate([summed, zero], 1), jnp.concatenate([zero, summed], 1)], 0
    )
    total = None
    for _ in range(3):
        part = rest.astype(jnp.bfloat16)
        rest = rest - part.astype(jnp.float32)
        term = lax.dot_general(member, part, (((1,), (1,)), ((), ())), preferred_element_type=jnp.float32)
        total = term if total is None else total + term
    out[...] = total


def sum_kernel(parts, out):
    total = parts[0]
    for i in range(1, parts.shape[0]):
        total = total + parts[i]
    out[...] = total


def flipped(bit):
    return [(i, i ^ bit) for i in range(X)]


def whole(shape):
    return pl.BlockSpec(shape, lambda g, at: (0,) * len(shape))


def placed_scores(at, mantissas, scale, queries, doc_ids, owners):
    docs = owners.shape[0]
    x = lax.axis_index("x")
    grads = mantissas * spread(scale)
    scores = lax.dot_general(queries, grads, (((1,), (1,)), ((), ())), preferred_element_type=jnp.float32)
    count, rows = scores.shape
    share, half = count // X, docs // (YH * Z) // 2
    upper = x // 2
    got = lax.ppermute(lax.dynamic_slice_in_dim(scores, (1 - upper) * 2 * share, 2 * share, 0), "x", flipped(2))
    pair = lax.dynamic_slice_in_dim(scores, upper * 2 * share, 2 * share, 0) + got
    got = lax.ppermute(lax.dynamic_slice_in_dim(pair, (1 - x % 2) * share, share, 0), "x", flipped(1))
    shapes = (X // 2, share, rows), (share, rows), (1, rows), (1, docs)
    placed = pl.pallas_call(
        place_kernel,
        grid_spec=pltpu.PrefetchScalarGridSpec(
            num_scalar_prefetch=1, grid=(1,), in_specs=[whole(shape) for shape in shapes],
            out_specs=whole((YH * Z * half, 2 * share)),
        ),
        out_shape=jax.ShapeDtypeStruct((YH * Z * half, 2 * share), jnp.float32),
        compiler_params=params(10),
        cost_estimate=cost(1 << 28, 1 << 20),
        name="place",
    )(at, pair.reshape(shapes[0]), got, doc_ids.reshape(1, rows), owners.reshape(1, docs))
    return pair, placed


def assemble_kernel(at, pair, far_pair, out):
    half, double = pair.shape[1:]
    share = double // 2
    values = []
    for source in range(X):
        near = (source // 2) == at[AT_X] // 2
        first = (source % 2) == at[AT_X] % 2
        own = jnp.where(first, pair[0], pair[1])
        other = jnp.where(first, far_pair[0], far_pair[1])
        values.append(jnp.where(near, own, other))
    out[0:half] = jnp.concatenate([v[:, :share] for v in values], 1)
    out[half:] = jnp.concatenate([v[:, share:] for v in values], 1)


def own_slots(placed):
    double = placed.shape[1]
    half = placed.shape[0] // (YH * Z)
    blocks = lax.all_to_all(placed.reshape(YH * Z, half, double), ("yh", "z"), 0, 0, tiled=True)
    return pl.pallas_call(
        sum_kernel,
        out_shape=jax.ShapeDtypeStruct((half, double), jnp.float32),
        compiler_params=params(4),
        cost_estimate=cost(1 << 16, 1 << 18),
        name="sum",
    )(blocks)


def doc_block(at, mine):
    half, double = mine.shape
    pair = jnp.stack([mine, lax.ppermute(mine, "x", flipped(1))])
    far_pair = lax.ppermute(pair, "x", flipped(2))
    return pl.pallas_call(
        assemble_kernel,
        grid_spec=pltpu.PrefetchScalarGridSpec(
            num_scalar_prefetch=1, grid=(1,), in_specs=[whole(pair.shape)] * 2,
            out_specs=whole((2 * half, X * double // 2)),
        ),
        out_shape=jax.ShapeDtypeStruct((2 * half, X * double // 2), jnp.float32),
        compiler_params=params(2),
        cost_estimate=cost(0, 1 << 17),
        name="assemble",
    )(at, pair, far_pair)


def per_device(mantissas, exponents, queries, doc_ids, owners):
    mantissas = mantissas[:, 0, :]
    exponents = exponents[:, 0, :]
    total_rows = mantissas.shape[0] * YH * Z
    yh, z, x = lax.axis_index("yh"), lax.axis_index("z"), lax.axis_index("x")
    yl, core = lax.axis_index("yl"), lax.axis_index("core")
    other = (1 - yl) * Z
    at = jnp.stack([z, core, yl, other + z, other + lax.rem(z + Z // 2, Z), yh, x]).astype(jnp.int32)
    pair, placed = placed_scores(at, mantissas, powers(exponents), queries[:, 0, :], doc_ids, owners)
    given, kept, mine = fisher_terms(at, mantissas, exponents.T, pair, placed)
    got = lax.ppermute(given, "yh", SWAP)
    return finish(1.0 / total_rows, kept + [got])[None], doc_block(at, mine)


def solution(mesh):
    fine = Mesh(mesh.devices.reshape(YH, Z, X, YL, CORE), ("yh", "z", "x", "yl", "core"))
    in_specs = (
        P(ROW_AXES, "x", None),
        P(ROW_AXES, "x", None),
        P(COL_AXES, "x", None),
        P(ROW_AXES),
        P(),
    )
    out_specs = (P("x", ROW_AXES, COL_AXES), P(ROW_AXES, COL_AXES))
    return jax.shard_map(per_device, mesh=fine, in_specs=in_specs, out_specs=out_specs, check_vma=False)
```

```python
import functools

import jax
import jax.numpy as jnp
from jax import lax
from jax.experimental import pallas as pl
from jax.experimental.pallas import tpu as pltpu
from jax.sharding import Mesh, PartitionSpec as P

YH, Z, X, YL, CORE = 2, 8, 4, 2, 2
ROW_AXES = ("yh", "z")
COL_AXES = ("yl", "core")
SWAP = [(0, 1), (1, 0)]
RING = [(2 * i, 2 * ((i + 1) % Z)) for i in range(Z)] + [(2 * i + 1, 2 * ((i - 1) % Z) + 1) for i in range(Z)]
TURNED = (((0,), (0,)), ((), ()))


def powers(exponents):
    return jnp.exp2(exponents.astype(jnp.float32)).astype(jnp.bfloat16)


def params(mebibytes):
    return pltpu.CompilerParams(vmem_limit_bytes=mebibytes << 20)


def cost(flops, moved):
    return pl.CostEstimate(flops=flops, bytes_accessed=moved, transcendentals=0)


AT_Z, AT_CORE, AT_YL, AT_OWN, AT_FAR, AT_YH, AT_X = 0, 1, 2, 3, 4, 5, 6


def wide_scale(turned, first_block, columns):
    blocks = turned.shape[0]
    lane_block = lax.broadcasted_iota(jnp.int32, (blocks, columns), 1) // 128 + first_block
    pick = (lane_block == lax.broadcasted_iota(jnp.int32, (blocks, columns), 0)).astype(jnp.bfloat16)
    return lax.dot_general(turned, pick, TURNED, preferred_element_type=jnp.float32)


FAR = 32


def dequant_kernel(at, exps, values, own_values, far_values, low, high, low_half, high_half, own, far_scale):
    step = pl.program_id(0)
    rows, half = values.shape[0], own.shape[0]
    turned = powers(exps[...])

    @pl.when(step == 0)
    def _():
        far_scale[...] = wide_scale(turned, at[AT_FAR] * 2, 256)
        scale = wide_scale(turned, at[AT_OWN] * 2, 256)
        scale = jnp.where(at[AT_CORE] == 0, scale[:half], scale[half:])
        own[...] = (own_values[...].astype(jnp.float32) * scale).astype(jnp.bfloat16)

    grads = values[...].astype(jnp.float32) * wide_scale(turned, at[AT_YL] * 16 + step * 4, 512)
    grads = grads.astype(jnp.bfloat16)
    lows = jnp.concatenate([grads[:, 0:128], grads[:, 256:384]], 1)
    highs = jnp.concatenate([grads[:, 128:256], grads[:, 384:512]], 1)
    low[0:rows], high[...] = lows, highs
    low_half[...] = jnp.where(at[AT_CORE] == 0, lows[:half], lows[half:])
    high_half[...] = jnp.where(at[AT_CORE] == 0, highs[:half], highs[half:])
    scale = far_scale[pl.ds(pl.multiple_of(at[AT_CORE] * half + step * FAR, FAR), FAR)]
    low[rows : rows + FAR] = (far_values[...].astype(jnp.float32) * scale).astype(jnp.bfloat16)


def dequant(at, exps, mantissas):
    rows, width = mantissas.shape
    half = rows // 2
    return pl.pallas_call(
        dequant_kernel,
        grid_spec=pltpu.PrefetchScalarGridSpec(
            num_scalar_prefetch=1,
            grid=(4,),
            in_specs=[
                pl.BlockSpec(exps.shape, lambda g, at: (0, 0)),
                pl.BlockSpec((rows, 512), lambda g, at: (0, at[AT_YL] * 4 + g)),
                pl.BlockSpec((half, 256), lambda g, at: (at[AT_CORE], at[AT_OWN])),
                pl.BlockSpec((FAR, 256), lambda g, at: (at[AT_CORE] * 4 + g, at[AT_FAR])),
            ],
            out_specs=[
                pl.BlockSpec((rows + FAR, 256), lambda g, at: (0, g)),
                pl.BlockSpec((rows, 256), lambda g, at: (0, g)),
                pl.BlockSpec((half, 256), lambda g, at: (0, g)),
                pl.BlockSpec((half, 256), lambda g, at: (0, g)),
                pl.BlockSpec((half, 256), lambda g, at: (0, 0)),
            ],
            scratch_shapes=[pltpu.VMEM((rows, 256), jnp.float32)],
        ),
        out_shape=[
            jax.ShapeDtypeStruct((rows + FAR, width // 4), jnp.bfloat16),
            jax.ShapeDtypeStruct((rows, width // 4), jnp.bfloat16),
            jax.ShapeDtypeStruct((half, width // 4), jnp.bfloat16),
            jax.ShapeDtypeStruct((half, width // 4), jnp.bfloat16),
            jax.ShapeDtypeStruct((half, 256), jnp.bfloat16),
        ],
        compiler_params=params(62),
        cost_estimate=cost(1 << 25, 2 << 20),
        name="dequant",
    )(at, exps, mantissas, mantissas, mantissas)


def halve_kernel(at, low, far, high, low_lanes, high_lanes, after, low_half, high_half, third):
    del after
    half = low.shape[0]
    low_half[0:half] = low[...]
    low_half[half : half + FAR] = far[...]
    high_half[...] = high[...]
    third[...] = jnp.concatenate([low_lanes[...], high_lanes[...]], 1)


def halve(at, low, high, after):
    rows, width = high.shape
    half = rows // 2
    return pl.pallas_call(
        halve_kernel,
        grid_spec=pltpu.PrefetchScalarGridSpec(
            num_scalar_prefetch=1,
            grid=(1,),
            in_specs=[
                pl.BlockSpec((half, width), lambda g, at: (at[AT_CORE], 0)),
                pl.BlockSpec((FAR, width), lambda g, at: (rows // FAR, 0)),
                pl.BlockSpec((half, width), lambda g, at: (at[AT_CORE], 0)),
                lanes_at_z(rows, False),
                lanes_at_z(rows, False),
                pl.BlockSpec(memory_space=pl.ANY),
            ],
            out_specs=[
                pl.BlockSpec((half + FAR, width), lambda g, at: (0, 0)),
                pl.BlockSpec((half, width), lambda g, at: (0, 0)),
                pl.BlockSpec((rows, 256), lambda g, at: (0, 0)),
            ],
        ),
        out_shape=[
            jax.ShapeDtypeStruct((half + FAR, width), jnp.bfloat16),
            jax.ShapeDtypeStruct((half, width), jnp.bfloat16),
            jax.ShapeDtypeStruct((rows, 256), jnp.bfloat16),
        ],
        compiler_params=params(8),
        cost_estimate=cost(0, 2 << 20),
        name="halve",
    )(at, low, low, high, low, high, after)


def pick_kernel(count, at, *refs):
    sides, out = refs[: 2 * count], refs[-1]
    row = 0
    for i in range(count):
        rows = sides[2 * i].shape[0]
        out[row : row + rows] = jnp.concatenate([sides[2 * i][...], sides[2 * i + 1][...]], 1)
        row += rows


def lanes_at_z(rows, by_core):
    if by_core:
        return pl.BlockSpec((rows, 128), lambda g, at: (at[AT_CORE], at[AT_Z]))
    return pl.BlockSpec((rows, 128), lambda g, at: (0, at[AT_Z]))


def pick(at, pieces, *after):
    rows = sum(n for n, _, _, _ in pieces)
    specs = [lanes_at_z(n, by_core) for n, by_core, _, _ in pieces for _ in range(2)]
    specs += [pl.BlockSpec(memory_space=pl.ANY)] * len(after)
    return pl.pallas_call(
        functools.partial(pick_kernel, len(pieces)),
        grid_spec=pltpu.PrefetchScalarGridSpec(
            num_scalar_prefetch=1, grid=(1,), in_specs=specs,
            out_specs=pl.BlockSpec((rows, 256), lambda g, at: (0, 0)),
        ),
        out_shape=jax.ShapeDtypeStruct((rows, 256), jnp.bfloat16),
        compiler_params=params(6),
        cost_estimate=cost(0, rows * 1024),
        name="pick",
    )(at, *[side for _, _, low, high in pieces for side in (low, high)], *after)


def gram_kernel(sizes, kept, parts, at, *refs):
    count = len(sizes)
    lows, highs = refs[:count], refs[count : 2 * count]
    low_rights, high_rights = refs[2 * count : 3 * count], refs[3 * count : 4 * count]
    own, near, third, far = refs[4 * count : 4 * count + 4]
    outs = refs[-1 - 2 * parts : -1]
    left = refs[-1]
    step = pl.program_id(0)

    @pl.when(step == 0)
    def _():
        mine_first = at[AT_YL] == at[AT_YH]
        use_mine = mine_first if kept else jnp.logical_not(mine_first)
        row, start = 0, 0
        for i, rows in enumerate(sizes):
            mine = jnp.concatenate([lows[i][...], highs[i][...]], 1)
            if 0 < i < count - 2:
                theirs = near[row : row + rows]
                row += rows
            else:
                theirs = (own if i == 0 else third)[...] if i < count - 1 else jnp.concatenate(
                    [far[:, lane : lane + 256] for lane in range(0, 1024, 256)], 0
                )
            left[start : start + rows] = jnp.where(use_mine, mine, theirs)
            start += rows

    def terms(rights):
        total, start = None, 0
        for i, rows in enumerate(sizes):
            term = lax.dot_general(
                left[start : start + rows], rights[i][...], TURNED, preferred_element_type=jnp.float32
            )
            total = term if total is None else total + term
            start += rows
        return total

    for part in range(parts):

        @pl.when(step == part)
        def _(part=part):
            outs[2 * part][...] = terms(low_rights)
            outs[2 * part + 1][...] = terms(high_rights)


def gram(at, pieces, received, kept, parts, *after):
    first = parts[0]
    sizes = tuple(n for n, _, _, _ in pieces)
    specs = [lanes_at_z(n, by_core) for n, by_core, _, _ in pieces] * 2
    for n, by_core, _, _ in pieces:
        specs.append(
            pl.BlockSpec(
                (n, 512),
                lambda g, at, by_core=by_core: (
                    at[AT_CORE] if by_core else 0,
                    (1 - first - g) * (1 - at[AT_CORE]) + (first + g) * at[AT_CORE],
                ),
            )
        )
    specs += specs[-len(pieces) :]
    specs += [pl.BlockSpec(r.shape, lambda g, at: (0, 0)) for r in received]
    last = pieces[-1][2]
    specs.append(pl.BlockSpec((FAR, last.shape[1]), lambda g, at: (last.shape[0] // FAR - 1, 0)))
    specs += [pl.BlockSpec(memory_space=pl.ANY)] * len(after)
    sides = [p[2] for p in pieces], [p[3] for p in pieces]
    return pl.pallas_call(
        functools.partial(gram_kernel, sizes, kept, len(parts)),
        grid_spec=pltpu.PrefetchScalarGridSpec(
            num_scalar_prefetch=1, grid=(len(parts),), in_specs=specs,
            out_specs=[pl.BlockSpec((256, 512), lambda g, at: (0, 0))] * (2 * len(parts)),
            scratch_shapes=[pltpu.VMEM((sum(sizes), 256), jnp.bfloat16)],
        ),
        out_shape=[jax.ShapeDtypeStruct((256, 512), jnp.float32)] * (2 * len(parts)),
        compiler_params=params(20),
        cost_estimate=cost(0, 0),
        name="gram",
    )(at, *sides[0], *sides[1], *sides[0], *sides[1], *received, last, *after)


def add_kernel(low, high, low_got, high_got, out):
    columns = low.shape[1]
    out[:, 0:columns] = low[...] + low_got[...]
    out[:, columns:] = high[...] + high_got[...]


def add(terms):
    rows, columns = terms[0].shape
    return pl.pallas_call(
        add_kernel,
        grid=(2,),
        in_specs=[pl.BlockSpec((rows // 2, columns), lambda g: (g, 0))] * 4,
        out_specs=pl.BlockSpec((rows // 2, 2 * columns), lambda g: (g, 0)),
        out_shape=jax.ShapeDtypeStruct((rows, 2 * columns), jnp.float32),
        compiler_params=params(6),
        cost_estimate=cost(0, 0),
        name="add",
    )(*terms)


def finish_kernel(factor, low, high, low_core, high_core, got, out):
    for i in range(4):
        lanes = slice(i * 128, i * 128 + 128)
        first = (low[:, lanes] + low_core[:, lanes]) + got[:, lanes]
        second = (high[:, lanes] + high_core[:, lanes]) + got[:, 512 + i * 128 : 640 + i * 128]
        out[:, i * 256 : i * 256 + 128] = first * factor
        out[:, i * 256 + 128 : i * 256 + 256] = second * factor


def finish(factor, terms):
    rows, columns = terms[0].shape
    return pl.pallas_call(
        functools.partial(finish_kernel, factor),
        grid=(4,),
        in_specs=[pl.BlockSpec((rows // 4, columns), lambda g: (g, 0))] * 4
        + [pl.BlockSpec((rows // 4, 2 * columns), lambda g: (g, 0))],
        out_specs=pl.BlockSpec((rows // 4, 2 * columns), lambda g: (g, 0)),
        out_shape=jax.ShapeDtypeStruct((rows, 2 * columns), jnp.float32),
        compiler_params=params(8),
        cost_estimate=cost(1 << 20, 4 << 20),
        name="finish",
    )(*terms)


def tie_kernel(*refs):
    del refs


def tie(value, *earlier):
    return pl.pallas_call(
        tie_kernel,
        in_specs=[pl.BlockSpec(memory_space=pl.ANY)] * (1 + len(earlier)),
        out_specs=pl.BlockSpec(memory_space=pl.ANY),
        out_shape=jax.ShapeDtypeStruct(value.shape, value.dtype),
        input_output_aliases={0: 0},
        compiler_params=params(1),
        cost_estimate=cost(0, 0),
        name="tie",
    )(value, *earlier)


def fisher_terms(at, mantissas, exps, pair, placed):
    rows = mantissas.shape[0]
    low, high, low_half, high_half, own = dequant(at, exps, mantissas)

    half = rows // 2
    pieces = [(half, False, low_half, high_half)]
    for step in range(1, Z // 2 + 1):
        if step == Z // 2:
            low, high, third = halve(at, low, high, near)
        low = lax.ppermute(low, ("z", "core"), RING)
        high = lax.ppermute(high, ("z", "core"), RING)
        if step == 1:
            low = tie(low, pair)
        if step == 2:
            low = tie(low, placed)
        pieces.append((rows if step < Z // 2 else half, False, low, high))
        if step == 2:
            near = pick(at, pieces[1:3])
            placed = tie(placed, near)
            near = lax.ppermute(near, "yl", SWAP)
    mine = own_slots(placed)
    received = (own, near, lax.ppermute(third, "yl", SWAP))

    given_other = gram(at, pieces, received, False, (0,))
    swapped = [lax.ppermute(g, "core", SWAP) for g in given_other]
    given_own = gram(at, pieces, received, False, (1,), *given_other)
    given = add([*given_own, *swapped])
    *kept_other, low_kept, high_kept = gram(at, pieces, received, True, (0, 1), given, mine)
    kept = [lax.ppermute(k, "core", SWAP) for k in kept_other]
    return given, [low_kept, high_kept, *kept], mine


def spread(scale):
    blocks = scale.shape[1]
    lane_block = jnp.arange(blocks * 128, dtype=jnp.int32) // 128
    pick = (lane_block[None, :] == jnp.arange(blocks, dtype=jnp.int32)[:, None]).astype(jnp.bfloat16)
    wide = lax.dot_general(scale, pick, (((1,), (0,)), ((), ())), preferred_element_type=jnp.float32)
    return wide.astype(jnp.bfloat16)


def place_kernel(at, pair, got, ids, owners, out):
    docs, rows = owners.shape[1], ids.shape[1]
    summed = jnp.where(at[AT_X] % 2 == 0, pair[0], pair[1]) + got[...]
    owner = jnp.broadcast_to(owners[...], (8, docs))
    digit = jnp.where(lax.broadcasted_iota(jnp.int32, (8, docs), 0) == 0, owner >> 5, owner & 31)
    doc = (lax.broadcasted_iota(jnp.int32, (docs, rows), 0) == ids[...]).astype(jnp.bfloat16)
    digits = lax.dot_general(
        digit.astype(jnp.float32).astype(jnp.bfloat16), doc, (((1,), (0,)), ((), ())),
        preferred_element_type=jnp.float32,
    )
    slots = (digits[0:1] * 32.0 + digits[1:2]).astype(jnp.int32)
    count = out.shape[0]
    own_docs = docs // (YH * Z)
    half = own_docs // 2
    place = lax.broadcasted_iota(jnp.int32, (count, rows), 0)
    place = (place // half) * own_docs + place % half
    member = jnp.concatenate([place == slots, place + half == slots], 1)
    member = jnp.where(member, 1.0, 0.0).astype(jnp.bfloat16)
    zero = jnp.zeros_like(summed)
    rest = jnp.concatenate(
        [jnp.concatenate([summed, zero], 1), jnp.concatenate([zero, summed], 1)], 0
    )
    total = None
    for _ in range(3):
        part = rest.astype(jnp.bfloat16)
        rest = rest - part.astype(jnp.float32)
        term = lax.dot_general(member, part, (((1,), (1,)), ((), ())), preferred_element_type=jnp.float32)
        total = term if total is None else total + term
    out[...] = total


def sum_kernel(parts, out):
    total = parts[0]
    for i in range(1, parts.shape[0]):
        total = total + parts[i]
    out[...] = total


def flipped(bit):
    return [(i, i ^ bit) for i in range(X)]


def whole(shape):
    return pl.BlockSpec(shape, lambda g, at: (0,) * len(shape))


def placed_scores(at, mantissas, scale, queries, doc_ids, owners):
    docs = owners.shape[0]
    x = lax.axis_index("x")
    grads = mantissas * spread(scale)
    scores = lax.dot_general(queries, grads, (((1,), (1,)), ((), ())), preferred_element_type=jnp.float32)
    count, rows = scores.shape
    share, half = count // X, docs // (YH * Z) // 2
    upper = x // 2
    got = lax.ppermute(lax.dynamic_slice_in_dim(scores, (1 - upper) * 2 * share, 2 * share, 0), "x", flipped(2))
    pair = lax.dynamic_slice_in_dim(scores, upper * 2 * share, 2 * share, 0) + got
    got = lax.ppermute(lax.dynamic_slice_in_dim(pair, (1 - x % 2) * share, share, 0), "x", flipped(1))
    shapes = (X // 2, share, rows), (share, rows), (1, rows), (1, docs)
    placed = pl.pallas_call(
        place_kernel,
        grid_spec=pltpu.PrefetchScalarGridSpec(
            num_scalar_prefetch=1, grid=(1,), in_specs=[whole(shape) for shape in shapes],
            out_specs=whole((YH * Z * half, 2 * share)),
        ),
        out_shape=jax.ShapeDtypeStruct((YH * Z * half, 2 * share), jnp.float32),
        compiler_params=params(10),
        cost_estimate=cost(1 << 28, 1 << 20),
        name="place",
    )(at, pair.reshape(shapes[0]), got, doc_ids.reshape(1, rows), owners.reshape(1, docs))
    return pair, placed


def assemble_kernel(at, pair, far_pair, out):
    half, double = pair.shape[1:]
    share = double // 2
    values = []
    for source in range(X):
        near = (source // 2) == at[AT_X] // 2
        first = (source % 2) == at[AT_X] % 2
        own = jnp.where(first, pair[0], pair[1])
        other = jnp.where(first, far_pair[0], far_pair[1])
        values.append(jnp.where(near, own, other))
    out[0:half] = jnp.concatenate([v[:, :share] for v in values], 1)
    out[half:] = jnp.concatenate([v[:, share:] for v in values], 1)


def own_slots(placed):
    double = placed.shape[1]
    half = placed.shape[0] // (YH * Z)
    blocks = lax.all_to_all(placed.reshape(YH * Z, half, double), ("yh", "z"), 0, 0, tiled=True)
    return pl.pallas_call(
        sum_kernel,
        out_shape=jax.ShapeDtypeStruct((half, double), jnp.float32),
        compiler_params=params(4),
        cost_estimate=cost(1 << 16, 1 << 18),
        name="sum",
    )(blocks)


def doc_block(at, mine):
    half, double = mine.shape
    pair = jnp.stack([mine, lax.ppermute(mine, "x", flipped(1))])
    far_pair = lax.ppermute(pair, "x", flipped(2))
    return pl.pallas_call(
        assemble_kernel,
        grid_spec=pltpu.PrefetchScalarGridSpec(
            num_scalar_prefetch=1, grid=(1,), in_specs=[whole(pair.shape)] * 2,
            out_specs=whole((2 * half, X * double // 2)),
        ),
        out_shape=jax.ShapeDtypeStruct((2 * half, X * double // 2), jnp.float32),
        compiler_params=params(2),
        cost_estimate=cost(0, 1 << 17),
        name="assemble",
    )(at, pair, far_pair)


def per_device(mantissas, exponents, queries, doc_ids, owners):
    mantissas = mantissas[:, 0, :]
    exponents = exponents[:, 0, :]
    total_rows = mantissas.shape[0] * YH * Z
    yh, z, x = lax.axis_index("yh"), lax.axis_index("z"), lax.axis_index("x")
    yl, core = lax.axis_index("yl"), lax.axis_index("core")
    other = (1 - yl) * Z
    at = jnp.stack([z, core, yl, other + z, other + lax.rem(z + Z // 2, Z), yh, x]).astype(jnp.int32)
    pair, placed = placed_scores(at, mantissas, powers(exponents), queries[:, 0, :], doc_ids, owners)
    given, kept, mine = fisher_terms(at, mantissas, exponents.T, pair, placed)
    got = lax.ppermute(given, "yh", SWAP)
    return finish(1.0 / total_rows, kept + [got])[None], doc_block(at, mine)


def solution(mesh):
    fine = Mesh(mesh.devices.reshape(YH, Z, X, YL, CORE), ("yh", "z", "x", "yl", "core"))
    in_specs = (
        P(ROW_AXES, "x", None),
        P(ROW_AXES, "x", None),
        P(COL_AXES, "x", None),
        P(ROW_AXES),
        P(),
    )
    out_specs = (P("x", ROW_AXES, COL_AXES), P(ROW_AXES, COL_AXES))
    return jax.shard_map(per_device, mesh=fine, in_specs=in_specs, out_specs=out_specs, check_vma=False)
```

```python
import functools

import jax
import jax.numpy as jnp
from jax import lax
from jax.experimental import pallas as pl
from jax.experimental.pallas import tpu as pltpu
from jax.sharding import Mesh, PartitionSpec as P

YH, Z, X, YL, CORE = 2, 8, 4, 2, 2
ROW_AXES = ("yh", "z")
COL_AXES = ("yl", "core")
SWAP = [(0, 1), (1, 0)]
RING = [(2 * i, 2 * ((i + 1) % Z)) for i in range(Z)] + [(2 * i + 1, 2 * ((i - 1) % Z) + 1) for i in range(Z)]
TURNED = (((0,), (0,)), ((), ()))


def powers(exponents):
    return jnp.exp2(exponents.astype(jnp.float32)).astype(jnp.bfloat16)


def params(mebibytes):
    return pltpu.CompilerParams(vmem_limit_bytes=mebibytes << 20)


def cost(flops, moved):
    return pl.CostEstimate(flops=flops, bytes_accessed=moved, transcendentals=0)


AT_Z, AT_CORE, AT_YL, AT_OWN, AT_FAR, AT_YH, AT_X = 0, 1, 2, 3, 4, 5, 6


def wide_scale(turned, first_block, columns):
    blocks = turned.shape[0]
    lane_block = lax.broadcasted_iota(jnp.int32, (blocks, columns), 1) // 128 + first_block
    pick = (lane_block == lax.broadcasted_iota(jnp.int32, (blocks, columns), 0)).astype(jnp.bfloat16)
    return lax.dot_general(turned, pick, TURNED, preferred_element_type=jnp.float32)


FAR = 32


def dequant_kernel(at, exps, values, own_values, far_values, low, high, low_half, high_half, own, far_scale):
    step = pl.program_id(0)
    rows, half = values.shape[0], own.shape[0]
    turned = powers(exps[...])

    @pl.when(step == 0)
    def _():
        far_scale[...] = wide_scale(turned, at[AT_FAR] * 2, 256)
        scale = wide_scale(turned, at[AT_OWN] * 2, 256)
        scale = jnp.where(at[AT_CORE] == 0, scale[:half], scale[half:])
        own[...] = (own_values[...].astype(jnp.float32) * scale).astype(jnp.bfloat16)

    grads = values[...].astype(jnp.float32) * wide_scale(turned, at[AT_YL] * 16 + step * 4, 512)
    grads = grads.astype(jnp.bfloat16)
    lows = jnp.concatenate([grads[:, 0:128], grads[:, 256:384]], 1)
    highs = jnp.concatenate([grads[:, 128:256], grads[:, 384:512]], 1)
    low[0:rows], high[...] = lows, highs
    low_half[...] = jnp.where(at[AT_CORE] == 0, lows[:half], lows[half:])
    high_half[...] = jnp.where(at[AT_CORE] == 0, highs[:half], highs[half:])
    scale = far_scale[pl.ds(pl.multiple_of(at[AT_CORE] * half + step * FAR, FAR), FAR)]
    low[rows : rows + FAR] = (far_values[...].astype(jnp.float32) * scale).astype(jnp.bfloat16)


def dequant(at, exps, mantissas):
    rows, width = mantissas.shape
    half = rows // 2
    return pl.pallas_call(
        dequant_kernel,
        grid_spec=pltpu.PrefetchScalarGridSpec(
            num_scalar_prefetch=1,
            grid=(4,),
            in_specs=[
                pl.BlockSpec(exps.shape, lambda g, at: (0, 0)),
                pl.BlockSpec((rows, 512), lambda g, at: (0, at[AT_YL] * 4 + g)),
                pl.BlockSpec((half, 256), lambda g, at: (at[AT_CORE], at[AT_OWN])),
                pl.BlockSpec((FAR, 256), lambda g, at: (at[AT_CORE] * 4 + g, at[AT_FAR])),
            ],
            out_specs=[
                pl.BlockSpec((rows + FAR, 256), lambda g, at: (0, g)),
                pl.BlockSpec((rows, 256), lambda g, at: (0, g)),
                pl.BlockSpec((half, 256), lambda g, at: (0, g)),
                pl.BlockSpec((half, 256), lambda g, at: (0, g)),
                pl.BlockSpec((half, 256), lambda g, at: (0, 0)),
            ],
            scratch_shapes=[pltpu.VMEM((rows, 256), jnp.float32)],
        ),
        out_shape=[
            jax.ShapeDtypeStruct((rows + FAR, width // 4), jnp.bfloat16),
            jax.ShapeDtypeStruct((rows, width // 4), jnp.bfloat16),
            jax.ShapeDtypeStruct((half, width // 4), jnp.bfloat16),
            jax.ShapeDtypeStruct((half, width // 4), jnp.bfloat16),
            jax.ShapeDtypeStruct((half, 256), jnp.bfloat16),
        ],
        compiler_params=params(62),
        cost_estimate=cost(1 << 25, 2 << 20),
        name="dequant",
    )(at, exps, mantissas, mantissas, mantissas)


def halve_low_kernel(at, low, far, low_half):
    half = low.shape[0]
    low_half[0:half] = low[...]
    low_half[half : half + FAR] = far[...]


def halve_low(at, low):
    rows, width = low.shape[0] - FAR, low.shape[1]
    half = rows // 2
    return pl.pallas_call(
        halve_low_kernel,
        grid_spec=pltpu.PrefetchScalarGridSpec(
            num_scalar_prefetch=1,
            grid=(1,),
            in_specs=[
                pl.BlockSpec((half, width), lambda g, at: (at[AT_CORE], 0)),
                pl.BlockSpec((FAR, width), lambda g, at: (rows // FAR, 0)),
            ],
            out_specs=pl.BlockSpec((half + FAR, width), lambda g, at: (0, 0)),
        ),
        out_shape=jax.ShapeDtypeStruct((half + FAR, width), jnp.bfloat16),
        compiler_params=params(8),
        cost_estimate=cost(0, 1 << 19),
        name="halve_low",
    )(at, low, low)


def halve_high_kernel(at, high, low_lanes, high_lanes, after, high_half, third):
    del after
    high_half[...] = high[...]
    third[...] = jnp.concatenate([low_lanes[...], high_lanes[...]], 1)


def halve_high(at, low, high, after):
    rows, width = high.shape
    half = rows // 2
    return pl.pallas_call(
        halve_high_kernel,
        grid_spec=pltpu.PrefetchScalarGridSpec(
            num_scalar_prefetch=1,
            grid=(1,),
            in_specs=[
                pl.BlockSpec((half, width), lambda g, at: (at[AT_CORE], 0)),
                lanes_at_z(rows, False),
                lanes_at_z(rows, False),
                pl.BlockSpec(memory_space=pl.ANY),
            ],
            out_specs=[
                pl.BlockSpec((half, width), lambda g, at: (0, 0)),
                pl.BlockSpec((rows, 256), lambda g, at: (0, 0)),
            ],
        ),
        out_shape=[
            jax.ShapeDtypeStruct((half, width), jnp.bfloat16),
            jax.ShapeDtypeStruct((rows, 256), jnp.bfloat16),
        ],
        compiler_params=params(8),
        cost_estimate=cost(0, 1 << 20),
        name="halve_high",
    )(at, high, low, high, after)


def pick_kernel(count, at, *refs):
    sides, out = refs[: 2 * count], refs[-1]
    row = 0
    for i in range(count):
        rows = sides[2 * i].shape[0]
        out[row : row + rows] = jnp.concatenate([sides[2 * i][...], sides[2 * i + 1][...]], 1)
        row += rows


def lanes_at_z(rows, by_core):
    if by_core:
        return pl.BlockSpec((rows, 128), lambda g, at: (at[AT_CORE], at[AT_Z]))
    return pl.BlockSpec((rows, 128), lambda g, at: (0, at[AT_Z]))


def pick(at, pieces, *after):
    rows = sum(n for n, _, _, _ in pieces)
    specs = [lanes_at_z(n, by_core) for n, by_core, _, _ in pieces for _ in range(2)]
    specs += [pl.BlockSpec(memory_space=pl.ANY)] * len(after)
    return pl.pallas_call(
        functools.partial(pick_kernel, len(pieces)),
        grid_spec=pltpu.PrefetchScalarGridSpec(
            num_scalar_prefetch=1, grid=(1,), in_specs=specs,
            out_specs=pl.BlockSpec((rows, 256), lambda g, at: (0, 0)),
        ),
        out_shape=jax.ShapeDtypeStruct((rows, 256), jnp.bfloat16),
        compiler_params=params(6),
        cost_estimate=cost(0, rows * 1024),
        name="pick",
    )(at, *[side for _, _, low, high in pieces for side in (low, high)], *after)


def gram_kernel(sizes, kept, parts, at, *refs):
    count = len(sizes)
    lows, highs = refs[:count], refs[count : 2 * count]
    low_rights, high_rights = refs[2 * count : 3 * count], refs[3 * count : 4 * count]
    own, near, third, far = refs[4 * count : 4 * count + 4]
    outs = refs[-1 - 2 * parts : -1]
    left = refs[-1]
    step = pl.program_id(0)

    @pl.when(step == 0)
    def _():
        mine_first = at[AT_YL] == at[AT_YH]
        use_mine = mine_first if kept else jnp.logical_not(mine_first)
        row, start = 0, 0
        for i, rows in enumerate(sizes):
            mine = jnp.concatenate([lows[i][...], highs[i][...]], 1)
            if 0 < i < count - 2:
                theirs = near[row : row + rows]
                row += rows
            else:
                theirs = (own if i == 0 else third)[...] if i < count - 1 else jnp.concatenate(
                    [far[:, lane : lane + 256] for lane in range(0, 1024, 256)], 0
                )
            left[start : start + rows] = jnp.where(use_mine, mine, theirs)
            start += rows

    def terms(rights):
        total, start = None, 0
        for i, rows in enumerate(sizes):
            term = lax.dot_general(
                left[start : start + rows], rights[i][...], TURNED, preferred_element_type=jnp.float32
            )
            total = term if total is None else total + term
            start += rows
        return total

    for part in range(parts):

        @pl.when(step == part)
        def _(part=part):
            outs[2 * part][...] = terms(low_rights)
            outs[2 * part + 1][...] = terms(high_rights)


def gram(at, pieces, received, kept, parts, *after):
    first = parts[0]
    sizes = tuple(n for n, _, _, _ in pieces)
    specs = [lanes_at_z(n, by_core) for n, by_core, _, _ in pieces] * 2
    for n, by_core, _, _ in pieces:
        specs.append(
            pl.BlockSpec(
                (n, 512),
                lambda g, at, by_core=by_core: (
                    at[AT_CORE] if by_core else 0,
                    (1 - first - g) * (1 - at[AT_CORE]) + (first + g) * at[AT_CORE],
                ),
            )
        )
    specs += specs[-len(pieces) :]
    specs += [pl.BlockSpec(r.shape, lambda g, at: (0, 0)) for r in received]
    last = pieces[-1][2]
    specs.append(pl.BlockSpec((FAR, last.shape[1]), lambda g, at: (last.shape[0] // FAR - 1, 0)))
    specs += [pl.BlockSpec(memory_space=pl.ANY)] * len(after)
    sides = [p[2] for p in pieces], [p[3] for p in pieces]
    return pl.pallas_call(
        functools.partial(gram_kernel, sizes, kept, len(parts)),
        grid_spec=pltpu.PrefetchScalarGridSpec(
            num_scalar_prefetch=1, grid=(len(parts),), in_specs=specs,
            out_specs=[pl.BlockSpec((256, 512), lambda g, at: (0, 0))] * (2 * len(parts)),
            scratch_shapes=[pltpu.VMEM((sum(sizes), 256), jnp.bfloat16)],
        ),
        out_shape=[jax.ShapeDtypeStruct((256, 512), jnp.float32)] * (2 * len(parts)),
        compiler_params=params(20),
        cost_estimate=cost(0, 0),
        name="gram",
    )(at, *sides[0], *sides[1], *sides[0], *sides[1], *received, last, *after)


def add_kernel(low, high, low_got, high_got, out):
    columns = low.shape[1]
    out[:, 0:columns] = low[...] + low_got[...]
    out[:, columns:] = high[...] + high_got[...]


def add(terms):
    rows, columns = terms[0].shape
    return pl.pallas_call(
        add_kernel,
        grid=(2,),
        in_specs=[pl.BlockSpec((rows // 2, columns), lambda g: (g, 0))] * 4,
        out_specs=pl.BlockSpec((rows // 2, 2 * columns), lambda g: (g, 0)),
        out_shape=jax.ShapeDtypeStruct((rows, 2 * columns), jnp.float32),
        compiler_params=params(6),
        cost_estimate=cost(0, 0),
        name="add",
    )(*terms)


def finish_kernel(factor, low, high, low_core, high_core, got, out):
    for i in range(4):
        lanes = slice(i * 128, i * 128 + 128)
        first = (low[:, lanes] + low_core[:, lanes]) + got[:, lanes]
        second = (high[:, lanes] + high_core[:, lanes]) + got[:, 512 + i * 128 : 640 + i * 128]
        out[:, i * 256 : i * 256 + 128] = first * factor
        out[:, i * 256 + 128 : i * 256 + 256] = second * factor


def finish(factor, terms):
    rows, columns = terms[0].shape
    return pl.pallas_call(
        functools.partial(finish_kernel, factor),
        grid=(4,),
        in_specs=[pl.BlockSpec((rows // 4, columns), lambda g: (g, 0))] * 4
        + [pl.BlockSpec((rows // 4, 2 * columns), lambda g: (g, 0))],
        out_specs=pl.BlockSpec((rows // 4, 2 * columns), lambda g: (g, 0)),
        out_shape=jax.ShapeDtypeStruct((rows, 2 * columns), jnp.float32),
        compiler_params=params(8),
        cost_estimate=cost(1 << 20, 4 << 20),
        name="finish",
    )(*terms)


def tie_kernel(*refs):
    del refs


def tie(value, *earlier):
    return pl.pallas_call(
        tie_kernel,
        in_specs=[pl.BlockSpec(memory_space=pl.ANY)] * (1 + len(earlier)),
        out_specs=pl.BlockSpec(memory_space=pl.ANY),
        out_shape=jax.ShapeDtypeStruct(value.shape, value.dtype),
        input_output_aliases={0: 0},
        compiler_params=params(1),
        cost_estimate=cost(0, 0),
        name="tie",
    )(value, *earlier)


def fisher_terms(at, mantissas, exps, pair, placed):
    rows = mantissas.shape[0]
    low, high, low_half, high_half, own = dequant(at, exps, mantissas)

    half = rows // 2
    pieces = [(half, False, low_half, high_half)]
    for step in range(1, Z // 2 + 1):
        if step == Z // 2:
            high, third = halve_high(at, low, high, near)
            low = halve_low(at, low)
        low = lax.ppermute(low, ("z", "core"), RING)
        high = lax.ppermute(high, ("z", "core"), RING)
        if step == 1:
            low = tie(low, pair)
        if step == 2:
            low = tie(low, placed)
        pieces.append((rows if step < Z // 2 else half, False, low, high))
        if step == 2:
            near = pick(at, pieces[1:3])
            placed = tie(placed, near)
            near = lax.ppermute(near, "yl", SWAP)
    mine = own_slots(placed)
    received = (own, near, lax.ppermute(third, "yl", SWAP))

    given_other = gram(at, pieces, received, False, (0,), mine)
    swapped = [lax.ppermute(g, "core", SWAP) for g in given_other]
    given_own = gram(at, pieces, received, False, (1,), *given_other)
    given = add([*given_own, *swapped])
    *kept_other, low_kept, high_kept = gram(at, pieces, received, True, (0, 1), given)
    kept = [lax.ppermute(k, "core", SWAP) for k in kept_other]
    return given, [low_kept, high_kept, *kept], mine


def spread(scale):
    blocks = scale.shape[1]
    lane_block = jnp.arange(blocks * 128, dtype=jnp.int32) // 128
    pick = (lane_block[None, :] == jnp.arange(blocks, dtype=jnp.int32)[:, None]).astype(jnp.bfloat16)
    wide = lax.dot_general(scale, pick, (((1,), (0,)), ((), ())), preferred_element_type=jnp.float32)
    return wide.astype(jnp.bfloat16)


def place_kernel(at, pair, got, ids, owners, out):
    docs, rows = owners.shape[1], ids.shape[1]
    summed = jnp.where(at[AT_X] % 2 == 0, pair[0], pair[1]) + got[...]
    owner = jnp.broadcast_to(owners[...], (8, docs))
    digit = jnp.where(lax.broadcasted_iota(jnp.int32, (8, docs), 0) == 0, owner >> 5, owner & 31)
    doc = (lax.broadcasted_iota(jnp.int32, (docs, rows), 0) == ids[...]).astype(jnp.bfloat16)
    digits = lax.dot_general(
        digit.astype(jnp.float32).astype(jnp.bfloat16), doc, (((1,), (0,)), ((), ())),
        preferred_element_type=jnp.float32,
    )
    slots = (digits[0:1] * 32.0 + digits[1:2]).astype(jnp.int32)
    count = out.shape[0]
    own_docs = docs // (YH * Z)
    half = own_docs // 2
    place = lax.broadcasted_iota(jnp.int32, (count, rows), 0)
    place = (place // half) * own_docs + place % half
    member = jnp.concatenate([place == slots, place + half == slots], 1)
    member = jnp.where(member, 1.0, 0.0).astype(jnp.bfloat16)
    zero = jnp.zeros_like(summed)
    rest = jnp.concatenate(
        [jnp.concatenate([summed, zero], 1), jnp.concatenate([zero, summed], 1)], 0
    )
    total = None
    for _ in range(3):
        part = rest.astype(jnp.bfloat16)
        rest = rest - part.astype(jnp.float32)
        term = lax.dot_general(member, part, (((1,), (1,)), ((), ())), preferred_element_type=jnp.float32)
        total = term if total is None else total + term
    out[...] = total


def sum_kernel(parts, out):
    total = parts[0]
    for i in range(1, parts.shape[0]):
        total = total + parts[i]
    out[...] = total


def flipped(bit):
    return [(i, i ^ bit) for i in range(X)]


def whole(shape):
    return pl.BlockSpec(shape, lambda g, at: (0,) * len(shape))


def placed_scores(at, mantissas, scale, queries, doc_ids, owners):
    docs = owners.shape[0]
    x = lax.axis_index("x")
    grads = mantissas * spread(scale)
    scores = lax.dot_general(queries, grads, (((1,), (1,)), ((), ())), preferred_element_type=jnp.float32)
    count, rows = scores.shape
    share, half = count // X, docs // (YH * Z) // 2
    upper = x // 2
    got = lax.ppermute(lax.dynamic_slice_in_dim(scores, (1 - upper) * 2 * share, 2 * share, 0), "x", flipped(2))
    pair = lax.dynamic_slice_in_dim(scores, upper * 2 * share, 2 * share, 0) + got
    got = lax.ppermute(lax.dynamic_slice_in_dim(pair, (1 - x % 2) * share, share, 0), "x", flipped(1))
    shapes = (X // 2, share, rows), (share, rows), (1, rows), (1, docs)
    placed = pl.pallas_call(
        place_kernel,
        grid_spec=pltpu.PrefetchScalarGridSpec(
            num_scalar_prefetch=1, grid=(1,), in_specs=[whole(shape) for shape in shapes],
            out_specs=whole((YH * Z * half, 2 * share)),
        ),
        out_shape=jax.ShapeDtypeStruct((YH * Z * half, 2 * share), jnp.float32),
        compiler_params=params(10),
        cost_estimate=cost(1 << 28, 1 << 20),
        name="place",
    )(at, pair.reshape(shapes[0]), got, doc_ids.reshape(1, rows), owners.reshape(1, docs))
    return pair, placed


def assemble_kernel(at, pair, far_pair, out):
    half, double = pair.shape[1:]
    share = double // 2
    values = []
    for source in range(X):
        near = (source // 2) == at[AT_X] // 2
        first = (source % 2) == at[AT_X] % 2
        own = jnp.where(first, pair[0], pair[1])
        other = jnp.where(first, far_pair[0], far_pair[1])
        values.append(jnp.where(near, own, other))
    out[0:half] = jnp.concatenate([v[:, :share] for v in values], 1)
    out[half:] = jnp.concatenate([v[:, share:] for v in values], 1)


def own_slots(placed):
    double = placed.shape[1]
    half = placed.shape[0] // (YH * Z)
    blocks = lax.all_to_all(placed.reshape(YH * Z, half, double), ("yh", "z"), 0, 0, tiled=True)
    return pl.pallas_call(
        sum_kernel,
        out_shape=jax.ShapeDtypeStruct((half, double), jnp.float32),
        compiler_params=params(4),
        cost_estimate=cost(1 << 16, 1 << 18),
        name="sum",
    )(blocks)


def doc_block(at, mine):
    half, double = mine.shape
    pair = jnp.stack([mine, lax.ppermute(mine, "x", flipped(1))])
    far_pair = lax.ppermute(pair, "x", flipped(2))
    return pl.pallas_call(
        assemble_kernel,
        grid_spec=pltpu.PrefetchScalarGridSpec(
            num_scalar_prefetch=1, grid=(1,), in_specs=[whole(pair.shape)] * 2,
            out_specs=whole((2 * half, X * double // 2)),
        ),
        out_shape=jax.ShapeDtypeStruct((2 * half, X * double // 2), jnp.float32),
        compiler_params=params(2),
        cost_estimate=cost(0, 1 << 17),
        name="assemble",
    )(at, pair, far_pair)


def per_device(mantissas, exponents, queries, doc_ids, owners):
    mantissas = mantissas[:, 0, :]
    exponents = exponents[:, 0, :]
    total_rows = mantissas.shape[0] * YH * Z
    yh, z, x = lax.axis_index("yh"), lax.axis_index("z"), lax.axis_index("x")
    yl, core = lax.axis_index("yl"), lax.axis_index("core")
    other = (1 - yl) * Z
    at = jnp.stack([z, core, yl, other + z, other + lax.rem(z + Z // 2, Z), yh, x]).astype(jnp.int32)
    pair, placed = placed_scores(at, mantissas, powers(exponents), queries[:, 0, :], doc_ids, owners)
    given, kept, mine = fisher_terms(at, mantissas, exponents.T, pair, placed)
    got = lax.ppermute(given, "yh", SWAP)
    return finish(1.0 / total_rows, kept + [got])[None], doc_block(at, mine)


def solution(mesh):
    fine = Mesh(mesh.devices.reshape(YH, Z, X, YL, CORE), ("yh", "z", "x", "yl", "core"))
    in_specs = (
        P(ROW_AXES, "x", None),
        P(ROW_AXES, "x", None),
        P(COL_AXES, "x", None),
        P(ROW_AXES),
        P(),
    )
    out_specs = (P("x", ROW_AXES, COL_AXES), P(ROW_AXES, COL_AXES))
    return jax.shard_map(per_device, mesh=fine, in_specs=in_specs, out_specs=out_specs, check_vma=False)
```

```python
import functools

import jax
import jax.numpy as jnp
from jax import lax
from jax.experimental import pallas as pl
from jax.experimental.pallas import tpu as pltpu
from jax.sharding import Mesh, PartitionSpec as P

YH, Z, X, YL, CORE = 2, 8, 4, 2, 2
ROW_AXES = ("yh", "z")
COL_AXES = ("yl", "core")
SWAP = [(0, 1), (1, 0)]
RING = [(2 * i, 2 * ((i + 1) % Z)) for i in range(Z)] + [(2 * i + 1, 2 * ((i - 1) % Z) + 1) for i in range(Z)]
TURNED = (((0,), (0,)), ((), ()))


def powers(exponents):
    return jnp.exp2(exponents.astype(jnp.float32)).astype(jnp.bfloat16)


def params(mebibytes):
    return pltpu.CompilerParams(vmem_limit_bytes=mebibytes << 20)


def cost(flops, moved):
    return pl.CostEstimate(flops=flops, bytes_accessed=moved, transcendentals=0)


AT_Z, AT_CORE, AT_YL, AT_OWN, AT_FAR, AT_YH, AT_X = 0, 1, 2, 3, 4, 5, 6


def wide_scale(turned, first_block, columns):
    blocks = turned.shape[0]
    lane_block = lax.broadcasted_iota(jnp.int32, (blocks, columns), 1) // 128 + first_block
    pick = (lane_block == lax.broadcasted_iota(jnp.int32, (blocks, columns), 0)).astype(jnp.bfloat16)
    return lax.dot_general(turned, pick, TURNED, preferred_element_type=jnp.float32)


FAR = 32


def dequant_kernel(at, exps, values, own_values, far_values, low, high, low_half, high_half, own, far_scale):
    step = pl.program_id(0)
    rows, half = values.shape[0], own.shape[0]
    turned = powers(exps[...])

    @pl.when(step == 0)
    def _():
        far_scale[...] = wide_scale(turned, at[AT_FAR] * 2, 256)
        scale = wide_scale(turned, at[AT_OWN] * 2, 256)
        scale = jnp.where(at[AT_CORE] == 0, scale[:half], scale[half:])
        own[...] = (own_values[...].astype(jnp.float32) * scale).astype(jnp.bfloat16)

    grads = values[...] * wide_scale(turned, at[AT_YL] * 16 + step * 4, 512).astype(jnp.bfloat16)
    lows = jnp.concatenate([grads[:, 0:128], grads[:, 256:384]], 1)
    highs = jnp.concatenate([grads[:, 128:256], grads[:, 384:512]], 1)
    low[0:rows], high[...] = lows, highs
    low_half[...] = jnp.where(at[AT_CORE] == 0, lows[:half], lows[half:])
    high_half[...] = jnp.where(at[AT_CORE] == 0, highs[:half], highs[half:])
    scale = far_scale[pl.ds(pl.multiple_of(at[AT_CORE] * half + step * FAR, FAR), FAR)]
    low[rows : rows + FAR] = (far_values[...].astype(jnp.float32) * scale).astype(jnp.bfloat16)


def dequant(at, exps, mantissas):
    rows, width = mantissas.shape
    half = rows // 2
    return pl.pallas_call(
        dequant_kernel,
        grid_spec=pltpu.PrefetchScalarGridSpec(
            num_scalar_prefetch=1,
            grid=(4,),
            in_specs=[
                pl.BlockSpec(exps.shape, lambda g, at: (0, 0)),
                pl.BlockSpec((rows, 512), lambda g, at: (0, at[AT_YL] * 4 + g)),
                pl.BlockSpec((half, 256), lambda g, at: (at[AT_CORE], at[AT_OWN])),
                pl.BlockSpec((FAR, 256), lambda g, at: (at[AT_CORE] * 4 + g, at[AT_FAR])),
            ],
            out_specs=[
                pl.BlockSpec((rows + FAR, 256), lambda g, at: (0, g)),
                pl.BlockSpec((rows, 256), lambda g, at: (0, g)),
                pl.BlockSpec((half, 256), lambda g, at: (0, g)),
                pl.BlockSpec((half, 256), lambda g, at: (0, g)),
                pl.BlockSpec((half, 256), lambda g, at: (0, 0)),
            ],
            scratch_shapes=[pltpu.VMEM((rows, 256), jnp.float32)],
        ),
        out_shape=[
            jax.ShapeDtypeStruct((rows + FAR, width // 4), jnp.bfloat16),
            jax.ShapeDtypeStruct((rows, width // 4), jnp.bfloat16),
            jax.ShapeDtypeStruct((half, width // 4), jnp.bfloat16),
            jax.ShapeDtypeStruct((half, width // 4), jnp.bfloat16),
            jax.ShapeDtypeStruct((half, 256), jnp.bfloat16),
        ],
        compiler_params=params(62),
        cost_estimate=cost(1 << 25, 2 << 20),
        name="dequant",
    )(at, exps, mantissas, mantissas, mantissas)


def halve_low_kernel(at, low, far, low_half):
    half = low.shape[0]
    low_half[0:half] = low[...]
    low_half[half : half + FAR] = far[...]


def halve_low(at, low):
    rows, width = low.shape[0] - FAR, low.shape[1]
    half = rows // 2
    return pl.pallas_call(
        halve_low_kernel,
        grid_spec=pltpu.PrefetchScalarGridSpec(
            num_scalar_prefetch=1,
            grid=(1,),
            in_specs=[
                pl.BlockSpec((half, width), lambda g, at: (at[AT_CORE], 0)),
                pl.BlockSpec((FAR, width), lambda g, at: (rows // FAR, 0)),
            ],
            out_specs=pl.BlockSpec((half + FAR, width), lambda g, at: (0, 0)),
        ),
        out_shape=jax.ShapeDtypeStruct((half + FAR, width), jnp.bfloat16),
        compiler_params=params(8),
        cost_estimate=cost(0, 1 << 19),
        name="halve_low",
    )(at, low, low)


def halve_high_kernel(at, high, low_lanes, high_lanes, after, high_half, third):
    del after
    high_half[...] = high[...]
    third[...] = jnp.concatenate([low_lanes[...], high_lanes[...]], 1)


def halve_high(at, low, high, after):
    rows, width = high.shape
    half = rows // 2
    return pl.pallas_call(
        halve_high_kernel,
        grid_spec=pltpu.PrefetchScalarGridSpec(
            num_scalar_prefetch=1,
            grid=(1,),
            in_specs=[
                pl.BlockSpec((half, width), lambda g, at: (at[AT_CORE], 0)),
                lanes_at_z(rows, False),
                lanes_at_z(rows, False),
                pl.BlockSpec(memory_space=pl.ANY),
            ],
            out_specs=[
                pl.BlockSpec((half, width), lambda g, at: (0, 0)),
                pl.BlockSpec((rows, 256), lambda g, at: (0, 0)),
            ],
        ),
        out_shape=[
            jax.ShapeDtypeStruct((half, width), jnp.bfloat16),
            jax.ShapeDtypeStruct((rows, 256), jnp.bfloat16),
        ],
        compiler_params=params(8),
        cost_estimate=cost(0, 1 << 20),
        name="halve_high",
    )(at, high, low, high, after)


def pick_kernel(count, at, *refs):
    sides, out = refs[: 2 * count], refs[-1]
    row = 0
    for i in range(count):
        rows = sides[2 * i].shape[0]
        out[row : row + rows] = jnp.concatenate([sides[2 * i][...], sides[2 * i + 1][...]], 1)
        row += rows


def lanes_at_z(rows, by_core):
    if by_core:
        return pl.BlockSpec((rows, 128), lambda g, at: (at[AT_CORE], at[AT_Z]))
    return pl.BlockSpec((rows, 128), lambda g, at: (0, at[AT_Z]))


def pick(at, pieces, *after):
    rows = sum(n for n, _, _, _ in pieces)
    specs = [lanes_at_z(n, by_core) for n, by_core, _, _ in pieces for _ in range(2)]
    specs += [pl.BlockSpec(memory_space=pl.ANY)] * len(after)
    return pl.pallas_call(
        functools.partial(pick_kernel, len(pieces)),
        grid_spec=pltpu.PrefetchScalarGridSpec(
            num_scalar_prefetch=1, grid=(1,), in_specs=specs,
            out_specs=pl.BlockSpec((rows, 256), lambda g, at: (0, 0)),
        ),
        out_shape=jax.ShapeDtypeStruct((rows, 256), jnp.bfloat16),
        compiler_params=params(6),
        cost_estimate=cost(0, rows * 1024),
        name="pick",
    )(at, *[side for _, _, low, high in pieces for side in (low, high)], *after)


def gram_kernel(sizes, kept, parts, at, *refs):
    count = len(sizes)
    lows, highs = refs[:count], refs[count : 2 * count]
    low_rights, high_rights = refs[2 * count : 3 * count], refs[3 * count : 4 * count]
    own, near, third, far = refs[4 * count : 4 * count + 4]
    outs = refs[-1 - 2 * parts : -1]
    left = refs[-1]
    step = pl.program_id(0)

    @pl.when(step == 0)
    def _():
        mine_first = at[AT_YL] == at[AT_YH]
        use_mine = mine_first if kept else jnp.logical_not(mine_first)
        row, start = 0, 0
        for i, rows in enumerate(sizes):
            mine = jnp.concatenate([lows[i][...], highs[i][...]], 1)
            if 0 < i < count - 2:
                theirs = near[row : row + rows]
                row += rows
            else:
                theirs = (own if i == 0 else third)[...] if i < count - 1 else jnp.concatenate(
                    [far[:, lane : lane + 256] for lane in range(0, 1024, 256)], 0
                )
            left[start : start + rows] = jnp.where(use_mine, mine, theirs)
            start += rows

    def terms(rights):
        total, start = None, 0
        for i, rows in enumerate(sizes):
            term = lax.dot_general(
                left[start : start + rows], rights[i][...], TURNED, preferred_element_type=jnp.float32
            )
            total = term if total is None else total + term
            start += rows
        return total

    for part in range(parts):

        @pl.when(step == part)
        def _(part=part):
            outs[2 * part][...] = terms(low_rights)
            outs[2 * part + 1][...] = terms(high_rights)


def gram(at, pieces, received, kept, parts, *after):
    first = parts[0]
    sizes = tuple(n for n, _, _, _ in pieces)
    specs = [lanes_at_z(n, by_core) for n, by_core, _, _ in pieces] * 2
    for n, by_core, _, _ in pieces:
        specs.append(
            pl.BlockSpec(
                (n, 512),
                lambda g, at, by_core=by_core: (
                    at[AT_CORE] if by_core else 0,
                    (1 - first - g) * (1 - at[AT_CORE]) + (first + g) * at[AT_CORE],
                ),
            )
        )
    specs += specs[-len(pieces) :]
    specs += [pl.BlockSpec(r.shape, lambda g, at: (0, 0)) for r in received]
    last = pieces[-1][2]
    specs.append(pl.BlockSpec((FAR, last.shape[1]), lambda g, at: (last.shape[0] // FAR - 1, 0)))
    specs += [pl.BlockSpec(memory_space=pl.ANY)] * len(after)
    sides = [p[2] for p in pieces], [p[3] for p in pieces]
    return pl.pallas_call(
        functools.partial(gram_kernel, sizes, kept, len(parts)),
        grid_spec=pltpu.PrefetchScalarGridSpec(
            num_scalar_prefetch=1, grid=(len(parts),), in_specs=specs,
            out_specs=[pl.BlockSpec((256, 512), lambda g, at: (0, 0))] * (2 * len(parts)),
            scratch_shapes=[pltpu.VMEM((sum(sizes), 256), jnp.bfloat16)],
        ),
        out_shape=[jax.ShapeDtypeStruct((256, 512), jnp.float32)] * (2 * len(parts)),
        compiler_params=params(20),
        cost_estimate=cost(0, 0),
        name="gram",
    )(at, *sides[0], *sides[1], *sides[0], *sides[1], *received, last, *after)


def add_kernel(low, high, low_got, high_got, out):
    columns = low.shape[1]
    out[:, 0:columns] = low[...] + low_got[...]
    out[:, columns:] = high[...] + high_got[...]


def add(terms):
    rows, columns = terms[0].shape
    return pl.pallas_call(
        add_kernel,
        grid=(2,),
        in_specs=[pl.BlockSpec((rows // 2, columns), lambda g: (g, 0))] * 4,
        out_specs=pl.BlockSpec((rows // 2, 2 * columns), lambda g: (g, 0)),
        out_shape=jax.ShapeDtypeStruct((rows, 2 * columns), jnp.float32),
        compiler_params=params(6),
        cost_estimate=cost(0, 0),
        name="add",
    )(*terms)


def finish_kernel(factor, low, high, low_core, high_core, got, out):
    for i in range(4):
        lanes = slice(i * 128, i * 128 + 128)
        first = (low[:, lanes] + low_core[:, lanes]) + got[:, lanes]
        second = (high[:, lanes] + high_core[:, lanes]) + got[:, 512 + i * 128 : 640 + i * 128]
        out[:, i * 256 : i * 256 + 128] = first * factor
        out[:, i * 256 + 128 : i * 256 + 256] = second * factor


def finish(factor, terms):
    rows, columns = terms[0].shape
    return pl.pallas_call(
        functools.partial(finish_kernel, factor),
        grid=(4,),
        in_specs=[pl.BlockSpec((rows // 4, columns), lambda g: (g, 0))] * 4
        + [pl.BlockSpec((rows // 4, 2 * columns), lambda g: (g, 0))],
        out_specs=pl.BlockSpec((rows // 4, 2 * columns), lambda g: (g, 0)),
        out_shape=jax.ShapeDtypeStruct((rows, 2 * columns), jnp.float32),
        compiler_params=params(8),
        cost_estimate=cost(1 << 20, 4 << 20),
        name="finish",
    )(*terms)


def tie_kernel(*refs):
    del refs


def tie(value, *earlier):
    return pl.pallas_call(
        tie_kernel,
        in_specs=[pl.BlockSpec(memory_space=pl.ANY)] * (1 + len(earlier)),
        out_specs=pl.BlockSpec(memory_space=pl.ANY),
        out_shape=jax.ShapeDtypeStruct(value.shape, value.dtype),
        input_output_aliases={0: 0},
        compiler_params=params(1),
        cost_estimate=cost(0, 0),
        name="tie",
    )(value, *earlier)


def fisher_terms(at, mantissas, exps, pair, placed):
    rows = mantissas.shape[0]
    low, high, low_half, high_half, own = dequant(at, exps, mantissas)

    half = rows // 2
    pieces = [(half, False, low_half, high_half)]
    for step in range(1, Z // 2 + 1):
        if step == Z // 2:
            high, third = halve_high(at, low, high, near)
            low = halve_low(at, low)
        low = lax.ppermute(low, ("z", "core"), RING)
        high = lax.ppermute(high, ("z", "core"), RING)
        if step == 1:
            low = tie(low, pair)
        if step == 2:
            low = tie(low, placed)
        pieces.append((rows if step < Z // 2 else half, False, low, high))
        if step == 2:
            near = pick(at, pieces[1:3])
            placed = tie(placed, near)
            near = lax.ppermute(near, "yl", SWAP)
    mine = own_slots(placed)
    received = (own, near, lax.ppermute(third, "yl", SWAP))

    given_other = gram(at, pieces, received, False, (0,), mine)
    swapped = [lax.ppermute(g, "core", SWAP) for g in given_other]
    given_own = gram(at, pieces, received, False, (1,), *given_other)
    given = add([*given_own, *swapped])
    *kept_other, low_kept, high_kept = gram(at, pieces, received, True, (0, 1), given)
    kept = [lax.ppermute(k, "core", SWAP) for k in kept_other]
    return given, [low_kept, high_kept, *kept], mine


def spread(scale):
    blocks = scale.shape[1]
    lane_block = jnp.arange(blocks * 128, dtype=jnp.int32) // 128
    pick = (lane_block[None, :] == jnp.arange(blocks, dtype=jnp.int32)[:, None]).astype(jnp.bfloat16)
    wide = lax.dot_general(scale, pick, (((1,), (0,)), ((), ())), preferred_element_type=jnp.float32)
    return wide.astype(jnp.bfloat16)


def place_kernel(at, pair, got, ids, owners, out):
    docs, rows = owners.shape[1], ids.shape[1]
    summed = jnp.where(at[AT_X] % 2 == 0, pair[0], pair[1]) + got[...]
    owner = jnp.broadcast_to(owners[...], (8, docs))
    digit = jnp.where(lax.broadcasted_iota(jnp.int32, (8, docs), 0) == 0, owner >> 5, owner & 31)
    doc = (lax.broadcasted_iota(jnp.int32, (docs, rows), 0) == ids[...]).astype(jnp.bfloat16)
    digits = lax.dot_general(
        digit.astype(jnp.float32).astype(jnp.bfloat16), doc, (((1,), (0,)), ((), ())),
        preferred_element_type=jnp.float32,
    )
    slots = (digits[0:1] * 32.0 + digits[1:2]).astype(jnp.int32)
    count = out.shape[0]
    own_docs = docs // (YH * Z)
    half = own_docs // 2
    place = lax.broadcasted_iota(jnp.int32, (count, rows), 0)
    place = (place // half) * own_docs + place % half
    member = jnp.concatenate([place == slots, place + half == slots], 1)
    member = jnp.where(member, 1.0, 0.0).astype(jnp.bfloat16)
    zero = jnp.zeros_like(summed)
    rest = jnp.concatenate(
        [jnp.concatenate([summed, zero], 1), jnp.concatenate([zero, summed], 1)], 0
    )
    total = None
    for _ in range(3):
        part = rest.astype(jnp.bfloat16)
        rest = rest - part.astype(jnp.float32)
        term = lax.dot_general(member, part, (((1,), (1,)), ((), ())), preferred_element_type=jnp.float32)
        total = term if total is None else total + term
    out[...] = total


def sum_kernel(parts, out):
    total = parts[0]
    for i in range(1, parts.shape[0]):
        total = total + parts[i]
    out[...] = total


def flipped(bit):
    return [(i, i ^ bit) for i in range(X)]


def whole(shape):
    return pl.BlockSpec(shape, lambda g, at: (0,) * len(shape))


def placed_scores(at, mantissas, scale, queries, doc_ids, owners):
    docs = owners.shape[0]
    x = lax.axis_index("x")
    grads = mantissas * spread(scale)
    scores = lax.dot_general(queries, grads, (((1,), (1,)), ((), ())), preferred_element_type=jnp.float32)
    count, rows = scores.shape
    share, half = count // X, docs // (YH * Z) // 2
    upper = x // 2
    got = lax.ppermute(lax.dynamic_slice_in_dim(scores, (1 - upper) * 2 * share, 2 * share, 0), "x", flipped(2))
    pair = lax.dynamic_slice_in_dim(scores, upper * 2 * share, 2 * share, 0) + got
    got = lax.ppermute(lax.dynamic_slice_in_dim(pair, (1 - x % 2) * share, share, 0), "x", flipped(1))
    shapes = (X // 2, share, rows), (share, rows), (1, rows), (1, docs)
    placed = pl.pallas_call(
        place_kernel,
        grid_spec=pltpu.PrefetchScalarGridSpec(
            num_scalar_prefetch=1, grid=(1,), in_specs=[whole(shape) for shape in shapes],
            out_specs=whole((YH * Z * half, 2 * share)),
        ),
        out_shape=jax.ShapeDtypeStruct((YH * Z * half, 2 * share), jnp.float32),
        compiler_params=params(10),
        cost_estimate=cost(1 << 28, 1 << 20),
        name="place",
    )(at, pair.reshape(shapes[0]), got, doc_ids.reshape(1, rows), owners.reshape(1, docs))
    return pair, placed


def assemble_kernel(at, pair, far_pair, out):
    half, double = pair.shape[1:]
    share = double // 2
    values = []
    for source in range(X):
        near = (source // 2) == at[AT_X] // 2
        first = (source % 2) == at[AT_X] % 2
        own = jnp.where(first, pair[0], pair[1])
        other = jnp.where(first, far_pair[0], far_pair[1])
        values.append(jnp.where(near, own, other))
    out[0:half] = jnp.concatenate([v[:, :share] for v in values], 1)
    out[half:] = jnp.concatenate([v[:, share:] for v in values], 1)


def own_slots(placed):
    double = placed.shape[1]
    half = placed.shape[0] // (YH * Z)
    blocks = lax.all_to_all(placed.reshape(YH * Z, half, double), ("yh", "z"), 0, 0, tiled=True)
    return pl.pallas_call(
        sum_kernel,
        out_shape=jax.ShapeDtypeStruct((half, double), jnp.float32),
        compiler_params=params(4),
        cost_estimate=cost(1 << 16, 1 << 18),
        name="sum",
    )(blocks)


def doc_block(at, mine):
    half, double = mine.shape
    pair = jnp.stack([mine, lax.ppermute(mine, "x", flipped(1))])
    far_pair = lax.ppermute(pair, "x", flipped(2))
    return pl.pallas_call(
        assemble_kernel,
        grid_spec=pltpu.PrefetchScalarGridSpec(
            num_scalar_prefetch=1, grid=(1,), in_specs=[whole(pair.shape)] * 2,
            out_specs=whole((2 * half, X * double // 2)),
        ),
        out_shape=jax.ShapeDtypeStruct((2 * half, X * double // 2), jnp.float32),
        compiler_params=params(2),
        cost_estimate=cost(0, 1 << 17),
        name="assemble",
    )(at, pair, far_pair)


def per_device(mantissas, exponents, queries, doc_ids, owners):
    mantissas = mantissas[:, 0, :]
    exponents = exponents[:, 0, :]
    total_rows = mantissas.shape[0] * YH * Z
    yh, z, x = lax.axis_index("yh"), lax.axis_index("z"), lax.axis_index("x")
    yl, core = lax.axis_index("yl"), lax.axis_index("core")
    other = (1 - yl) * Z
    at = jnp.stack([z, core, yl, other + z, other + lax.rem(z + Z // 2, Z), yh, x]).astype(jnp.int32)
    pair, placed = placed_scores(at, mantissas, powers(exponents), queries[:, 0, :], doc_ids, owners)
    given, kept, mine = fisher_terms(at, mantissas, exponents.T, pair, placed)
    got = lax.ppermute(given, "yh", SWAP)
    return finish(1.0 / total_rows, kept + [got])[None], doc_block(at, mine)


def solution(mesh):
    fine = Mesh(mesh.devices.reshape(YH, Z, X, YL, CORE), ("yh", "z", "x", "yl", "core"))
    in_specs = (
        P(ROW_AXES, "x", None),
        P(ROW_AXES, "x", None),
        P(COL_AXES, "x", None),
        P(ROW_AXES),
        P(),
    )
    out_specs = (P("x", ROW_AXES, COL_AXES), P(ROW_AXES, COL_AXES))
    return jax.shard_map(per_device, mesh=fine, in_specs=in_specs, out_specs=out_specs, check_vma=False)
```
